256 devices in a mesh: lon: 32 (over z, y_hi, core), lat: 8 (over x, y_lo).
Axes of the slice: x: 4, y: 4 (y_hi: 2, y_lo: 2; y = y_hi * 2 + y_lo), z: 8, core: 2. Of those that a mesh axis runs over, the one named last changes fastest.
Arguments:
- heat_anomaly: float32 [8, 1536, 4096], P(None, 'lat', 'lon'), may hold values from -6 to 6
- saltiness_anomaly: float32 [8, 1536, 4096], P(None, 'lat', 'lon'), may hold values from -6 to 6
- zonal_current: float32 [8, 1536, 4096], P(None, 'lat', 'lon'), may hold values from -3 to 3
- meridional_current: float32 [8, 1536, 4096], P(None, 'lat', 'lon'), may hold values from -3 to 3
- free_elevation: float32 [1536, 4096], P('lat', 'lon'), may hold values from -3 to 3
- ocean_indicator: int32 [8, 1536, 4096], P(None, 'lat', 'lon'), may hold values from 0 to 1, as said below
- floor_layer_index: int32 [1536, 4096], P('lat', 'lon'), may hold values from 0 to 7, as said below
Outputs:
- temperature_next: float32 [8, 1536, 4096], P(None, 'lat', 'lon')
- salinity_next: float32 [8, 1536, 4096], P(None, 'lat', 'lon')
- zonal_next: float32 [8, 1536, 4096], P(None, 'lat', 'lon')
- meridional_next: float32 [8, 1536, 4096], P(None, 'lat', 'lon')
- height_next: float32 [1536, 4096], P('lat', 'lon')
The draws below stay inside these ranges and needn't reach their ends.
Inputs may be any that keep to these rules, and one draw needn't show every extreme that they name: In each column with water the cells with ocean_indicator 1 are one run of levels, starting at level 0, 1 or 2 and ending at floor_layer_index; columns without water have ocean_indicator 0 at every level. `floor_layer_index`: the deepest wet level where the column holds water, 0 where it is dry.
All inputs are finite; a program needn't handle non-finite values.
Results may differ from the reference program's by a relative error of at most 0.00002.
Values sent between devices are 32-bit elements; how exact they have to be, the bound alone decides.
No kernel may reach another device: no remote copies, remote signals or barrier semaphores. Data moves between devices by JAX's collectives and lax.ppermute only.
A program may use at most 128 MiB of HBM per device.

```python
import jax
import jax.numpy as jnp
from jax import lax

DEPTH_LAYERS = 8
MERIDIAN_SPAN = 1536
PARALLEL_SPAN = 4096


def column_shape(key):
    split_keys = jax.random.split(key, 4)
    array_shape = (MERIDIAN_SPAN, PARALLEL_SPAN)
    row_index = jnp.arange(MERIDIAN_SPAN, dtype=jnp.int32)[:, None]
    land_limit = 100 + 500 * row_index * row_index // (MERIDIAN_SPAN * MERIDIAN_SPAN)
    dry_land = jax.random.randint(split_keys[0], array_shape, 0, 1000) < land_limit
    deepest = jax.random.randint(split_keys[1], array_shape, 1, DEPTH_LAYERS + 1)
    deepest = jnp.where(dry_land, 0, deepest)
    shelf_cell = jax.random.randint(split_keys[2], array_shape, 0, 8) == 0
    shelf_top = jnp.minimum(jax.random.randint(split_keys[3], array_shape, 1, 3), deepest - 1)
    upper_level = jnp.where(shelf_cell & (deepest >= 2), shelf_top, 0)
    return (upper_level, deepest)


def draw_ocean_indicator(key, part):
    upper_level, deepest = column_shape(key)
    level_index = jnp.arange(DEPTH_LAYERS, dtype=jnp.int32)[:, None, None]
    return ((level_index >= upper_level[None]) & (level_index < deepest[None])).astype(jnp.int32)


def draw_floor_layer_index(key, part):
    upper_level, deepest = column_shape(key)
    return jnp.maximum(deepest - 1, 0).astype(jnp.int32)


def shard_levels(own_key, dims, cuts, low, top_value):
    def one(dim, shards_of):
        heights = jax.random.uniform(jax.random.fold_in(jax.random.fold_in(own_key, 6), dim), (shards_of,), jnp.float32, low / len(cuts), top_value / len(cuts))
        return jnp.repeat(jnp.exp(heights), dims[dim] // shards_of).reshape((-1,) + (1,) * (len(dims) - dim - 1))

    gain = one(*cuts[0])
    for cut in cuts[1:]:
        gain = gain * one(*cut)
    return gain


def gaussian(own_key, dims, width, most, cuts=(), kind=jnp.bfloat16):
    array = width * jax.random.normal(own_key, dims, jnp.float32)
    if cuts:
        array = array * shard_levels(own_key, dims, cuts, -0.22, 0.18)
    return jnp.clip(array, -most, most).astype(kind)


def setup_inputs(seed: int = 0) -> dict:
    arg_keys = jax.random.split(jax.random.key(seed), 8)
    heat_anomaly = gaussian(arg_keys[0], (DEPTH_LAYERS, MERIDIAN_SPAN, PARALLEL_SPAN), 1.0, 6.0, ((1, 8), (2, 32)), jnp.float32)
    saltiness_anomaly = gaussian(arg_keys[1], (DEPTH_LAYERS, MERIDIAN_SPAN, PARALLEL_SPAN), 1.0, 6.0, ((1, 8), (2, 32)), jnp.float32)
    zonal_current = gaussian(arg_keys[2], (DEPTH_LAYERS, MERIDIAN_SPAN, PARALLEL_SPAN), 0.5, 3.0, ((1, 8), (2, 32)), jnp.float32)
    meridional_current = gaussian(arg_keys[3], (DEPTH_LAYERS, MERIDIAN_SPAN, PARALLEL_SPAN), 0.5, 3.0, ((1, 8), (2, 32)), jnp.float32)
    free_elevation = gaussian(arg_keys[4], (MERIDIAN_SPAN, PARALLEL_SPAN), 0.5, 3.0, ((0, 8), (1, 32)), jnp.float32)
    ocean_indicator = draw_ocean_indicator(jax.random.fold_in(arg_keys[7], 71), 0)
    floor_layer_index = draw_floor_layer_index(jax.random.fold_in(arg_keys[7], 71), 0)
    return {"heat_anomaly": heat_anomaly, "saltiness_anomaly": saltiness_anomaly, "zonal_current": zonal_current, "meridional_current": meridional_current, "free_elevation": free_elevation, "ocean_indicator": ocean_indicator, "floor_layer_index": floor_layer_index}


time_step = 0.2
viscosity = 0.5
diffusivity = 0.3
press_scale = 0.25
gravity = 1.0
drag_coef = 1.0
coriolis_max = 0.5

def offset_view(field, shift_row, shift_col):
    elevation_grid = field.shape[1] - 4
    breadth = field.shape[2] - 4
    return field[:, 2 + shift_row:2 + shift_row + elevation_grid, 2 + shift_col:2 + shift_col + breadth]

def laplace(field, wet_ext):
    centre = offset_view(field, 0, 0)
    wet_centre = offset_view(wet_ext, 0, 0)
    total = jnp.zeros_like(centre)
    for shift_row, shift_col in ((0, 1), (0, -1), (1, 0), (-1, 0)):
        total = total + wet_centre * offset_view(wet_ext, shift_row, shift_col) * (offset_view(field, shift_row, shift_col) - centre)
    return total

def coriolis_rows(first_row, count, total):
    row_index = first_row + jnp.arange(count, dtype=jnp.int32)
    return coriolis_max * (2.0 * (row_index.astype(jnp.float32) + 0.5) / total - 1.0)

def momentum(extended, coriolis, bottom):
    layer_pile = (extended.shape[0] - 1) // 5
    thermal = extended[:layer_pile]
    saline = extended[layer_pile:2 * layer_pile]
    eastward = extended[2 * layer_pile:3 * layer_pile]
    northward = extended[3 * layer_pile:4 * layer_pile]
    wet_ext = extended[4 * layer_pile:5 * layer_pile]
    surface = extended[5 * layer_pile:5 * layer_pile + 1]
    density = -0.2 * thermal + 0.8 * saline - 0.05 * thermal * thermal + 0.02 * thermal * saline
    pressure = press_scale * (jnp.cumsum(density, axis=0) - 0.5 * density) + gravity * surface
    slope_x = 0.5 * (offset_view(pressure, 0, 1) - offset_view(pressure, 0, -1))
    slope_y = 0.5 * (offset_view(pressure, 1, 0) - offset_view(pressure, -1, 0))
    wet_centre = offset_view(wet_ext, 0, 0)
    east_now = offset_view(eastward, 0, 0)
    north_now = offset_view(northward, 0, 0)
    spin = coriolis[None, :, None]
    east_trial = east_now + time_step * (spin * north_now - slope_x + viscosity * laplace(eastward, wet_ext))
    north_trial = north_now + time_step * (-spin * east_now - slope_y + viscosity * laplace(northward, wet_ext))
    level_index = lax.broadcasted_iota(jnp.int32, east_trial.shape, 0)
    speed = jnp.sqrt(east_trial * east_trial + north_trial * north_trial)
    damping = jnp.where(level_index == bottom[None], 1.0 / (1.0 + drag_coef * speed), 1.0)
    return (wet_centre * east_trial * damping, wet_centre * north_trial * damping)

def faces_x(field):
    elevation_grid = field.shape[1] - 4
    breadth = field.shape[2] - 4
    band = field[:, 2:2 + elevation_grid, :]
    return (7.0 * (band[:, :, 1:breadth + 2] + band[:, :, 2:breadth + 3]) - (band[:, :, 0:breadth + 1] + band[:, :, 3:breadth + 4])) / 12.0

def faces_y(field):
    elevation_grid = field.shape[1] - 4
    breadth = field.shape[2] - 4
    band = field[:, :, 2:2 + breadth]
    return (7.0 * (band[:, 1:elevation_grid + 2, :] + band[:, 2:elevation_grid + 3, :]) - (band[:, 0:elevation_grid + 1, :] + band[:, 3:elevation_grid + 4, :])) / 12.0

def normal_x(velocity, wet_ext):
    elevation_grid = velocity.shape[1] - 4
    breadth = velocity.shape[2] - 4
    band = velocity[:, 2:2 + elevation_grid, :]
    wetband = wet_ext[:, 2:2 + elevation_grid, :]
    return 0.5 * (band[:, :, 1:breadth + 2] + band[:, :, 2:breadth + 3]) * wetband[:, :, 1:breadth + 2] * wetband[:, :, 2:breadth + 3]

def normal_y(velocity, wet_ext):
    elevation_grid = velocity.shape[1] - 4
    breadth = velocity.shape[2] - 4
    band = velocity[:, :, 2:2 + breadth]
    wetband = wet_ext[:, :, 2:2 + breadth]
    return 0.5 * (band[:, 1:elevation_grid + 2, :] + band[:, 2:elevation_grid + 3, :]) * wetband[:, 1:elevation_grid + 2, :] * wetband[:, 2:elevation_grid + 3, :]

def tracers(extended, moved):
    layer_pile = (extended.shape[0] - 1) // 5
    wet_ext = extended[4 * layer_pile:5 * layer_pile]
    trans_x = normal_x(moved[:layer_pile], wet_ext)
    trans_y = normal_y(moved[layer_pile:], wet_ext)
    wet_centre = offset_view(wet_ext, 0, 0)

    def advance(field):
        flux_x = trans_x * faces_x(field)
        flux_y = trans_y * faces_y(field)
        spread = flux_x[:, :, 1:] - flux_x[:, :, :-1] + (flux_y[:, 1:, :] - flux_y[:, :-1, :])
        return wet_centre * (offset_view(field, 0, 0) - time_step * spread + time_step * diffusivity * laplace(field, wet_ext))
    thermal_next = advance(extended[:layer_pile])
    saline_next = advance(extended[layer_pile:2 * layer_pile])
    inflow = lax.optimization_barrier(jnp.sum(trans_x[:, :, 1:] - trans_x[:, :, :-1] + (trans_y[:, 1:, :] - trans_y[:, :-1, :]), axis=0))
    height_next = offset_view(extended[5 * layer_pile:5 * layer_pile + 1], 0, 0)[0] - time_step / layer_pile * inflow
    return (thermal_next, saline_next, height_next)

def extend_global(joined_tracer_grids, signs):
    south = jnp.zeros((joined_tracer_grids.shape[0], 2, joined_tracer_grids.shape[2]), jnp.float32)
    north = joined_tracer_grids[:, -2:, :][:, ::-1, ::-1] * signs[:, None, None]
    tall = jnp.concatenate([south, joined_tracer_grids, north], axis=1)
    return jnp.concatenate([tall[:, :, -2:], tall, tall[:, :, :2]], axis=2)

def reference(heat_anomaly, saltiness_anomaly, zonal_current, meridional_current, free_elevation, ocean_indicator, floor_layer_index):
    layer_pile = heat_anomaly.shape[0]
    holds_water = ocean_indicator.astype(jnp.float32)
    joined_tracer_grids = jnp.concatenate([heat_anomaly, saltiness_anomaly, zonal_current, meridional_current, holds_water, free_elevation[None]], axis=0)
    signs = jnp.concatenate([jnp.ones(2 * layer_pile, jnp.float32), -jnp.ones(2 * layer_pile, jnp.float32), jnp.ones(layer_pile + 1, jnp.float32)])
    extended = extend_global(joined_tracer_grids, signs)
    coriolis = coriolis_rows(0, joined_tracer_grids.shape[1], joined_tracer_grids.shape[1])
    east_next, north_next = momentum(extended, coriolis, floor_layer_index)
    moved = extend_global(jnp.concatenate([east_next, north_next], axis=0), -jnp.ones(2 * layer_pile, jnp.float32))
    thermal_next, saline_next, height_next = tracers(extended, moved)
    return (thermal_next, saline_next, east_next, north_next, height_next)
```

```python
import functools

import jax
import jax.numpy as jnp
from jax import lax
from jax.experimental import pallas as pl
from jax.experimental.pallas import tpu as pltpu
from jax.sharding import PartitionSpec as P

F32 = jnp.float32
LEVELS = 8
LANES = 128
FIELDS = 5
PLANES = FIELDS * LEVELS + 1
ROW_MSG = 2 * FIELDS * LEVELS + 8
BASE = 16
CHUNKS = 4
PACK_ROWS = 48
MAIN_ROWS = 96
EDGE_CHUNKS = 1

time_step = 0.2
viscosity = 0.5
diffusivity = 0.3
press_scale = 0.25
gravity = 1.0
drag_coef = 1.0
coriolis_max = 0.5

HBM = pl.BlockSpec(memory_space=pltpu.HBM)
VMEM = pl.BlockSpec(memory_space=pltpu.VMEM)


def params(mib):
    return pltpu.CompilerParams(vmem_limit_bytes=int(mib * 1024 * 1024))


def lanes(rows=8):
    return lax.broadcasted_iota(jnp.int32, (rows, LANES), 1)


def east(x):
    return pltpu.roll(x, LANES - 1, 1)


def west(x):
    return pltpu.roll(x, 1, 1)


def gather(x, index):
    return jnp.take_along_axis(x, index, axis=1)


def is_even(axis):
    return lax.rem(lax.axis_index(axis), 2) == 0


def row_pack_kernel(*refs):
    ins, (a_ref, b_ref), tiles, sems = refs[:6], refs[6:8], refs[8:20], refs[20]
    rows = ins[5].shape[0]
    copies = []
    for n, x in enumerate(ins):
        for side, start in enumerate((0, rows - 8)):
            src = x.at[:, pl.ds(start, 8), :] if n < FIELDS else x.at[pl.ds(start, 8), :]
            copies.append(pltpu.make_async_copy(src, tiles[2 * n + side], sems.at[2 * n + side]))
            copies[-1].start()
    for x in copies:
        x.wait()
    even = is_even("lat")
    for r in range(2):
        for f in range(FIELDS):
            low, high = tiles[2 * f : 2 * f + 2]
            bottom = low.reshape(LEVELS * 8, LANES)[pl.ds(r, LEVELS, stride=8), :].astype(F32)
            top = high.reshape(LEVELS * 8, LANES)[pl.ds(6 + r, LEVELS, stride=8), :].astype(F32)
            place = pl.ds((r * FIELDS + f) * LEVELS, LEVELS)
            a_ref[place, :] = jnp.where(even, top, bottom)
            b_ref[place, :] = jnp.where(even, bottom, top)
    place = pl.ds(2 * FIELDS * LEVELS, 8)
    low, high = tiles[10][...], tiles[11][...]
    a_ref[place, :] = jnp.where(even, high, low)
    b_ref[place, :] = jnp.where(even, low, high)


def row_pack(fields, surface):
    scratch = [pltpu.VMEM((LEVELS, 8, LANES), x.dtype) for x in fields for _ in range(2)]
    scratch += [pltpu.VMEM((8, LANES), F32)] * 2 + [pltpu.SemaphoreType.DMA((12,))]
    return pl.pallas_call(
        row_pack_kernel,
        in_specs=[HBM] * 6,
        out_specs=[VMEM] * 2,
        out_shape=[pltpu.VMEM((ROW_MSG, LANES), F32)] * 2,
        scratch_shapes=scratch,
        compiler_params=params(60),
        name="row_pack",
    )(*fields, surface)


def pack_columns(plane, rows):
    lane = lanes(rows)
    packed = []
    for first in range(0, PLANES, 16):
        group = None
        for p in range(first, min(first + 16, PLANES)):
            q = p - first
            moved = pltpu.roll(plane(p), (8 * q + 4) % LANES, 1)
            group = moved if group is None else jnp.where(lane >= 8 * q, moved, group)
        packed.append(group)
    return packed


def column_messages(packed, even, rows):
    lane = lanes(rows)
    base = 8 * ((lane // 2) % 16) + lane % 2
    messages = []
    for first in (True, False):
        eastern = even if first else jnp.logical_not(even)
        index = base + jnp.where(eastern, 2, 4)
        c0, c1, c2 = [gather(c, index) for c in packed]
        messages.append(jnp.where(lane < 32, c0, jnp.where(lane < 64, c1, c2)))
    return messages


def column_pack_kernel(t_in, s_in, u_in, v_in, w_in, e_in, t, s, u, v, w, e, p, c_ref, m0_ref, m1_ref, wi, sems):
    rows = e_in.shape[0]
    block = rows // CHUNKS
    even = is_even("lon")
    fields = (t, s, u, v, w)
    copies = []
    for c in range(CHUNKS):
        src, dst = pl.ds(c * block, block), pl.ds(BASE + c * block, block)
        pairs = [(x.at[:, src, :], y.at[:, dst, :]) for x, y in ((t_in, t), (s_in, s), (u_in, u), (v_in, v))]
        pairs += [(w_in.at[:, src, :], wi.at[:, src, :]), (e_in.at[src, :], e.at[dst, :])]
        copies.append([pltpu.make_async_copy(x, y, sems.at[6 * c + n]) for n, (x, y) in enumerate(pairs)])
        for x in copies[-1]:
            x.start()
    for c in range(CHUNKS):
        for x in copies[c]:
            x.wait()

        def step(i, _):
            out = pl.ds(pl.multiple_of(c * block + i * PACK_ROWS, 8), PACK_ROWS)
            here = pl.ds(pl.multiple_of(BASE + c * block + i * PACK_ROWS, 8), PACK_ROWS)
            for k in range(LEVELS):
                w[k, here, :] = wi[k, out, :].astype(F32)

            def plane(q):
                if q == PLANES - 1:
                    return e[here, :]
                return fields[q // LEVELS][q % LEVELS, here, :]

            packed = pack_columns(plane, PACK_ROWS)
            for n, x in enumerate(packed):
                c_ref[out, n * LANES : (n + 1) * LANES] = x
            m0_ref[out, :], m1_ref[out, :] = column_messages(packed, even, PACK_ROWS)
            pressure(here, t, s, e, p)
            return 0

        lax.fori_loop(0, block // PACK_ROWS, step, 0)


def column_pack(fields, surface):
    rows = surface.shape[0]
    tall = rows + BASE + 16
    big = pltpu.VMEM((LEVELS, tall, LANES), F32)
    return pl.pallas_call(
        column_pack_kernel,
        in_specs=[HBM] * 6,
        out_specs=[VMEM] * 10,
        out_shape=[big] * 5
        + [pltpu.VMEM((tall, LANES), F32), big]
        + [pltpu.VMEM((rows + 8, 3 * LANES), F32)]
        + [pltpu.VMEM((rows + 8, LANES), F32)] * 2,
        scratch_shapes=[pltpu.VMEM((LEVELS, rows, LANES), jnp.int32), pltpu.SemaphoreType.DMA((6 * CHUNKS,))],
        compiler_params=params(57.5),
        cost_estimate=pl.CostEstimate(flops=10_000_000, bytes_accessed=6_000_000, transcendentals=0),
        name="column_pack",
    )(*fields, surface)


def ghost_kernel(a_ref, b_ref, *refs):
    t, s, u, v, w, e, p, c_ref, m0_ref, m1_ref, g_ref = refs[10:]
    rows = m0_ref.shape[0] - 8
    even = is_even("lat")
    fold = lax.axis_index("lat") == lax.axis_size("lat") - 1
    mirror = LANES - 1 - lanes()
    flat = g_ref.reshape(PLANES * 8, LANES)
    g_ref[...] = jnp.zeros_like(g_ref)

    def both(start):
        a, b = a_ref[pl.ds(start, 8), :], b_ref[pl.ds(start, 8), :]
        return jnp.where(even, a, b), jnp.where(even, b, a)

    for f in range(FIELDS):
        sign = -1.0 if f in (2, 3) else 1.0
        north0, south0 = both(f * LEVELS)
        north1, south1 = both((FIELDS + f) * LEVELS)
        first = jnp.where(fold, sign * gather(north1, mirror), north0)
        second = jnp.where(fold, sign * gather(north0, mirror), north1)
        for row, value in ((0, first), (1, second), (6, south0), (7, south1)):
            flat[pl.ds(f * LEVELS * 8 + row, LEVELS, stride=8), :] = value
    north, south = both(2 * FIELDS * LEVELS)
    turned = gather(north, mirror)
    row = lax.broadcasted_iota(jnp.int32, (8, LANES), 0)
    folded = jnp.where(row == 0, pltpu.roll(turned, 1, 0), pltpu.roll(turned, 3, 0))
    g_ref[PLANES - 1] = jnp.where(row < 2, jnp.where(fold, folded, north), jnp.where(row >= 6, south, 0.0))
    packed = pack_columns(lambda q: g_ref[q], 8)
    last = pl.ds(rows, 8)
    for n, c in enumerate(packed):
        c_ref[last, n * LANES : (n + 1) * LANES] = c
    m0_ref[last, :], m1_ref[last, :] = column_messages(packed, is_even("lon"), 8)
    for side in (pl.ds(BASE - 8, 8), pl.ds(BASE + rows, 8)):
        for f, x in enumerate((t, s, u, v, w)):
            for k in range(LEVELS):
                x[k, side, :] = g_ref[f * LEVELS + k]
        e[side, :] = g_ref[PLANES - 1]
        pressure(side, t, s, e, p)


def ghosts(a, b, arrays):
    return pl.pallas_call(
        ghost_kernel,
        in_specs=[VMEM] * 12,
        out_specs=[VMEM] * 10,
        out_shape=[pltpu.VMEM(x.shape, F32) for x in arrays],
        scratch_shapes=[pltpu.VMEM((PLANES, 8, LANES), F32)],
        input_output_aliases={n + 2: n for n in range(10)},
        compiler_params=params(8),
        name="ghosts",
    )(a, b, *arrays)


def density_half(t, s):
    k = 0.5 * press_scale * 0.5 * time_step
    return t * (-0.2 * k + (-0.05 * k) * t + (0.02 * k) * s) + (0.8 * k) * s


def pressure(here, t, s, e, p):
    total = (gravity * 0.5 * time_step) * e[here, :]
    for k in range(LEVELS):
        h = density_half(t[k, here, :], s[k, here, :])
        at = total + h
        p[k, here, :] = at
        total = at + h


def coriolis_rows(start, count, rows):
    total = rows * lax.axis_size("lat")
    row = lax.broadcasted_iota(jnp.int32, (count, LANES), 0) + (start - BASE + lax.axis_index("lat") * rows)
    row = jnp.minimum(row, total - 1).astype(F32)
    return (time_step * coriolis_max) * (2.0 * (row + 0.5) / total - 1.0)


def velocity_trial(k, r, n, spin, u, v, w, p, m_east, m_north):
    here, up, down = pl.ds(r, n), pl.ds(r + 1, n), pl.ds(r - 1, n)
    wet = w[k, here, :]
    me = wet * east(wet)
    mw = wet * west(wet)
    mn = wet * w[k, up, :]
    ms = wet * w[k, down, :]
    m_east[k, here, :] = me
    m_north[k, here, :] = mn

    def lap(q_ref, q):
        return me * (east(q) - q) + mw * (west(q) - q) + (mn * (q_ref[k, up, :] - q) + ms * (q_ref[k, down, :] - q))

    un, vn = u[k, here, :], v[k, here, :]
    pc = p[k, here, :]
    u_trial = un + (spin * vn - (east(pc) - west(pc)) + (time_step * viscosity) * lap(u, un))
    v_trial = vn + ((time_step * viscosity) * lap(v, vn) - spin * un - (p[k, up, :] - p[k, down, :]))
    return wet, u_trial, v_trial


def damping(u, v):
    return 1.0 / (1.0 + drag_coef * jnp.sqrt(u * u + v * v))


FLUX = time_step * 0.5 / 12.0
HEIGHT = time_step / LEVELS * 0.5 / FLUX


def flux(q0, q1, qm, qp, tr, md):
    return tr * (7.0 * (q0 + q1) - (qm + qp)) - md * (q1 - q0)


def north_flux(k, r, n, vel, m_north, tracers, g_refs):
    here, up = pl.ds(r, n), pl.ds(r + 1, n)
    mn = m_north[k, here, :]
    tr = (FLUX * mn) * (vel[k, here, :] + vel[k, up, :])
    md = (time_step * diffusivity) * mn
    out = []
    for q, g in zip(tracers, g_refs):
        gy = flux(q[k, here, :], q[k, up, :], q[k, pl.ds(r - 1, n), :], q[k, pl.ds(r + 2, n), :], tr, md)
        g[k, here, :] = gy
        out.append(gy)
    return tr, out


def east_flux(k, r, n, u_next, m_east, tracers):
    here = pl.ds(r, n)
    me = m_east[k, here, :]
    tr = (FLUX * me) * (u_next + east(u_next))
    md = (time_step * diffusivity) * me
    out = []
    for q_ref in tracers:
        q = q_ref[k, here, :]
        out.append((q, flux(q, east(q), west(q), pltpu.roll(q, LANES - 2, 1), tr, md)))
    return tr, out


def main_kernel(t, s, u, v, w, e, p, t_out, s_out, u_out, v_out, h_out, me, mn, vel, gt, gs, hy):
    rows = h_out.shape[0]

    def loop(start, count, body):
        if count == 1:
            body(start)
            return

        def step(i, _):
            body(pl.multiple_of(start + i * MAIN_ROWS, 8))
            return 0

        lax.fori_loop(0, count, step, 0)

    def velocities(n, store):
        def body(r):
            here = pl.ds(r, n)
            spin = coriolis_rows(r, n, rows)
            trial = [velocity_trial(k, r, n, spin, u, v, w, p, me, mn) for k in range(LEVELS)]
            at_floor = [trial[k][0] > (trial[k + 1][0] if k + 1 < LEVELS else 0.0) for k in range(LEVELS)]
            u_floor, v_floor = trial[0][1], trial[0][2]
            for k in range(1, LEVELS):
                u_floor = jnp.where(at_floor[k], trial[k][1], u_floor)
                v_floor = jnp.where(at_floor[k], trial[k][2], v_floor)
            damp = damping(u_floor, v_floor)
            for k in range(LEVELS):
                factor = jnp.where(at_floor[k], damp, trial[k][0])
                v_next = factor * trial[k][2]
                vel[k, here, :] = v_next
                if store:
                    out = pl.ds(pl.multiple_of(r - BASE, 8), n)
                    u_out[k, out, :] = factor * trial[k][1]
                    v_out[k, out, :] = v_next

        return body

    def south_edge(r):
        total = 0.0
        for k in range(LEVELS):
            total = total + north_flux(k, r, 8, vel, mn, (t, s), (gt, gs))[0]
        hy[pl.ds(r, 8), :] = total

    def tracer(r):
        n = MAIN_ROWS
        here, down = pl.ds(r, n), pl.ds(r - 1, n)
        out = pl.ds(pl.multiple_of(r - BASE, 8), n)
        total_x = total_y = 0.0
        for k in range(LEVELS):
            tr_y, (gy_t, gy_s) = north_flux(k, r, n, vel, mn, (t, s), (gt, gs))
            tr_x, ((tc, gx_t), (sc, gx_s)) = east_flux(k, r, n, u_out[k, out, :], me, (t, s))
            total_x, total_y = total_x + tr_x, total_y + tr_y
            wet = w[k, here, :]
            t_out[k, out, :] = wet * (tc - (gx_t - west(gx_t) + (gy_t - gt[k, down, :])))
            s_out[k, out, :] = wet * (sc - (gx_s - west(gx_s) + (gy_s - gs[k, down, :])))
        hy[here, :] = total_y
        h_out[out, :] = e[here, :] - HEIGHT * (total_x - west(total_x) + (total_y - hy[down, :]))

    count = rows // MAIN_ROWS
    loop(BASE - 8, 1, velocities(8, False))
    loop(BASE + rows, 1, velocities(8, False))
    loop(BASE, count, velocities(MAIN_ROWS, True))
    south_edge(BASE - 8)
    loop(BASE, count, tracer)


def main(arrays, rows):
    big = pltpu.VMEM(arrays[0].shape, F32)
    out3 = pltpu.VMEM((LEVELS, rows, LANES), F32)
    return pl.pallas_call(
        main_kernel,
        in_specs=[VMEM] * 7,
        out_specs=[VMEM] * 5,
        out_shape=[out3] * 4 + [pltpu.VMEM((rows, LANES), F32)],
        scratch_shapes=[big] * 5 + [pltpu.VMEM(arrays[5].shape, F32)],
        compiler_params=params(16),
        cost_estimate=pl.CostEstimate(flops=40_000_000, bytes_accessed=8_000_000, transcendentals=100_000),
        name="main",
    )(*arrays)


def edge_kernel(c_ref, m0_ref, m1_ref, t_in, s_in, u_in, v_in, h_in, t_hbm, s_hbm, u_hbm, v_hbm, h_hbm,
                t, s, u, v, w, e, p, me, mn, un, vel, gt, gs, hy, ot, os, ou, ov, oh, sems):
    rows = h_in.shape[0]
    even = is_even("lon")

    def layout(n):
        lane = lanes(n)
        return lane, lane // 16, lane % 16

    def spread(source, place, n):
        lane, level, slot = layout(n)
        own = jnp.where(slot < 4, slot, jnp.where((slot >= 8) & (slot < 12), slot - 4, 0))
        other = jnp.where((slot == 5) | (slot == 7), 1, 0)
        from_east = (slot == 4) | (slot == 5)
        from_west = (slot == 6) | (slot == 7)
        src, here = pl.ds(source, n), pl.ds(place, n)
        m0, m1 = m0_ref[src, :], m1_ref[src, :]
        m_east, m_west = jnp.where(even, m0, m1), jnp.where(even, m1, m0)

        def strip(packed, own_lane, ghost_lane):
            return jnp.where(
                from_east,
                gather(m_east, ghost_lane),
                jnp.where(from_west, gather(m_west, ghost_lane), gather(packed, own_lane)),
            )

        for f, x in enumerate((t, s, u, v, w)):
            packed = c_ref[src, (f // 2) * LANES : (f // 2 + 1) * LANES]
            x[0, here, :] = strip(packed, 8 * level + own + 64 * (f % 2), 2 * level + other + 2 * LEVELS * f)
        e[here, :] = strip(c_ref[src, 2 * LANES : 3 * LANES], own + 64, other + 2 * (PLANES - 1))

    def strip_pressure(r, n):
        here = pl.ds(r, n)
        lane = lanes(n)
        h = density_half(t[0, here, :], s[0, here, :])
        total = h
        for step in (16, 32, 64):
            total = total + jnp.where(lane >= step, pltpu.roll(total, step, 1), 0.0)
        p[0, here, :] = (gravity * 0.5 * time_step) * e[here, :] + (2.0 * total - h)

    def velocities(r, n):
        here = pl.ds(r, n)
        lane = lanes(n)
        wet, u_trial, v_trial = velocity_trial(0, r, n, coriolis_rows(r, n, rows), u, v, w, p, me, mn)
        below = jnp.where(lane < LANES - 16, pltpu.roll(wet, LANES - 16, 1), 0.0)
        factor = jnp.where(wet > below, damping(u_trial, v_trial), wet)
        un[0, here, :] = factor * u_trial
        vel[0, here, :] = factor * v_trial

    def joined(strip, slot):
        return jnp.where(slot < 4, strip, pltpu.roll(strip, LANES - 4, 1))

    def tracer(r, n):
        lane, level, slot = layout(n)
        edge = (lane < 2) | (lane >= LANES - 2)
        here, down = pl.ds(r, n), pl.ds(r - 1, n)
        out = pl.ds(r - BASE, n)
        u_next = un[0, here, :]
        tr_y, (gy_t, gy_s) = north_flux(0, r, n, vel, mn, (t, s), (gt, gs))
        tr_x, ((tc, gx_t), (sc, gx_s)) = east_flux(0, r, n, u_next, me, (t, s))
        wet = w[0, here, :]
        hy[here, :] = tr_y
        strips = (
            wet * (tc - (gx_t - west(gx_t) + (gy_t - gt[0, down, :]))),
            wet * (sc - (gx_s - west(gx_s) + (gy_s - gs[0, down, :]))),
            u_next,
            vel[0, here, :],
        )
        for strip, main_in, out_ref in zip(strips, (t_in, s_in, u_in, v_in), (ot, os, ou, ov)):
            wide = joined(strip, slot)
            for k in range(LEVELS):
                placed = pltpu.roll(wide, (-(16 * k + 4)) % LANES, 1)
                out_ref[k, out, :] = jnp.where(edge, placed, main_in[k, out, :])
        inflow = tr_x - west(tr_x) + (tr_y - hy[down, :])
        for step in (16, 32, 64):
            inflow = inflow + pltpu.roll(inflow, step, 1)
        wide = joined(e[here, :] - HEIGHT * inflow, slot)
        oh[out, :] = jnp.where(edge, pltpu.roll(wide, LANES - 4, 1), h_in[out, :])

    spread(0, BASE, rows + 8)
    strip_pressure(BASE, rows + 8)
    for x in (t, s, u, v, w, p):
        x[0, pl.ds(BASE - 8, 8), :] = x[0, pl.ds(BASE + rows, 8), :]
    e[pl.ds(BASE - 8, 8), :] = e[pl.ds(BASE + rows, 8), :]
    velocities(BASE - 8, rows + 16)
    hy[pl.ds(BASE - 8, 8), :] = north_flux(0, BASE - 8, 8, vel, mn, (t, s), (gt, gs))[0]
    copies = []
    block = rows // EDGE_CHUNKS
    for c in range(EDGE_CHUNKS):
        tracer(BASE + c * block, block)
        at = pl.ds(c * block, block)
        for n, (x, y) in enumerate(((ot, t_hbm), (os, s_hbm), (ou, u_hbm), (ov, v_hbm))):
            copies.append(pltpu.make_async_copy(x.at[:, at, :], y.at[:, at, :], sems.at[c * 5 + n]))
        copies.append(pltpu.make_async_copy(oh.at[at, :], h_hbm.at[at, :], sems.at[c * 5 + 4]))
        for x in copies[-5:]:
            x.start()
    for x in copies:
        x.wait()


def edges(c, m0, m1, outs):
    rows = outs[4].shape[0]
    tall = rows + BASE + 16
    big = pltpu.VMEM((1, tall, LANES), F32)
    flat = pltpu.VMEM((tall, LANES), F32)
    out3 = jax.ShapeDtypeStruct((LEVELS, rows, LANES), F32)
    wide = pltpu.VMEM((LEVELS, rows, LANES), F32)
    return pl.pallas_call(
        edge_kernel,
        in_specs=[VMEM] * 8,
        out_specs=[HBM] * 5,
        out_shape=[out3] * 4 + [jax.ShapeDtypeStruct((rows, LANES), F32)],
        scratch_shapes=[big] * 5
        + [flat]
        + [big] * 7
        + [flat]
        + [wide] * 4
        + [pltpu.VMEM((rows, LANES), F32), pltpu.SemaphoreType.DMA((5 * EDGE_CHUNKS,))],
        compiler_params=params(16),
        name="edges",
    )(c, m0, m1, *outs)


def swaps():
    lon, lat = lax.axis_size("lon"), lax.axis_size("lat")

    def device(o, a):
        return o % lon * lat + a

    lat_first, lat_second, lon_first, lon_second = [], [], [], []
    for o in range(lon):
        for a in range(lat):
            lat_first.append((device(o, a), device(o, a ^ 1)))
            if a == lat - 1:
                lat_second.append((device(o, a), device(lon - 1 - o, a)))
            elif a > 0:
                lat_second.append((device(o, a), device(o, a + 1 if a % 2 else a - 1)))
            lon_first.append((device(o, a), device(o ^ 1, a)))
            lon_second.append((device(o, a), device(o + 1 if o % 2 else o - 1, a)))
    return lat_first, lat_second, lon_first, lon_second


def on_device(
    heat_anomaly,
    saltiness_anomaly,
    zonal_current,
    meridional_current,
    free_elevation,
    ocean_indicator,
    floor_layer_index,
):
    lat_first, lat_second, lon_first, lon_second = swaps()
    send = functools.partial(lax.ppermute, axis_name=("lon", "lat"))
    fields = (heat_anomaly, saltiness_anomaly, zonal_current, meridional_current, ocean_indicator)
    a, b = row_pack(fields, free_elevation)
    a = send(a, perm=lat_first)
    b = send(b, perm=lat_second)
    arrays = column_pack(fields, free_elevation)
    *arrays, c, m0, m1 = ghosts(a, b, arrays)
    m0 = send(m0, perm=lon_first)
    m1 = send(m1, perm=lon_second)
    outs = main(arrays, free_elevation.shape[0])
    return tuple(edges(c, m0, m1, outs))


def solution(mesh):
    return jax.shard_map(
        on_device,
        mesh=mesh,
        in_specs=(
            P(None, "lat", "lon"),
            P(None, "lat", "lon"),
            P(None, "lat", "lon"),
            P(None, "lat", "lon"),
            P("lat", "lon"),
            P(None, "lat", "lon"),
            P("lat", "lon"),
        ),
        out_specs=(
            P(None, "lat", "lon"),
            P(None, "lat", "lon"),
            P(None, "lat", "lon"),
            P(None, "lat", "lon"),
            P("lat", "lon"),
        ),
        check_vma=False,
    )
```

```python
import functools

import jax
import jax.numpy as jnp
from jax import lax
from jax.experimental import pallas as pl
from jax.experimental.pallas import tpu as pltpu
from jax.sharding import PartitionSpec as P

F32 = jnp.float32
BF16 = jnp.bfloat16
LEVELS = 8
LANES = 128
FIELDS = 5
PLANES = FIELDS * LEVELS + 1
ROW_MSG = 2 * FIELDS * LEVELS + 8
BASE = 16
PACK_ROWS = 96
MAIN_ROWS = 96
LAST_CHUNKS = 2

time_step = 0.2
viscosity = 0.5
diffusivity = 0.3
press_scale = 0.25
gravity = 1.0
drag_coef = 1.0
coriolis_max = 0.5

HBM = pl.BlockSpec(memory_space=pltpu.HBM)
VMEM = pl.BlockSpec(memory_space=pltpu.VMEM)


def params(mib):
    return pltpu.CompilerParams(vmem_limit_bytes=int(mib * 1024 * 1024))


def lanes(rows=8):
    return lax.broadcasted_iota(jnp.int32, (rows, LANES), 1)


def east(x):
    return pltpu.roll(x, LANES - 1, 1)


def west(x):
    return pltpu.roll(x, 1, 1)


def gather(x, index):
    return jnp.take_along_axis(x, index, axis=1)


def strip_layout(rows):
    lane = lanes(rows)
    return lane, lane // 16, lane % 16


def own_strips(packed, rows):
    _, level, slot = strip_layout(rows)
    own = jnp.where(slot < 4, slot, jnp.where((slot >= 8) & (slot < 12), slot - 4, 0))
    out = [gather(packed[f // 2], 8 * level + own + 64 * (f % 2)) for f in range(FIELDS)]
    return out + [gather(packed[2], own + 64)]


def split(x):
    high = x.astype(BF16)
    rest = x - high.astype(F32)
    middle = rest.astype(BF16)
    return high, middle, (rest - middle.astype(F32)).astype(BF16)


def face_matrix():
    row = lax.broadcasted_iota(jnp.int32, (LANES, LANES), 0)
    step = lax.rem(row - lax.broadcasted_iota(jnp.int32, (LANES, LANES), 1) + LANES, LANES)
    face = jnp.where(step < 2, 7.0, jnp.where((step == 2) | (step == LANES - 1), -1.0, 0.0))
    slope = jnp.where(step == 1, 1.0, jnp.where(step == 0, -1.0, 0.0))
    return jnp.concatenate([face, slope], axis=1).astype(BF16)


def is_even(axis):
    return lax.rem(lax.axis_index(axis), 2) == 0


def row_pack_kernel(*refs):
    ins, (a_ref, b_ref), tiles, sems = refs[:6], refs[6:8], refs[8:20], refs[20]
    rows = ins[5].shape[0]
    copies = []
    for n, x in enumerate(ins):
        for side, start in enumerate((0, rows - 8)):
            src = x.at[:, pl.ds(start, 8), :] if n < FIELDS else x.at[pl.ds(start, 8), :]
            copies.append(pltpu.make_async_copy(src, tiles[2 * n + side], sems.at[2 * n + side]))
            copies[-1].start()
    for x in copies:
        x.wait()
    even = is_even("lat")
    for r in range(2):
        for f in range(FIELDS):
            low, high = tiles[2 * f : 2 * f + 2]
            bottom = low.reshape(LEVELS * 8, LANES)[pl.ds(r, LEVELS, stride=8), :].astype(F32)
            top = high.reshape(LEVELS * 8, LANES)[pl.ds(6 + r, LEVELS, stride=8), :].astype(F32)
            place = pl.ds((r * FIELDS + f) * LEVELS, LEVELS)
            a_ref[place, :] = jnp.where(even, top, bottom)
            b_ref[place, :] = jnp.where(even, bottom, top)
    place = pl.ds(2 * FIELDS * LEVELS, 8)
    low, high = tiles[10][...], tiles[11][...]
    a_ref[place, :] = jnp.where(even, high, low)
    b_ref[place, :] = jnp.where(even, low, high)


def row_pack(fields, surface):
    scratch = [pltpu.VMEM((LEVELS, 8, LANES), x.dtype) for x in fields for _ in range(2)]
    scratch += [pltpu.VMEM((8, LANES), F32)] * 2 + [pltpu.SemaphoreType.DMA((12,))]
    return pl.pallas_call(
        row_pack_kernel,
        in_specs=[HBM] * 6,
        out_specs=[VMEM] * 2,
        out_shape=[pltpu.VMEM((ROW_MSG, LANES), F32)] * 2,
        scratch_shapes=scratch,
        compiler_params=params(60),
        name="row_pack",
    )(*fields, surface)


def pack_columns(plane, rows):
    lane = lanes(rows)
    packed = []
    for first in range(0, PLANES, 16):
        group = None
        for p in range(first, min(first + 16, PLANES)):
            q = p - first
            moved = pltpu.roll(plane(p), (8 * q + 4) % LANES, 1)
            group = moved if group is None else jnp.where(lane >= 8 * q, moved, group)
        packed.append(group)
    return packed


def column_messages(packed, even, rows):
    lane = lanes(rows)
    base = 8 * ((lane // 2) % 16) + lane % 2
    messages = []
    for first in (True, False):
        eastern = even if first else jnp.logical_not(even)
        index = base + jnp.where(eastern, 2, 4)
        c0, c1, c2 = [gather(c, index) for c in packed]
        messages.append(jnp.where(lane < 32, c0, jnp.where(lane < 64, c1, c2)))
    return messages


def column_pack_kernel(t_in, s_in, u_in, v_in, w_in, e_in, t, s, u, v, w, e, p, c_ref, m0_ref, m1_ref, face, slope):
    rows = e_in.shape[0]
    even = is_even("lon")
    matrix = face_matrix()

    def step(i, _):
        out = pl.ds(pl.multiple_of(i * PACK_ROWS, 8), PACK_ROWS)
        here = pl.ds(pl.multiple_of(BASE + i * PACK_ROWS, 8), PACK_ROWS)
        for x, y in ((t_in, t), (s_in, s), (u_in, u), (v_in, v), (w_in, w)):
            for k in range(LEVELS):
                y[k, here, :] = x[k, out, :].astype(F32)
        e[here, :] = e_in[out, :]

        def plane(q):
            if q == PLANES - 1:
                return e_in[out, :]
            return (t_in, s_in, u_in, v_in, w_in)[q // LEVELS][q % LEVELS, out, :].astype(F32)

        packed = pack_columns(plane, PACK_ROWS)
        for n, x in enumerate(own_strips(packed, PACK_ROWS)):
            c_ref[n, out, :] = x
        m0_ref[out, :], m1_ref[out, :] = column_messages(packed, even, PACK_ROWS)
        total = (gravity * 0.5 * time_step) * e_in[out, :]
        for k in range(LEVELS):
            h = density_half(t_in[k, out, :], s_in[k, out, :])
            at = total + h
            p[k, here, :] = at
            total = at + h
        for n, x in enumerate((t_in, s_in)):
            for k in range(LEVELS):
                both = sum(jnp.dot(part, matrix, preferred_element_type=F32) for part in split(x[k, out, :])[::-1])
                face[n * LEVELS + k, out, :] = both[:, :LANES]
                slope[n * LEVELS + k, out, :] = both[:, LANES:]
        return 0

    lax.fori_loop(0, rows // PACK_ROWS, step, 0)


def column_pack(fields, surface):
    rows = surface.shape[0]
    tall = rows + BASE + 16
    big = pltpu.VMEM((LEVELS, tall, LANES), F32)
    return pl.pallas_call(
        column_pack_kernel,
        in_specs=[VMEM] * 6,
        out_specs=[VMEM] * 12,
        out_shape=[big] * 5
        + [pltpu.VMEM((tall, LANES), F32), big]
        + [pltpu.VMEM((FIELDS + 1, rows + 8, LANES), F32)]
        + [pltpu.VMEM((rows + 8, LANES), F32)] * 2
        + [pltpu.VMEM((2 * LEVELS, rows, LANES), F32)] * 2,
        compiler_params=params(16),
        cost_estimate=pl.CostEstimate(flops=10_000_000, bytes_accessed=6_000_000, transcendentals=0),
        name="column_pack",
    )(*fields, surface)


def ghost_kernel(a_ref, b_ref, *refs):
    t, s, u, v, w, e, p, c_ref, m0_ref, m1_ref, g_ref = refs[10:]
    rows = m0_ref.shape[0] - 8
    even = is_even("lat")
    fold = lax.axis_index("lat") == lax.axis_size("lat") - 1
    mirror = LANES - 1 - lanes()
    flat = g_ref.reshape(PLANES * 8, LANES)
    g_ref[...] = jnp.zeros_like(g_ref)

    def both(start):
        a, b = a_ref[pl.ds(start, 8), :], b_ref[pl.ds(start, 8), :]
        return jnp.where(even, a, b), jnp.where(even, b, a)

    for f in range(FIELDS):
        sign = -1.0 if f in (2, 3) else 1.0
        north0, south0 = both(f * LEVELS)
        north1, south1 = both((FIELDS + f) * LEVELS)
        first = jnp.where(fold, sign * gather(north1, mirror), north0)
        second = jnp.where(fold, sign * gather(north0, mirror), north1)
        for row, value in ((0, first), (1, second), (6, south0), (7, south1)):
            flat[pl.ds(f * LEVELS * 8 + row, LEVELS, stride=8), :] = value
    north, south = both(2 * FIELDS * LEVELS)
    turned = gather(north, mirror)
    row = lax.broadcasted_iota(jnp.int32, (8, LANES), 0)
    folded = jnp.where(row == 0, pltpu.roll(turned, 1, 0), pltpu.roll(turned, 3, 0))
    g_ref[PLANES - 1] = jnp.where(row < 2, jnp.where(fold, folded, north), jnp.where(row >= 6, south, 0.0))
    packed = pack_columns(lambda q: g_ref[q], 8)
    last = pl.ds(rows, 8)
    for n, x in enumerate(own_strips(packed, 8)):
        c_ref[n, last, :] = x
    m0_ref[last, :], m1_ref[last, :] = column_messages(packed, is_even("lon"), 8)
    for side in (pl.ds(BASE - 8, 8), pl.ds(BASE + rows, 8)):
        for f, x in enumerate((t, s, u, v, w)):
            for k in range(LEVELS):
                x[k, side, :] = g_ref[f * LEVELS + k]
        e[side, :] = g_ref[PLANES - 1]
        pressure(side, t, s, e, p)


def ghosts(a, b, arrays):
    return pl.pallas_call(
        ghost_kernel,
        in_specs=[VMEM] * 12,
        out_specs=[VMEM] * 10,
        out_shape=[pltpu.VMEM(x.shape, F32) for x in arrays],
        scratch_shapes=[pltpu.VMEM((PLANES, 8, LANES), F32)],
        input_output_aliases={n + 2: n for n in range(10)},
        compiler_params=params(8),
        name="ghosts",
    )(a, b, *arrays)


def density_half(t, s):
    k = 0.5 * press_scale * 0.5 * time_step
    return t * (-0.2 * k + (-0.05 * k) * t + (0.02 * k) * s) + (0.8 * k) * s


def pressure(here, t, s, e, p):
    total = (gravity * 0.5 * time_step) * e[here, :]
    for k in range(LEVELS):
        h = density_half(t[k, here, :], s[k, here, :])
        at = total + h
        p[k, here, :] = at
        total = at + h


def coriolis_rows(start, count, rows):
    total = rows * lax.axis_size("lat")
    row = lax.broadcasted_iota(jnp.int32, (count, LANES), 0) + (start - BASE + lax.axis_index("lat") * rows)
    row = jnp.minimum(row, total - 1).astype(F32)
    return (time_step * coriolis_max) * (2.0 * (row + 0.5) / total - 1.0)


def velocity_trial(k, r, n, spin, u, v, w, p, m_east, m_north):
    here, up, down = pl.ds(r, n), pl.ds(r + 1, n), pl.ds(r - 1, n)
    wet = w[k, here, :]
    me = wet * east(wet)
    mw = wet * west(wet)
    mn = wet * w[k, up, :]
    ms = wet * w[k, down, :]
    m_east[k, here, :] = me
    m_north[k, here, :] = mn

    def lap(q_ref, q):
        return me * (east(q) - q) + mw * (west(q) - q) + (mn * (q_ref[k, up, :] - q) + ms * (q_ref[k, down, :] - q))

    un, vn = u[k, here, :], v[k, here, :]
    pc = p[k, here, :]
    u_trial = un + (spin * vn - (east(pc) - west(pc)) + (time_step * viscosity) * lap(u, un))
    v_trial = vn + ((time_step * viscosity) * lap(v, vn) - spin * un - (p[k, up, :] - p[k, down, :]))
    return wet, u_trial, v_trial


def damping(u, v):
    return 1.0 / (1.0 + drag_coef * jnp.sqrt(u * u + v * v))


FLUX = time_step * 0.5 / 12.0
HEIGHT = time_step / LEVELS * 0.5 / FLUX


def flux(q0, q1, qm, qp, tr, md):
    return tr * (7.0 * (q0 + q1) - (qm + qp)) - md * (q1 - q0)


def north_flux(k, r, n, vel, m_north, tracers, g_refs):
    here, up = pl.ds(r, n), pl.ds(r + 1, n)
    mn = m_north[k, here, :]
    tr = (FLUX * mn) * (vel[k, here, :] + vel[k, up, :])
    md = (time_step * diffusivity) * mn
    out = []
    for q, g in zip(tracers, g_refs):
        gy = flux(q[k, here, :], q[k, up, :], q[k, pl.ds(r - 1, n), :], q[k, pl.ds(r + 2, n), :], tr, md)
        g[k, here, :] = gy
        out.append(gy)
    return tr, out


def east_flux(k, r, n, u_next, m_east, tracers):
    here = pl.ds(r, n)
    me = m_east[k, here, :]
    tr = (FLUX * me) * (u_next + east(u_next))
    md = (time_step * diffusivity) * me
    out = []
    for q_ref in tracers:
        q = q_ref[k, here, :]
        out.append((q, flux(q, east(q), west(q), pltpu.roll(q, LANES - 2, 1), tr, md)))
    return tr, out


def velocity_kernel(u, v, w, p, un, vel, me, mn):
    rows = un.shape[1]

    def velocities(r, n, store):
        here = pl.ds(r, n)
        spin = coriolis_rows(r, n, rows)
        trial = [velocity_trial(k, r, n, spin, u, v, w, p, me, mn) for k in range(LEVELS)]
        at_floor = [trial[k][0] > (trial[k + 1][0] if k + 1 < LEVELS else 0.0) for k in range(LEVELS)]
        u_floor, v_floor = trial[0][1], trial[0][2]
        for k in range(1, LEVELS):
            u_floor = jnp.where(at_floor[k], trial[k][1], u_floor)
            v_floor = jnp.where(at_floor[k], trial[k][2], v_floor)
        damp = damping(u_floor, v_floor)
        for k in range(LEVELS):
            factor = jnp.where(at_floor[k], damp, trial[k][0])
            vel[k, here, :] = factor * trial[k][2]
            if store:
                un[k, pl.ds(r - BASE, n), :] = factor * trial[k][1]

    velocities(BASE - 8, 8, False)
    velocities(BASE + rows, 8, False)

    def step(i, _):
        velocities(pl.multiple_of(BASE + i * MAIN_ROWS, 8), MAIN_ROWS, True)
        return 0

    lax.fori_loop(0, rows // MAIN_ROWS, step, 0)


def new_velocities(u, v, w, p, rows):
    big = pltpu.VMEM(u.shape, F32)
    return pl.pallas_call(
        velocity_kernel,
        in_specs=[VMEM] * 4,
        out_specs=[VMEM] * 4,
        out_shape=[pltpu.VMEM((LEVELS, rows, LANES), F32), big, big, big],
        compiler_params=params(16),
        cost_estimate=pl.CostEstimate(flops=20_000_000, bytes_accessed=6_000_000, transcendentals=100_000),
        name="velocities",
    )(u, v, w, p)


def last_kernel(c_ref, m0_ref, m1_ref, mt, ms, mw, mh, mu, mv, mme, mmn, mface, mslope, t_hbm, s_hbm, u_hbm, v_hbm, h_hbm,
                t, s, u, v, w, e, p, me, mn, un, vel, gt, gs, hy, mgt, mgs, mhy, st, ss, sh, ot, os, ou, ov, oh, sems):
    rows = oh.shape[0]
    even = is_even("lon")

    def complete(source, place, n):
        lane, level, slot = strip_layout(n)
        ghost = (slot >= 4) & (slot < 8)
        src, here = pl.ds(source, n), pl.ds(place, n)
        m0, m1 = m0_ref[src, :], m1_ref[src, :]
        m_east, m_west = jnp.where(even, m0, m1), jnp.where(even, m1, m0)
        four = jnp.where(lane < 64, m_east, pltpu.roll(m_west, 64, 1))
        rest = jnp.where(lane < 96, m_east, pltpu.roll(m_west, 32, 1))
        at = jnp.where(slot % 2 == 1, 1, 0)
        west_side = slot >= 6
        for f, x in enumerate((t, s, u, v)):
            other = gather(four, 2 * LEVELS * f + 2 * level + at + jnp.where(west_side, 64, 0))
            x[0, here, :] = jnp.where(ghost, other, c_ref[f, src, :])
        other = gather(rest, 64 + 2 * level + at + jnp.where(west_side, 32, 0))
        w[0, here, :] = jnp.where(ghost, other, c_ref[FIELDS - 1, src, :])
        other = gather(rest, 80 + at + jnp.where(west_side, 32, 0))
        e[here, :] = jnp.where(ghost, other, c_ref[FIELDS, src, :])

    def strip_pressure(r, n):
        here = pl.ds(r, n)
        lane = lanes(n)
        h = density_half(t[0, here, :], s[0, here, :])
        total = h
        for step in (16, 32, 64):
            total = total + jnp.where(lane >= step, pltpu.roll(total, step, 1), 0.0)
        p[0, here, :] = (gravity * 0.5 * time_step) * e[here, :] + (2.0 * total - h)

    def strip_velocities(r, n):
        here = pl.ds(r, n)
        lane = lanes(n)
        wet, u_trial, v_trial = velocity_trial(0, r, n, coriolis_rows(r, n, rows), u, v, w, p, me, mn)
        below = jnp.where(lane < LANES - 16, pltpu.roll(wet, LANES - 16, 1), 0.0)
        factor = jnp.where(wet > below, damping(u_trial, v_trial), wet)
        un[0, here, :] = factor * u_trial
        vel[0, here, :] = factor * v_trial

    def joined(strip):
        slot = strip_layout(strip.shape[0])[2]
        return jnp.where(slot < 4, strip, pltpu.roll(strip, LANES - 4, 1))

    def on_edge(n):
        lane = lanes(n)
        return (lane < 2) | (lane >= LANES - 2)

    def placed(wide, k):
        return pltpu.roll(wide, (-(16 * k + 4)) % LANES, 1)

    def strip_tracers(r, n):
        here, down = pl.ds(r, n), pl.ds(r - 1, n)
        out = pl.ds(r - BASE, n)
        tr_y, (gy_t, gy_s) = north_flux(0, r, n, vel, mn, (t, s), (gt, gs))
        tr_x, ((tc, gx_t), (sc, gx_s)) = east_flux(0, r, n, un[0, here, :], me, (t, s))
        wet = w[0, here, :]
        hy[here, :] = tr_y
        st[out, :] = joined(wet * (tc - (gx_t - west(gx_t) + (gy_t - gt[0, down, :]))))
        ss[out, :] = joined(wet * (sc - (gx_s - west(gx_s) + (gy_s - gs[0, down, :]))))
        inflow = tr_x - west(tr_x) + (tr_y - hy[down, :])
        for step in (16, 32, 64):
            inflow = inflow + pltpu.roll(inflow, step, 1)
        sh[out, :] = joined(e[here, :] - HEIGHT * inflow)

    def tracers(r, n):
        here, down = pl.ds(r, n), pl.ds(r - 1, n)
        out = pl.ds(r - BASE, n)
        edge = on_edge(n)
        wide_t, wide_s = st[out, :], ss[out, :]
        total_x = total_y = 0.0
        for k in range(LEVELS):
            tr_y, (gy_t, gy_s) = north_flux(k, r, n, mv, mmn, (mt, ms), (mgt, mgs))
            u_next = mu[k, out, :]
            mask = mme[k, here, :]
            tr_x = (FLUX * mask) * (u_next + east(u_next))
            md = (time_step * diffusivity) * mask
            gx_t = tr_x * mface[k, out, :] - md * mslope[k, out, :]
            gx_s = tr_x * mface[LEVELS + k, out, :] - md * mslope[LEVELS + k, out, :]
            tc, sc = mt[k, here, :], ms[k, here, :]
            total_x, total_y = total_x + tr_x, total_y + tr_y
            wet = mw[k, here, :]
            t_next = wet * (tc - (gx_t - west(gx_t) + (gy_t - mgt[k, down, :])))
            s_next = wet * (sc - (gx_s - west(gx_s) + (gy_s - mgs[k, down, :])))
            ot[k, out, :] = jnp.where(edge, placed(wide_t, k), t_next)
            os[k, out, :] = jnp.where(edge, placed(wide_s, k), s_next)
        mhy[here, :] = total_y
        height = mh[here, :] - HEIGHT * (total_x - west(total_x) + (total_y - mhy[down, :]))
        oh[out, :] = jnp.where(edge, placed(sh[out, :], 0), height)

    copies = []

    def send(x, y):
        copies.append(pltpu.make_async_copy(x, y, sems.at[len(copies)]))
        copies[-1].start()

    complete(0, BASE, rows + 8)
    strip_pressure(BASE, rows + 8)
    for x in (t, s, u, v, w, p):
        x[0, pl.ds(BASE - 8, 8), :] = x[0, pl.ds(BASE + rows, 8), :]
    e[pl.ds(BASE - 8, 8), :] = e[pl.ds(BASE + rows, 8), :]
    strip_velocities(BASE - 8, rows + 16)
    south = pl.ds(BASE - 8, 8)
    hy[south, :] = north_flux(0, BASE - 8, 8, vel, mn, (t, s), (gt, gs))[0]
    total = 0.0
    for k in range(LEVELS):
        total = total + north_flux(k, BASE - 8, 8, mv, mmn, (mt, ms), (mgt, mgs))[0]
    mhy[south, :] = total
    whole = pl.ds(BASE, rows)
    edge = on_edge(rows)
    wide_u, wide_v = joined(un[0, whole, :]), joined(vel[0, whole, :])
    for k in range(LEVELS):
        ou[k] = jnp.where(edge, placed(wide_u, k), mu[k])
        ov[k] = jnp.where(edge, placed(wide_v, k), mv[k, whole, :])
    send(ou, u_hbm)
    send(ov, v_hbm)
    strip_tracers(BASE, rows)
    block = rows // LAST_CHUNKS
    for c in range(LAST_CHUNKS):
        tracers(BASE + c * block, block)
        at = pl.ds(c * block, block)
        send(ot.at[:, at, :], t_hbm.at[:, at, :])
        send(os.at[:, at, :], s_hbm.at[:, at, :])
    send(oh, h_hbm)
    for x in copies:
        x.wait()


def last(c, m0, m1, t, s, w, e, un, vel, me, mn, face, slope):
    rows, tall = un.shape[1], t.shape[1]
    big = pltpu.VMEM((1, tall, LANES), F32)
    flat = pltpu.VMEM((tall, LANES), F32)
    high = pltpu.VMEM((LEVELS, tall, LANES), F32)
    short = pltpu.VMEM((rows, LANES), F32)
    out3 = jax.ShapeDtypeStruct((LEVELS, rows, LANES), F32)
    wide = pltpu.VMEM((LEVELS, rows, LANES), F32)
    return pl.pallas_call(
        last_kernel,
        in_specs=[VMEM] * 13,
        out_specs=[HBM] * 5,
        out_shape=[out3] * 4 + [jax.ShapeDtypeStruct((rows, LANES), F32)],
        scratch_shapes=[big] * 5
        + [flat]
        + [big] * 7
        + [flat]
        + [high, high, flat]
        + [short] * 3
        + [wide] * 4
        + [short, pltpu.SemaphoreType.DMA((3 + 2 * LAST_CHUNKS,))],
        compiler_params=params(24),
        name="last",
    )(c, m0, m1, t, s, w, e, un, vel, me, mn, face, slope)


def swaps():
    lon, lat = lax.axis_size("lon"), lax.axis_size("lat")

    def device(o, a):
        return o % lon * lat + a

    lat_first, lat_second, lon_first, lon_second = [], [], [], []
    for o in range(lon):
        for a in range(lat):
            lat_first.append((device(o, a), device(o, a ^ 1)))
            if a == lat - 1:
                lat_second.append((device(o, a), device(lon - 1 - o, a)))
            elif a > 0:
                lat_second.append((device(o, a), device(o, a + 1 if a % 2 else a - 1)))
            lon_first.append((device(o, a), device(o ^ 1, a)))
            lon_second.append((device(o, a), device(o + 1 if o % 2 else o - 1, a)))
    return lat_first, lat_second, lon_first, lon_second


def on_device(
    heat_anomaly,
    saltiness_anomaly,
    zonal_current,
    meridional_current,
    free_elevation,
    ocean_indicator,
    floor_layer_index,
):
    lat_first, lat_second, lon_first, lon_second = swaps()
    send = functools.partial(lax.ppermute, axis_name=("lon", "lat"))
    fields = (heat_anomaly, saltiness_anomaly, zonal_current, meridional_current, ocean_indicator)
    a, b = row_pack(fields, free_elevation)
    a = send(a, perm=lat_first)
    b = send(b, perm=lat_second)
    *arrays, face, slope = column_pack(fields, free_elevation)
    t, s, u, v, w, e, p, c, m0, m1 = ghosts(a, b, arrays)
    m0 = send(m0, perm=lon_first)
    m1 = send(m1, perm=lon_second)
    un, vel, me, mn = new_velocities(u, v, w, p, free_elevation.shape[0])
    return tuple(last(c, m0, m1, t, s, w, e, un, vel, me, mn, face, slope))


def solution(mesh):
    return jax.shard_map(
        on_device,
        mesh=mesh,
        in_specs=(
            P(None, "lat", "lon"),
            P(None, "lat", "lon"),
            P(None, "lat", "lon"),
            P(None, "lat", "lon"),
            P("lat", "lon"),
            P(None, "lat", "lon"),
            P("lat", "lon"),
        ),
        out_specs=(
            P(None, "lat", "lon"),
            P(None, "lat", "lon"),
            P(None, "lat", "lon"),
            P(None, "lat", "lon"),
            P("lat", "lon"),
        ),
        check_vma=False,
    )
```

```python
import functools

import jax
import jax.numpy as jnp
from jax import lax
from jax.experimental import pallas as pl
from jax.experimental.pallas import tpu as pltpu
from jax.sharding import PartitionSpec as P

F32 = jnp.float32
BF16 = jnp.bfloat16
LEVELS = 8
LANES = 128
FIELDS = 5
PLANES = FIELDS * LEVELS + 1
ROW_MSG = 2 * FIELDS * LEVELS + 8
BASE = 16
PACK_ROWS = 96
MAIN_ROWS = 192
LAST_CHUNKS = 2

time_step = 0.2
viscosity = 0.5
diffusivity = 0.3
press_scale = 0.25
gravity = 1.0
drag_coef = 1.0
coriolis_max = 0.5

HBM = pl.BlockSpec(memory_space=pltpu.HBM)
VMEM = pl.BlockSpec(memory_space=pltpu.VMEM)


def params(mib):
    return pltpu.CompilerParams(vmem_limit_bytes=int(mib * 1024 * 1024))


def lanes(rows=8):
    return lax.broadcasted_iota(jnp.int32, (rows, LANES), 1)


def east(x):
    return pltpu.roll(x, LANES - 1, 1)


def west(x):
    return pltpu.roll(x, 1, 1)


def gather(x, index):
    return jnp.take_along_axis(x, index, axis=1)


def strip_layout(rows):
    lane = lanes(rows)
    return lane, lane // 16, lane % 16


def own_strips(packed, rows):
    _, level, slot = strip_layout(rows)
    own = jnp.where(slot < 4, slot, jnp.where((slot >= 8) & (slot < 12), slot - 4, 0))
    out = [gather(packed[f // 2], 8 * level + own + 64 * (f % 2)) for f in range(FIELDS)]
    return out + [gather(packed[2], own + 64)]


def split(x):
    high = x.astype(BF16)
    rest = x - high.astype(F32)
    middle = rest.astype(BF16)
    return high, middle, (rest - middle.astype(F32)).astype(BF16)


def face_matrix():
    step = lane_step()
    face = jnp.where(step < 2, 7.0, jnp.where((step == 2) | (step == LANES - 1), -1.0, 0.0))
    slope = jnp.where(step == 1, 1.0, jnp.where(step == 0, -1.0, 0.0))
    return jnp.concatenate([face, slope], axis=1).astype(BF16)


def product(x, matrix):
    return sum(jnp.dot(part, matrix, preferred_element_type=F32) for part in split(x)[::-1])


def lane_step():
    row = lax.broadcasted_iota(jnp.int32, (LANES, LANES), 0)
    return lax.rem(row - lax.broadcasted_iota(jnp.int32, (LANES, LANES), 1) + LANES, LANES)


def neighbour_matrix():
    step = lane_step()
    return jnp.concatenate([jnp.where(step == 1, 1.0, 0.0), jnp.where(step == LANES - 1, 1.0, 0.0)], axis=1).astype(BF16)


def difference_matrix():
    step = lane_step()
    return jnp.where(step == 1, 1.0, jnp.where(step == LANES - 1, -1.0, 0.0)).astype(BF16)


def place_matrix(level):
    lane, row = (lax.broadcasted_iota(jnp.int32, (LANES, LANES), n) for n in (1, 0))
    slot = jnp.where(lane < 2, lane + 8, jnp.where(lane >= LANES - 2, lane - (LANES - 4), -LANES))
    return jnp.where(row == 16 * level + slot, 1.0, 0.0).astype(BF16)


def is_even(axis):
    return lax.rem(lax.axis_index(axis), 2) == 0


def row_pack_kernel(*refs):
    ins, (a_ref, b_ref), tiles, sems = refs[:6], refs[6:8], refs[8:20], refs[20]
    rows = ins[5].shape[0]
    copies = []
    for n, x in enumerate(ins):
        for side, start in enumerate((0, rows - 8)):
            src = x.at[:, pl.ds(start, 8), :] if n < FIELDS else x.at[pl.ds(start, 8), :]
            copies.append(pltpu.make_async_copy(src, tiles[2 * n + side], sems.at[2 * n + side]))
            copies[-1].start()
    for x in copies:
        x.wait()
    even = is_even("lat")
    for r in range(2):
        for f in range(FIELDS):
            low, high = tiles[2 * f : 2 * f + 2]
            bottom = low.reshape(LEVELS * 8, LANES)[pl.ds(r, LEVELS, stride=8), :].astype(F32)
            top = high.reshape(LEVELS * 8, LANES)[pl.ds(6 + r, LEVELS, stride=8), :].astype(F32)
            place = pl.ds((r * FIELDS + f) * LEVELS, LEVELS)
            a_ref[place, :] = jnp.where(even, top, bottom)
            b_ref[place, :] = jnp.where(even, bottom, top)
    place = pl.ds(2 * FIELDS * LEVELS, 8)
    low, high = tiles[10][...], tiles[11][...]
    a_ref[place, :] = jnp.where(even, high, low)
    b_ref[place, :] = jnp.where(even, low, high)


def row_pack(fields, surface):
    scratch = [pltpu.VMEM((LEVELS, 8, LANES), x.dtype) for x in fields for _ in range(2)]
    scratch += [pltpu.VMEM((8, LANES), F32)] * 2 + [pltpu.SemaphoreType.DMA((12,))]
    return pl.pallas_call(
        row_pack_kernel,
        in_specs=[HBM] * 6,
        out_specs=[VMEM] * 2,
        out_shape=[pltpu.VMEM((ROW_MSG, LANES), F32)] * 2,
        scratch_shapes=scratch,
        compiler_params=params(60),
        name="row_pack",
    )(*fields, surface)


def pack_columns(plane, rows):
    lane = lanes(rows)
    packed = []
    for first in range(0, PLANES, 16):
        group = None
        for p in range(first, min(first + 16, PLANES)):
            q = p - first
            moved = pltpu.roll(plane(p), (8 * q + 4) % LANES, 1)
            group = moved if group is None else jnp.where(lane >= 8 * q, moved, group)
        packed.append(group)
    return packed


def column_messages(packed, even, rows):
    lane = lanes(rows)
    base = 8 * ((lane // 2) % 16) + lane % 2
    messages = []
    for first in (True, False):
        eastern = even if first else jnp.logical_not(even)
        index = base + jnp.where(eastern, 2, 4)
        c0, c1, c2 = [gather(c, index) for c in packed]
        messages.append(jnp.where(lane < 32, c0, jnp.where(lane < 64, c1, c2)))
    return messages


def column_pack_kernel(t_in, s_in, u_in, v_in, w_in, e_in, t, s, u, v, w, e, p, c_ref, m0_ref, m1_ref, face, slope, place):
    rows = e_in.shape[0]
    even = is_even("lon")
    matrix = face_matrix()
    for k in range(LEVELS):
        place[:, k * LANES : (k + 1) * LANES] = place_matrix(k)

    def step(i, _):
        out = pl.ds(pl.multiple_of(i * PACK_ROWS, 8), PACK_ROWS)
        here = pl.ds(pl.multiple_of(BASE + i * PACK_ROWS, 8), PACK_ROWS)
        for x, y in ((t_in, t), (s_in, s), (u_in, u), (v_in, v), (w_in, w)):
            for k in range(LEVELS):
                y[k, here, :] = x[k, out, :].astype(F32)
        e[here, :] = e_in[out, :]

        def plane(q):
            if q == PLANES - 1:
                return e_in[out, :]
            return (t_in, s_in, u_in, v_in, w_in)[q // LEVELS][q % LEVELS, out, :].astype(F32)

        packed = pack_columns(plane, PACK_ROWS)
        for n, x in enumerate(own_strips(packed, PACK_ROWS)):
            c_ref[n, out, :] = x
        m0_ref[out, :], m1_ref[out, :] = column_messages(packed, even, PACK_ROWS)
        total = (gravity * 0.5 * time_step) * e_in[out, :]
        for k in range(LEVELS):
            h = density_half(t_in[k, out, :], s_in[k, out, :])
            at = total + h
            p[k, here, :] = at
            total = at + h
        for n, x in enumerate((t_in, s_in)):
            for k in range(LEVELS):
                both = product(x[k, out, :], matrix)
                face[n * LEVELS + k, out, :] = both[:, :LANES]
                slope[n * LEVELS + k, out, :] = both[:, LANES:]
        return 0

    lax.fori_loop(0, rows // PACK_ROWS, step, 0)


def column_pack(fields, surface):
    rows = surface.shape[0]
    tall = rows + BASE + 16
    big = pltpu.VMEM((LEVELS, tall, LANES), F32)
    return pl.pallas_call(
        column_pack_kernel,
        in_specs=[VMEM] * 6,
        out_specs=[VMEM] * 13,
        out_shape=[big] * 5
        + [pltpu.VMEM((tall, LANES), F32), big]
        + [pltpu.VMEM((FIELDS + 1, rows + 8, LANES), F32)]
        + [pltpu.VMEM((rows + 8, LANES), F32)] * 2
        + [pltpu.VMEM((2 * LEVELS, rows, LANES), F32)] * 2
        + [pltpu.VMEM((LANES, LEVELS * LANES), BF16)],
        compiler_params=params(16),
        cost_estimate=pl.CostEstimate(flops=10_000_000, bytes_accessed=6_000_000, transcendentals=0),
        name="column_pack",
    )(*fields, surface)


def ghost_kernel(a_ref, b_ref, *refs):
    t, s, u, v, w, e, p, c_ref, m0_ref, m1_ref, g_ref = refs[10:]
    rows = m0_ref.shape[0] - 8
    even = is_even("lat")
    fold = lax.axis_index("lat") == lax.axis_size("lat") - 1
    mirror = LANES - 1 - lanes()
    flat = g_ref.reshape(PLANES * 8, LANES)
    g_ref[...] = jnp.zeros_like(g_ref)

    def both(start):
        a, b = a_ref[pl.ds(start, 8), :], b_ref[pl.ds(start, 8), :]
        return jnp.where(even, a, b), jnp.where(even, b, a)

    for f in range(FIELDS):
        sign = -1.0 if f in (2, 3) else 1.0
        north0, south0 = both(f * LEVELS)
        north1, south1 = both((FIELDS + f) * LEVELS)
        first = jnp.where(fold, sign * gather(north1, mirror), north0)
        second = jnp.where(fold, sign * gather(north0, mirror), north1)
        for row, value in ((0, first), (1, second), (6, south0), (7, south1)):
            flat[pl.ds(f * LEVELS * 8 + row, LEVELS, stride=8), :] = value
    north, south = both(2 * FIELDS * LEVELS)
    turned = gather(north, mirror)
    row = lax.broadcasted_iota(jnp.int32, (8, LANES), 0)
    folded = jnp.where(row == 0, pltpu.roll(turned, 1, 0), pltpu.roll(turned, 3, 0))
    g_ref[PLANES - 1] = jnp.where(row < 2, jnp.where(fold, folded, north), jnp.where(row >= 6, south, 0.0))
    packed = pack_columns(lambda q: g_ref[q], 8)
    last = pl.ds(rows, 8)
    for n, x in enumerate(own_strips(packed, 8)):
        c_ref[n, last, :] = x
    m0_ref[last, :], m1_ref[last, :] = column_messages(packed, is_even("lon"), 8)
    for side in (pl.ds(BASE - 8, 8), pl.ds(BASE + rows, 8)):
        for f, x in enumerate((t, s, u, v, w)):
            for k in range(LEVELS):
                x[k, side, :] = g_ref[f * LEVELS + k]
        e[side, :] = g_ref[PLANES - 1]
        pressure(side, t, s, e, p)


def ghosts(a, b, arrays):
    return pl.pallas_call(
        ghost_kernel,
        in_specs=[VMEM] * 12,
        out_specs=[VMEM] * 10,
        out_shape=[pltpu.VMEM(x.shape, F32) for x in arrays],
        scratch_shapes=[pltpu.VMEM((PLANES, 8, LANES), F32)],
        input_output_aliases={n + 2: n for n in range(10)},
        compiler_params=params(8),
        name="ghosts",
    )(a, b, *arrays)


def density_half(t, s):
    k = 0.5 * press_scale * 0.5 * time_step
    return t * (-0.2 * k + (-0.05 * k) * t + (0.02 * k) * s) + (0.8 * k) * s


def pressure(here, t, s, e, p):
    total = (gravity * 0.5 * time_step) * e[here, :]
    for k in range(LEVELS):
        h = density_half(t[k, here, :], s[k, here, :])
        at = total + h
        p[k, here, :] = at
        total = at + h


def coriolis_rows(start, count, rows):
    total = rows * lax.axis_size("lat")
    row = lax.broadcasted_iota(jnp.int32, (count, LANES), 0) + (start - BASE + lax.axis_index("lat") * rows)
    row = jnp.minimum(row, total - 1).astype(F32)
    return (time_step * coriolis_max) * (2.0 * (row + 0.5) / total - 1.0)


def velocity_trial(k, r, n, spin, u, v, w, p, m_east, m_north, matrices=None):
    here, up, down = pl.ds(r, n), pl.ds(r + 1, n), pl.ds(r - 1, n)
    wet = w[k, here, :]
    pc = p[k, here, :]
    if matrices is None:
        wet_east, wet_west, slope = east(wet), west(wet), east(pc) - west(pc)
    else:
        both = jnp.dot(wet.astype(BF16), matrices[0], preferred_element_type=F32)
        wet_east, wet_west, slope = both[:, :LANES], both[:, LANES:], product(pc, matrices[1])
    me = wet * wet_east
    mw = wet * wet_west
    mn = wet * w[k, up, :]
    ms = wet * w[k, down, :]
    m_east[k, here, :] = me
    m_north[k, here, :] = mn

    def lap(q_ref, q):
        return me * (east(q) - q) + mw * (west(q) - q) + (mn * (q_ref[k, up, :] - q) + ms * (q_ref[k, down, :] - q))

    un, vn = u[k, here, :], v[k, here, :]
    u_trial = un + (spin * vn - slope + (time_step * viscosity) * lap(u, un))
    v_trial = vn + ((time_step * viscosity) * lap(v, vn) - spin * un - (p[k, up, :] - p[k, down, :]))
    return wet, u_trial, v_trial


def damping(u, v):
    return 1.0 / (1.0 + drag_coef * jnp.sqrt(u * u + v * v))


FLUX = time_step * 0.5 / 12.0
HEIGHT = time_step / LEVELS * 0.5 / FLUX


def flux(q0, q1, qm, qp, tr, md):
    return tr * (7.0 * (q0 + q1) - (qm + qp)) - md * (q1 - q0)


def north_flux(k, r, n, vel, m_north, tracers, g_refs):
    here, up = pl.ds(r, n), pl.ds(r + 1, n)
    mn = m_north[k, here, :]
    tr = (FLUX * mn) * (vel[k, here, :] + vel[k, up, :])
    md = (time_step * diffusivity) * mn
    out = []
    for q, g in zip(tracers, g_refs):
        gy = flux(q[k, here, :], q[k, up, :], q[k, pl.ds(r - 1, n), :], q[k, pl.ds(r + 2, n), :], tr, md)
        g[k, here, :] = gy
        out.append(gy)
    return tr, out


def east_flux(k, r, n, u_next, m_east, tracers):
    here = pl.ds(r, n)
    me = m_east[k, here, :]
    tr = (FLUX * me) * (u_next + east(u_next))
    md = (time_step * diffusivity) * me
    out = []
    for q_ref in tracers:
        q = q_ref[k, here, :]
        out.append((q, flux(q, east(q), west(q), pltpu.roll(q, LANES - 2, 1), tr, md)))
    return tr, out


def velocity_kernel(u, v, w, p, un, vel, me, mn):
    rows = un.shape[1]
    matrices = neighbour_matrix(), difference_matrix()

    def velocities(r, n, store):
        here = pl.ds(r, n)
        spin = coriolis_rows(r, n, rows)
        on_unit = matrices if n % 16 == 0 else None
        trial = [velocity_trial(k, r, n, spin, u, v, w, p, me, mn, on_unit) for k in range(LEVELS)]
        at_floor = [trial[k][0] > (trial[k + 1][0] if k + 1 < LEVELS else 0.0) for k in range(LEVELS)]
        u_floor, v_floor = trial[0][1], trial[0][2]
        for k in range(1, LEVELS):
            u_floor = jnp.where(at_floor[k], trial[k][1], u_floor)
            v_floor = jnp.where(at_floor[k], trial[k][2], v_floor)
        damp = damping(u_floor, v_floor)
        for k in range(LEVELS):
            factor = jnp.where(at_floor[k], damp, trial[k][0])
            vel[k, here, :] = factor * trial[k][2]
            if store:
                un[k, pl.ds(r - BASE, n), :] = factor * trial[k][1]

    velocities(BASE - 8, 8, False)
    velocities(BASE + rows, 8, False)

    def step(i, _):
        velocities(pl.multiple_of(BASE + i * MAIN_ROWS, 8), MAIN_ROWS, True)
        return 0

    lax.fori_loop(0, rows // MAIN_ROWS, step, 0)


def new_velocities(u, v, w, p, rows):
    big = pltpu.VMEM(u.shape, F32)
    return pl.pallas_call(
        velocity_kernel,
        in_specs=[VMEM] * 4,
        out_specs=[VMEM] * 4,
        out_shape=[pltpu.VMEM((LEVELS, rows, LANES), F32), big, big, big],
        compiler_params=params(16),
        cost_estimate=pl.CostEstimate(flops=20_000_000, bytes_accessed=6_000_000, transcendentals=100_000),
        name="velocities",
    )(u, v, w, p)


def last_kernel(c_ref, m0_ref, m1_ref, mt, ms, mw, mh, mu, mv, mme, mmn, mface, mslope, place, t_hbm, s_hbm, u_hbm, v_hbm, h_hbm,
                t, s, u, v, w, e, p, me, mn, un, vel, gt, gs, hy, mgt, mgs, mhy, st, ss, sh, ot, os, ou, ov, oh, sems):
    rows = oh.shape[0]
    even = is_even("lon")

    def complete(source, place, n):
        lane, level, slot = strip_layout(n)
        ghost = (slot >= 4) & (slot < 8)
        src, here = pl.ds(source, n), pl.ds(place, n)
        m0, m1 = m0_ref[src, :], m1_ref[src, :]
        m_east, m_west = jnp.where(even, m0, m1), jnp.where(even, m1, m0)
        four = jnp.where(lane < 64, m_east, pltpu.roll(m_west, 64, 1))
        rest = jnp.where(lane < 96, m_east, pltpu.roll(m_west, 32, 1))
        at = jnp.where(slot % 2 == 1, 1, 0)
        west_side = slot >= 6
        for f, x in enumerate((t, s, u, v)):
            other = gather(four, 2 * LEVELS * f + 2 * level + at + jnp.where(west_side, 64, 0))
            x[0, here, :] = jnp.where(ghost, other, c_ref[f, src, :])
        other = gather(rest, 64 + 2 * level + at + jnp.where(west_side, 32, 0))
        w[0, here, :] = jnp.where(ghost, other, c_ref[FIELDS - 1, src, :])
        other = gather(rest, 80 + at + jnp.where(west_side, 32, 0))
        e[here, :] = jnp.where(ghost, other, c_ref[FIELDS, src, :])

    def strip_pressure(r, n):
        here = pl.ds(r, n)
        lane = lanes(n)
        h = density_half(t[0, here, :], s[0, here, :])
        total = h
        for step in (16, 32, 64):
            total = total + jnp.where(lane >= step, pltpu.roll(total, step, 1), 0.0)
        p[0, here, :] = (gravity * 0.5 * time_step) * e[here, :] + (2.0 * total - h)

    def strip_velocities(r, n):
        here = pl.ds(r, n)
        lane = lanes(n)
        wet, u_trial, v_trial = velocity_trial(0, r, n, coriolis_rows(r, n, rows), u, v, w, p, me, mn)
        below = jnp.where(lane < LANES - 16, pltpu.roll(wet, LANES - 16, 1), 0.0)
        factor = jnp.where(wet > below, damping(u_trial, v_trial), wet)
        un[0, here, :] = factor * u_trial
        vel[0, here, :] = factor * v_trial

    def on_edge(n):
        lane = lanes(n)
        return (lane < 2) | (lane >= LANES - 2)

    def placed(strip, levels=LEVELS):
        out = []
        for k in range(0, levels, 2):
            both = product(strip, place[:, k * LANES : (k + 2) * LANES])
            out += [both[:, :LANES], both[:, LANES:]]
        return out

    def strip_tracers(r, n):
        here, down = pl.ds(r, n), pl.ds(r - 1, n)
        out = pl.ds(r - BASE, n)
        tr_y, (gy_t, gy_s) = north_flux(0, r, n, vel, mn, (t, s), (gt, gs))
        tr_x, ((tc, gx_t), (sc, gx_s)) = east_flux(0, r, n, un[0, here, :], me, (t, s))
        wet = w[0, here, :]
        hy[here, :] = tr_y
        st[out, :] = wet * (tc - (gx_t - west(gx_t) + (gy_t - gt[0, down, :])))
        ss[out, :] = wet * (sc - (gx_s - west(gx_s) + (gy_s - gs[0, down, :])))
        inflow = tr_x - west(tr_x) + (tr_y - hy[down, :])
        for step in (16, 32, 64):
            inflow = inflow + pltpu.roll(inflow, step, 1)
        sh[out, :] = e[here, :] - HEIGHT * inflow

    def tracers(r, n):
        here, down = pl.ds(r, n), pl.ds(r - 1, n)
        out = pl.ds(r - BASE, n)
        edge = on_edge(n)
        wide_t, wide_s = placed(st[out, :]), placed(ss[out, :])
        total_x = total_y = 0.0
        for k in range(LEVELS):
            tr_y, (gy_t, gy_s) = north_flux(k, r, n, mv, mmn, (mt, ms), (mgt, mgs))
            u_next = mu[k, out, :]
            mask = mme[k, here, :]
            tr_x = (FLUX * mask) * (u_next + east(u_next))
            md = (time_step * diffusivity) * mask
            gx_t = tr_x * mface[k, out, :] - md * mslope[k, out, :]
            gx_s = tr_x * mface[LEVELS + k, out, :] - md * mslope[LEVELS + k, out, :]
            tc, sc = mt[k, here, :], ms[k, here, :]
            total_x, total_y = total_x + tr_x, total_y + tr_y
            wet = mw[k, here, :]
            t_next = wet * (tc - (gx_t - west(gx_t) + (gy_t - mgt[k, down, :])))
            s_next = wet * (sc - (gx_s - west(gx_s) + (gy_s - mgs[k, down, :])))
            ot[k, out, :] = jnp.where(edge, wide_t[k], t_next)
            os[k, out, :] = jnp.where(edge, wide_s[k], s_next)
        mhy[here, :] = total_y
        height = mh[here, :] - HEIGHT * (total_x - west(total_x) + (total_y - mhy[down, :]))
        oh[out, :] = jnp.where(edge, placed(sh[out, :], 2)[0], height)

    copies = []

    def send(x, y):
        copies.append(pltpu.make_async_copy(x, y, sems.at[len(copies)]))
        copies[-1].start()

    complete(0, BASE, rows + 8)
    strip_pressure(BASE, rows + 8)
    for x in (t, s, u, v, w, p):
        x[0, pl.ds(BASE - 8, 8), :] = x[0, pl.ds(BASE + rows, 8), :]
    e[pl.ds(BASE - 8, 8), :] = e[pl.ds(BASE + rows, 8), :]
    strip_velocities(BASE - 8, rows + 16)
    south = pl.ds(BASE - 8, 8)
    hy[south, :] = north_flux(0, BASE - 8, 8, vel, mn, (t, s), (gt, gs))[0]
    total = 0.0
    for k in range(LEVELS):
        total = total + north_flux(k, BASE - 8, 8, mv, mmn, (mt, ms), (mgt, mgs))[0]
    mhy[south, :] = total
    whole = pl.ds(BASE, rows)
    edge = on_edge(rows)
    wide_u, wide_v = placed(un[0, whole, :]), placed(vel[0, whole, :])
    for k in range(LEVELS):
        ou[k] = jnp.where(edge, wide_u[k], mu[k])
        ov[k] = jnp.where(edge, wide_v[k], mv[k, whole, :])
    send(ou, u_hbm)
    send(ov, v_hbm)
    strip_tracers(BASE, rows)
    block = rows // LAST_CHUNKS
    for c in range(LAST_CHUNKS):
        tracers(BASE + c * block, block)
        at = pl.ds(c * block, block)
        send(ot.at[:, at, :], t_hbm.at[:, at, :])
        send(os.at[:, at, :], s_hbm.at[:, at, :])
    send(oh, h_hbm)
    for x in copies:
        x.wait()


def last(c, m0, m1, t, s, w, e, un, vel, me, mn, face, slope, place):
    rows, tall = un.shape[1], t.shape[1]
    big = pltpu.VMEM((1, tall, LANES), F32)
    flat = pltpu.VMEM((tall, LANES), F32)
    high = pltpu.VMEM((LEVELS, tall, LANES), F32)
    short = pltpu.VMEM((rows, LANES), F32)
    out3 = jax.ShapeDtypeStruct((LEVELS, rows, LANES), F32)
    wide = pltpu.VMEM((LEVELS, rows, LANES), F32)
    return pl.pallas_call(
        last_kernel,
        in_specs=[VMEM] * 14,
        out_specs=[HBM] * 5,
        out_shape=[out3] * 4 + [jax.ShapeDtypeStruct((rows, LANES), F32)],
        scratch_shapes=[big] * 5
        + [flat]
        + [big] * 7
        + [flat]
        + [high, high, flat]
        + [short] * 3
        + [wide] * 4
        + [short, pltpu.SemaphoreType.DMA((3 + 2 * LAST_CHUNKS,))],
        compiler_params=params(24),
        name="last",
    )(c, m0, m1, t, s, w, e, un, vel, me, mn, face, slope, place)


def swaps():
    lon, lat = lax.axis_size("lon"), lax.axis_size("lat")

    def device(o, a):
        return o % lon * lat + a

    lat_first, lat_second, lon_first, lon_second = [], [], [], []
    for o in range(lon):
        for a in range(lat):
            lat_first.append((device(o, a), device(o, a ^ 1)))
            if a == lat - 1:
                lat_second.append((device(o, a), device(lon - 1 - o, a)))
            elif a > 0:
                lat_second.append((device(o, a), device(o, a + 1 if a % 2 else a - 1)))
            lon_first.append((device(o, a), device(o ^ 1, a)))
            lon_second.append((device(o, a), device(o + 1 if o % 2 else o - 1, a)))
    return lat_first, lat_second, lon_first, lon_second


def on_device(
    heat_anomaly,
    saltiness_anomaly,
    zonal_current,
    meridional_current,
    free_elevation,
    ocean_indicator,
    floor_layer_index,
):
    lat_first, lat_second, lon_first, lon_second = swaps()
    send = functools.partial(lax.ppermute, axis_name=("lon", "lat"))
    fields = (heat_anomaly, saltiness_anomaly, zonal_current, meridional_current, ocean_indicator)
    a, b = row_pack(fields, free_elevation)
    a = send(a, perm=lat_first)
    b = send(b, perm=lat_second)
    *arrays, face, slope, place = column_pack(fields, free_elevation)
    t, s, u, v, w, e, p, c, m0, m1 = ghosts(a, b, arrays)
    m0 = send(m0, perm=lon_first)
    m1 = send(m1, perm=lon_second)
    un, vel, me, mn = new_velocities(u, v, w, p, free_elevation.shape[0])
    return tuple(last(c, m0, m1, t, s, w, e, un, vel, me, mn, face, slope, place))


def solution(mesh):
    return jax.shard_map(
        on_device,
        mesh=mesh,
        in_specs=(
            P(None, "lat", "lon"),
            P(None, "lat", "lon"),
            P(None, "lat", "lon"),
            P(None, "lat", "lon"),
            P("lat", "lon"),
            P(None, "lat", "lon"),
            P("lat", "lon"),
        ),
        out_specs=(
            P(None, "lat", "lon"),
            P(None, "lat", "lon"),
            P(None, "lat", "lon"),
            P(None, "lat", "lon"),
            P("lat", "lon"),
        ),
        check_vma=False,
    )
```

```python
import functools

import jax
import jax.numpy as jnp
from jax import lax
from jax.experimental import pallas as pl
from jax.experimental.pallas import tpu as pltpu
from jax.sharding import PartitionSpec as P

F32 = jnp.float32
BF16 = jnp.bfloat16
LEVELS = 8
LANES = 128
FIELDS = 5
PLANES = FIELDS * LEVELS + 1
ROW_MSG = 2 * FIELDS * LEVELS + 8
BASE = 16
PACK_ROWS = 96
REST_ROWS = 32
REST_LANES = 2 * LEVELS + 2
MAIN_ROWS = 192
LAST_CHUNKS = 2

time_step = 0.2
viscosity = 0.5
diffusivity = 0.3
press_scale = 0.25
gravity = 1.0
drag_coef = 1.0
coriolis_max = 0.5

HBM = pl.BlockSpec(memory_space=pltpu.HBM)
VMEM = pl.BlockSpec(memory_space=pltpu.VMEM)


def params(mib):
    return pltpu.CompilerParams(vmem_limit_bytes=int(mib * 1024 * 1024))


def lanes(rows=8):
    return lax.broadcasted_iota(jnp.int32, (rows, LANES), 1)


def east(x):
    return pltpu.roll(x, LANES - 1, 1)


def west(x):
    return pltpu.roll(x, 1, 1)


def gather(x, index):
    return jnp.take_along_axis(x, index, axis=1)


def strip_layout(rows):
    lane = lanes(rows)
    return lane, lane // 16, lane % 16


def own_strips(packed, rows):
    _, level, slot = strip_layout(rows)
    own = jnp.where(slot < 4, slot, jnp.where((slot >= 8) & (slot < 12), slot - 4, 0))
    out = [gather(packed[f // 2], 8 * level + own + 64 * (f % 2)) for f in range(FIELDS)]
    return out + [gather(packed[2], own + 64)]


def split(x):
    high = x.astype(BF16)
    rest = x - high.astype(F32)
    middle = rest.astype(BF16)
    return high, middle, (rest - middle.astype(F32)).astype(BF16)


def face_matrix():
    step = lane_step()
    face = jnp.where(step < 2, 7.0, jnp.where((step == 2) | (step == LANES - 1), -1.0, 0.0))
    slope = jnp.where(step == 1, 1.0, jnp.where(step == 0, -1.0, 0.0))
    return jnp.concatenate([face, slope], axis=1).astype(BF16)


def product(x, matrix):
    return sum(jnp.dot(part, matrix, preferred_element_type=F32) for part in split(x)[::-1])


def lane_step():
    row = lax.broadcasted_iota(jnp.int32, (LANES, LANES), 0)
    return lax.rem(row - lax.broadcasted_iota(jnp.int32, (LANES, LANES), 1) + LANES, LANES)


def neighbour_matrix():
    step = lane_step()
    return jnp.concatenate([jnp.where(step == 1, 1.0, 0.0), jnp.where(step == LANES - 1, 1.0, 0.0)], axis=1).astype(BF16)


def difference_matrix():
    step = lane_step()
    return jnp.where(step == 1, 1.0, jnp.where(step == LANES - 1, -1.0, 0.0)).astype(BF16)


def place_matrix(level):
    lane, row = (lax.broadcasted_iota(jnp.int32, (LANES, LANES), n) for n in (1, 0))
    slot = jnp.where(lane < 2, lane + 8, jnp.where(lane >= LANES - 2, lane - (LANES - 4), -LANES))
    return jnp.where(row == 16 * level + slot, 1.0, 0.0).astype(BF16)


def is_even(axis):
    return lax.rem(lax.axis_index(axis), 2) == 0


def row_pack_kernel(*refs):
    ins, (a_ref, b_ref), tiles, sems = refs[:6], refs[6:8], refs[8:20], refs[20]
    rows = ins[5].shape[0]
    copies = []
    for n, x in enumerate(ins):
        for side, start in enumerate((0, rows - 8)):
            src = x.at[:, pl.ds(start, 8), :] if n < FIELDS else x.at[pl.ds(start, 8), :]
            copies.append(pltpu.make_async_copy(src, tiles[2 * n + side], sems.at[2 * n + side]))
            copies[-1].start()
    for x in copies:
        x.wait()
    even = is_even("lat")
    for r in range(2):
        for f in range(FIELDS):
            low, high = tiles[2 * f : 2 * f + 2]
            bottom = low.reshape(LEVELS * 8, LANES)[pl.ds(r, LEVELS, stride=8), :].astype(F32)
            top = high.reshape(LEVELS * 8, LANES)[pl.ds(6 + r, LEVELS, stride=8), :].astype(F32)
            place = pl.ds((r * FIELDS + f) * LEVELS, LEVELS)
            a_ref[place, :] = jnp.where(even, top, bottom)
            b_ref[place, :] = jnp.where(even, bottom, top)
    place = pl.ds(2 * FIELDS * LEVELS, 8)
    low, high = tiles[10][...], tiles[11][...]
    a_ref[place, :] = jnp.where(even, high, low)
    b_ref[place, :] = jnp.where(even, low, high)


def row_pack(fields, surface):
    scratch = [pltpu.VMEM((LEVELS, 8, LANES), x.dtype) for x in fields for _ in range(2)]
    scratch += [pltpu.VMEM((8, LANES), F32)] * 2 + [pltpu.SemaphoreType.DMA((12,))]
    return pl.pallas_call(
        row_pack_kernel,
        in_specs=[HBM] * 6,
        out_specs=[VMEM] * 2,
        out_shape=[pltpu.VMEM((ROW_MSG, LANES), F32)] * 2,
        scratch_shapes=scratch,
        compiler_params=params(60),
        name="row_pack",
    )(*fields, surface)


def pack_columns(plane, rows):
    lane = lanes(rows)
    packed = []
    for first in range(0, PLANES, 16):
        group = None
        for p in range(first, min(first + 16, PLANES)):
            q = p - first
            moved = pltpu.roll(plane(p), (8 * q + 4) % LANES, 1)
            group = moved if group is None else jnp.where(lane >= 8 * q, moved, group)
        packed.append(group)
    return packed


def column_messages(packed, even, rows):
    lane = lanes(rows)
    base = 8 * ((lane // 2) % 16) + lane % 2
    messages = []
    for first in (True, False):
        eastern = even if first else jnp.logical_not(even)
        index = base + jnp.where(eastern, 2, 4)
        c0, c1, c2 = [gather(c, index) for c in packed]
        messages.append(jnp.where(lane < 32, c0, jnp.where(lane < 64, c1, c2)))
    return messages


def message_rows(rows):
    half = (rows + 8 + 15) // 16 * 8
    return half, half + REST_ROWS


def compact(message, rows):
    half, _ = message_rows(rows)
    lane = lanes(half)
    second = jnp.concatenate([message[half:rows, :], jnp.zeros((2 * half - rows, LANES), F32)], axis=0)
    main = jnp.where(lane < 64, message[:half, :], pltpu.roll(second, 64, 1))
    lane = lanes(REST_ROWS)
    rest = jnp.zeros((REST_ROWS, LANES), F32)
    for g in range(rows // REST_ROWS):
        part = pltpu.roll(message[g * REST_ROWS : (g + 1) * REST_ROWS, :], (REST_LANES * g - 64) % LANES, 1)
        rest = jnp.where((lane >= REST_LANES * g) & (lane < REST_LANES * (g + 1)), part, rest)
    return main, rest


def column_pack_kernel(t_in, s_in, u_in, v_in, w_in, e_in, t, s, u, v, w, e, p, c_ref, m0_ref, m1_ref, face, slope, place, m0_wide, m1_wide):
    rows = e_in.shape[0]
    even = is_even("lon")
    matrix = face_matrix()
    for k in range(LEVELS):
        place[:, k * LANES : (k + 1) * LANES] = place_matrix(k)

    def step(i, _):
        out = pl.ds(pl.multiple_of(i * PACK_ROWS, 8), PACK_ROWS)
        here = pl.ds(pl.multiple_of(BASE + i * PACK_ROWS, 8), PACK_ROWS)
        for x, y in ((t_in, t), (s_in, s), (u_in, u), (v_in, v), (w_in, w)):
            for k in range(LEVELS):
                y[k, here, :] = x[k, out, :].astype(F32)
        e[here, :] = e_in[out, :]

        def plane(q):
            if q == PLANES - 1:
                return e_in[out, :]
            return (t_in, s_in, u_in, v_in, w_in)[q // LEVELS][q % LEVELS, out, :].astype(F32)

        packed = pack_columns(plane, PACK_ROWS)
        for n, x in enumerate(own_strips(packed, PACK_ROWS)):
            c_ref[n, out, :] = x
        m0_wide[out, :], m1_wide[out, :] = column_messages(packed, even, PACK_ROWS)
        total = (gravity * 0.5 * time_step) * e_in[out, :]
        for k in range(LEVELS):
            h = density_half(t_in[k, out, :], s_in[k, out, :])
            at = total + h
            p[k, here, :] = at
            total = at + h
        for n, x in enumerate((t_in, s_in)):
            for k in range(LEVELS):
                both = product(x[k, out, :], matrix)
                face[n * LEVELS + k, out, :] = both[:, :LANES]
                slope[n * LEVELS + k, out, :] = both[:, LANES:]
        return 0

    lax.fori_loop(0, rows // PACK_ROWS, step, 0)
    half, _ = message_rows(rows)
    for wide, out in ((m0_wide, m0_ref), (m1_wide, m1_ref)):
        main, rest = compact(wide[...], rows)
        out[:half, :] = main
        out[half:, :] = rest


def column_pack(fields, surface):
    rows = surface.shape[0]
    tall = rows + BASE + 16
    big = pltpu.VMEM((LEVELS, tall, LANES), F32)
    return pl.pallas_call(
        column_pack_kernel,
        in_specs=[VMEM] * 6,
        out_specs=[VMEM] * 13,
        out_shape=[big] * 5
        + [pltpu.VMEM((tall, LANES), F32), big]
        + [pltpu.VMEM((FIELDS + 1, rows + 8, LANES), F32)]
        + [pltpu.VMEM((message_rows(rows)[1], LANES), F32)] * 2
        + [pltpu.VMEM((2 * LEVELS, rows, LANES), F32)] * 2
        + [pltpu.VMEM((LANES, LEVELS * LANES), BF16)],
        scratch_shapes=[pltpu.VMEM((rows, LANES), F32)] * 2,
        compiler_params=params(16),
        cost_estimate=pl.CostEstimate(flops=10_000_000, bytes_accessed=6_000_000, transcendentals=0),
        name="column_pack",
    )(*fields, surface)


def ghost_kernel(a_ref, b_ref, *refs):
    t, s, u, v, w, e, p, c_ref, m0_ref, m1_ref, g_ref = refs[10:]
    rows = c_ref.shape[1] - 8
    even = is_even("lat")
    fold = lax.axis_index("lat") == lax.axis_size("lat") - 1
    mirror = LANES - 1 - lanes()
    flat = g_ref.reshape(PLANES * 8, LANES)
    g_ref[...] = jnp.zeros_like(g_ref)

    southmost = lax.axis_index("lat") == 0

    def both(start):
        a, b = a_ref[pl.ds(start, 8), :], b_ref[pl.ds(start, 8), :]
        return jnp.where(even, a, b), jnp.where(southmost, 0.0, jnp.where(even, b, a))

    for f in range(FIELDS):
        sign = -1.0 if f in (2, 3) else 1.0
        north0, south0 = both(f * LEVELS)
        north1, south1 = both((FIELDS + f) * LEVELS)
        first = jnp.where(fold, sign * gather(north1, mirror), north0)
        second = jnp.where(fold, sign * gather(north0, mirror), north1)
        for row, value in ((0, first), (1, second), (6, south0), (7, south1)):
            flat[pl.ds(f * LEVELS * 8 + row, LEVELS, stride=8), :] = value
    north, south = both(2 * FIELDS * LEVELS)
    turned = gather(north, mirror)
    row = lax.broadcasted_iota(jnp.int32, (8, LANES), 0)
    folded = jnp.where(row == 0, pltpu.roll(turned, 1, 0), pltpu.roll(turned, 3, 0))
    g_ref[PLANES - 1] = jnp.where(row < 2, jnp.where(fold, folded, north), jnp.where(row >= 6, south, 0.0))
    packed = pack_columns(lambda q: g_ref[q], 8)
    last = pl.ds(rows, 8)
    for n, x in enumerate(own_strips(packed, 8)):
        c_ref[n, last, :] = x
    half, _ = message_rows(rows)
    lane = lanes()
    first = REST_LANES * (rows // REST_ROWS)
    for out, message in zip((m0_ref, m1_ref), column_messages(packed, is_even("lon"), 8)):
        place = pl.ds(rows - half, 8)
        out[place, :] = jnp.where(lane < 64, out[place, :], pltpu.roll(message, 64, 1))
        place = pl.ds(half, 8)
        moved = pltpu.roll(message, (first - 64) % LANES, 1)
        out[place, :] = jnp.where((lane >= first) & (lane < first + REST_LANES), moved, out[place, :])
    for side in (pl.ds(BASE - 8, 8), pl.ds(BASE + rows, 8)):
        for f, x in enumerate((t, s, u, v, w)):
            for k in range(LEVELS):
                x[k, side, :] = g_ref[f * LEVELS + k]
        e[side, :] = g_ref[PLANES - 1]
        pressure(side, t, s, e, p)


def ghosts(a, b, arrays):
    return pl.pallas_call(
        ghost_kernel,
        in_specs=[VMEM] * 12,
        out_specs=[VMEM] * 10,
        out_shape=[pltpu.VMEM(x.shape, F32) for x in arrays],
        scratch_shapes=[pltpu.VMEM((PLANES, 8, LANES), F32)],
        input_output_aliases={n + 2: n for n in range(10)},
        compiler_params=params(8),
        name="ghosts",
    )(a, b, *arrays)


def density_half(t, s):
    k = 0.5 * press_scale * 0.5 * time_step
    return t * (-0.2 * k + (-0.05 * k) * t + (0.02 * k) * s) + (0.8 * k) * s


def pressure(here, t, s, e, p):
    total = (gravity * 0.5 * time_step) * e[here, :]
    for k in range(LEVELS):
        h = density_half(t[k, here, :], s[k, here, :])
        at = total + h
        p[k, here, :] = at
        total = at + h


def coriolis_rows(start, count, rows):
    total = rows * lax.axis_size("lat")
    row = lax.broadcasted_iota(jnp.int32, (count, LANES), 0) + (start - BASE + lax.axis_index("lat") * rows)
    row = jnp.minimum(row, total - 1).astype(F32)
    return (time_step * coriolis_max) * (2.0 * (row + 0.5) / total - 1.0)


def velocity_trial(k, r, n, spin, u, v, w, p, m_east, m_north, matrices=None):
    here, up, down = pl.ds(r, n), pl.ds(r + 1, n), pl.ds(r - 1, n)
    wet = w[k, here, :]
    pc = p[k, here, :]
    if matrices is None:
        wet_east, wet_west, slope = east(wet), west(wet), east(pc) - west(pc)
    else:
        both = jnp.dot(wet.astype(BF16), matrices[0], preferred_element_type=F32)
        wet_east, wet_west, slope = both[:, :LANES], both[:, LANES:], product(pc, matrices[1])
    me = wet * wet_east
    mw = wet * wet_west
    mn = wet * w[k, up, :]
    ms = wet * w[k, down, :]
    m_east[k, here, :] = me
    m_north[k, here, :] = mn

    def lap(q_ref, q):
        return me * (east(q) - q) + mw * (west(q) - q) + (mn * (q_ref[k, up, :] - q) + ms * (q_ref[k, down, :] - q))

    un, vn = u[k, here, :], v[k, here, :]
    u_trial = un + (spin * vn - slope + (time_step * viscosity) * lap(u, un))
    v_trial = vn + ((time_step * viscosity) * lap(v, vn) - spin * un - (p[k, up, :] - p[k, down, :]))
    return wet, u_trial, v_trial


def damping(u, v):
    return 1.0 / (1.0 + drag_coef * jnp.sqrt(u * u + v * v))


FLUX = time_step * 0.5 / 12.0
HEIGHT = time_step / LEVELS * 0.5 / FLUX


def flux(q0, q1, qm, qp, tr, md):
    return tr * (7.0 * (q0 + q1) - (qm + qp)) - md * (q1 - q0)


def north_flux(k, r, n, vel, m_north, tracers, g_refs):
    here, up = pl.ds(r, n), pl.ds(r + 1, n)
    mn = m_north[k, here, :]
    tr = (FLUX * mn) * (vel[k, here, :] + vel[k, up, :])
    md = (time_step * diffusivity) * mn
    out = []
    for q, g in zip(tracers, g_refs):
        gy = flux(q[k, here, :], q[k, up, :], q[k, pl.ds(r - 1, n), :], q[k, pl.ds(r + 2, n), :], tr, md)
        g[k, here, :] = gy
        out.append(gy)
    return tr, out


def east_flux(k, r, n, u_next, m_east, tracers):
    here = pl.ds(r, n)
    me = m_east[k, here, :]
    tr = (FLUX * me) * (u_next + east(u_next))
    md = (time_step * diffusivity) * me
    out = []
    for q_ref in tracers:
        q = q_ref[k, here, :]
        out.append((q, flux(q, east(q), west(q), pltpu.roll(q, LANES - 2, 1), tr, md)))
    return tr, out


def velocity_kernel(u, v, w, p, un, vel, me, mn):
    rows = un.shape[1]
    matrices = neighbour_matrix(), difference_matrix()

    def velocities(r, n, store):
        here = pl.ds(r, n)
        spin = coriolis_rows(r, n, rows)
        on_unit = matrices if n % 16 == 0 else None
        trial = [velocity_trial(k, r, n, spin, u, v, w, p, me, mn, on_unit) for k in range(LEVELS)]
        at_floor = [trial[k][0] > (trial[k + 1][0] if k + 1 < LEVELS else 0.0) for k in range(LEVELS)]
        u_floor, v_floor = trial[0][1], trial[0][2]
        for k in range(1, LEVELS):
            u_floor = jnp.where(at_floor[k], trial[k][1], u_floor)
            v_floor = jnp.where(at_floor[k], trial[k][2], v_floor)
        damp = damping(u_floor, v_floor)
        for k in range(LEVELS):
            factor = jnp.where(at_floor[k], damp, trial[k][0])
            vel[k, here, :] = factor * trial[k][2]
            if store:
                un[k, pl.ds(r - BASE, n), :] = factor * trial[k][1]

    velocities(BASE - 8, 8, False)
    velocities(BASE + rows, 8, False)

    def step(i, _):
        velocities(pl.multiple_of(BASE + i * MAIN_ROWS, 8), MAIN_ROWS, True)
        return 0

    lax.fori_loop(0, rows // MAIN_ROWS, step, 0)


def new_velocities(u, v, w, p, rows):
    big = pltpu.VMEM(u.shape, F32)
    return pl.pallas_call(
        velocity_kernel,
        in_specs=[VMEM] * 4,
        out_specs=[VMEM] * 4,
        out_shape=[pltpu.VMEM((LEVELS, rows, LANES), F32), big, big, big],
        compiler_params=params(16),
        cost_estimate=pl.CostEstimate(flops=20_000_000, bytes_accessed=6_000_000, transcendentals=100_000),
        name="velocities",
    )(u, v, w, p)


def last_kernel(c_ref, m0_ref, m1_ref, mt, ms, mw, mh, mu, mv, mme, mmn, mface, mslope, place, t_hbm, s_hbm, u_hbm, v_hbm, h_hbm,
                t, s, u, v, w, e, p, me, mn, un, vel, gt, gs, hy, mgt, mgs, mhy, st, ss, sh, ot, os, ou, ov, oh, sems):
    rows = oh.shape[0]
    even = is_even("lon")

    def complete():
        n = rows + 8
        half, _ = message_rows(rows)
        m0, m1 = m0_ref[...], m1_ref[...]
        m_east, m_west = jnp.where(even, m0, m1), jnp.where(even, m1, m0)
        low = jnp.where(lanes(half) < 64, m_east[:half, :], pltpu.roll(m_west[:half, :], 64, 1))
        high = jnp.where(lanes(n - half) < 64, pltpu.roll(m_east[: n - half, :], 64, 1), m_west[: n - half, :])
        four = jnp.concatenate([low, high], axis=0)
        rest_east, rest_west = m_east[half:, :], pltpu.roll(m_west[half:, :], 64, 1)

        def slots(count):
            _, level, slot = strip_layout(count)
            west_side = jnp.where(slot >= 6, 64, 0)
            return level, (slot >= 4) & (slot < 8), west_side + jnp.where(slot % 2 == 1, 1, 0)

        level, ghost, at = slots(n)
        here = pl.ds(BASE, n)
        for f, x in enumerate((t, s, u, v)):
            x[0, here, :] = jnp.where(ghost, gather(four, 2 * LEVELS * f + 2 * level + at), c_ref[f])
        for g in range(-(-n // REST_ROWS)):
            count = min(REST_ROWS, n - g * REST_ROWS)
            level, ghost, at = slots(count)
            lane = lanes(count)
            mine = (lane >= REST_LANES * g) & (lane < REST_LANES * (g + 1))
            rest = jnp.where(mine, rest_east[:count, :], rest_west[:count, :])
            src, dst = pl.ds(g * REST_ROWS, count), pl.ds(BASE + g * REST_ROWS, count)
            index = (REST_LANES * g + 2 * level + at) % LANES
            w[0, dst, :] = jnp.where(ghost, gather(rest, index), c_ref[FIELDS - 1, src, :])
            index = (REST_LANES * g + 2 * LEVELS + at) % LANES
            e[dst, :] = jnp.where(ghost, gather(rest, index), c_ref[FIELDS, src, :])

    def strip_pressure(r, n):
        here = pl.ds(r, n)
        lane = lanes(n)
        h = density_half(t[0, here, :], s[0, here, :])
        total = h
        for step in (16, 32, 64):
            total = total + jnp.where(lane >= step, pltpu.roll(total, step, 1), 0.0)
        p[0, here, :] = (gravity * 0.5 * time_step) * e[here, :] + (2.0 * total - h)

    def strip_velocities(r, n):
        here = pl.ds(r, n)
        lane = lanes(n)
        wet, u_trial, v_trial = velocity_trial(0, r, n, coriolis_rows(r, n, rows), u, v, w, p, me, mn)
        below = jnp.where(lane < LANES - 16, pltpu.roll(wet, LANES - 16, 1), 0.0)
        factor = jnp.where(wet > below, damping(u_trial, v_trial), wet)
        un[0, here, :] = factor * u_trial
        vel[0, here, :] = factor * v_trial

    def on_edge(n):
        lane = lanes(n)
        return (lane < 2) | (lane >= LANES - 2)

    def placed(strip, levels=LEVELS):
        out = []
        for k in range(0, levels, 2):
            both = product(strip, place[:, k * LANES : (k + 2) * LANES])
            out += [both[:, :LANES], both[:, LANES:]]
        return out

    def strip_tracers(r, n):
        here, down = pl.ds(r, n), pl.ds(r - 1, n)
        out = pl.ds(r - BASE, n)
        tr_y, (gy_t, gy_s) = north_flux(0, r, n, vel, mn, (t, s), (gt, gs))
        tr_x, ((tc, gx_t), (sc, gx_s)) = east_flux(0, r, n, un[0, here, :], me, (t, s))
        wet = w[0, here, :]
        hy[here, :] = tr_y
        st[out, :] = wet * (tc - (gx_t - west(gx_t) + (gy_t - gt[0, down, :])))
        ss[out, :] = wet * (sc - (gx_s - west(gx_s) + (gy_s - gs[0, down, :])))
        inflow = tr_x - west(tr_x) + (tr_y - hy[down, :])
        for step in (16, 32, 64):
            inflow = inflow + pltpu.roll(inflow, step, 1)
        sh[out, :] = e[here, :] - HEIGHT * inflow

    def tracers(r, n):
        here, down = pl.ds(r, n), pl.ds(r - 1, n)
        out = pl.ds(r - BASE, n)
        edge = on_edge(n)
        wide_t, wide_s = placed(st[out, :]), placed(ss[out, :])
        total_x = total_y = 0.0
        for k in range(LEVELS):
            tr_y, (gy_t, gy_s) = north_flux(k, r, n, mv, mmn, (mt, ms), (mgt, mgs))
            u_next = mu[k, out, :]
            mask = mme[k, here, :]
            tr_x = (FLUX * mask) * (u_next + east(u_next))
            md = (time_step * diffusivity) * mask
            gx_t = tr_x * mface[k, out, :] - md * mslope[k, out, :]
            gx_s = tr_x * mface[LEVELS + k, out, :] - md * mslope[LEVELS + k, out, :]
            tc, sc = mt[k, here, :], ms[k, here, :]
            total_x, total_y = total_x + tr_x, total_y + tr_y
            wet = mw[k, here, :]
            t_next = wet * (tc - (gx_t - west(gx_t) + (gy_t - mgt[k, down, :])))
            s_next = wet * (sc - (gx_s - west(gx_s) + (gy_s - mgs[k, down, :])))
            ot[k, out, :] = jnp.where(edge, wide_t[k], t_next)
            os[k, out, :] = jnp.where(edge, wide_s[k], s_next)
        mhy[here, :] = total_y
        height = mh[here, :] - HEIGHT * (total_x - west(total_x) + (total_y - mhy[down, :]))
        oh[out, :] = jnp.where(edge, placed(sh[out, :], 2)[0], height)

    copies = []

    def send(x, y):
        copies.append(pltpu.make_async_copy(x, y, sems.at[len(copies)]))
        copies[-1].start()

    complete()
    strip_pressure(BASE, rows + 8)
    for x in (t, s, u, v, w, p):
        x[0, pl.ds(BASE - 8, 8), :] = x[0, pl.ds(BASE + rows, 8), :]
    e[pl.ds(BASE - 8, 8), :] = e[pl.ds(BASE + rows, 8), :]
    strip_velocities(BASE - 8, rows + 16)
    south = pl.ds(BASE - 8, 8)
    hy[south, :] = north_flux(0, BASE - 8, 8, vel, mn, (t, s), (gt, gs))[0]
    total = 0.0
    for k in range(LEVELS):
        total = total + north_flux(k, BASE - 8, 8, mv, mmn, (mt, ms), (mgt, mgs))[0]
    mhy[south, :] = total
    whole = pl.ds(BASE, rows)
    edge = on_edge(rows)
    wide_u, wide_v = placed(un[0, whole, :]), placed(vel[0, whole, :])
    for k in range(LEVELS):
        ou[k] = jnp.where(edge, wide_u[k], mu[k])
        ov[k] = jnp.where(edge, wide_v[k], mv[k, whole, :])
    send(ou, u_hbm)
    send(ov, v_hbm)
    strip_tracers(BASE, rows)
    block = rows // LAST_CHUNKS
    for c in range(LAST_CHUNKS):
        tracers(BASE + c * block, block)
        at = pl.ds(c * block, block)
        send(ot.at[:, at, :], t_hbm.at[:, at, :])
        send(os.at[:, at, :], s_hbm.at[:, at, :])
    send(oh, h_hbm)
    for x in copies:
        x.wait()


def last(c, m0, m1, t, s, w, e, un, vel, me, mn, face, slope, place):
    rows, tall = un.shape[1], t.shape[1]
    big = pltpu.VMEM((1, tall, LANES), F32)
    flat = pltpu.VMEM((tall, LANES), F32)
    high = pltpu.VMEM((LEVELS, tall, LANES), F32)
    short = pltpu.VMEM((rows, LANES), F32)
    out3 = jax.ShapeDtypeStruct((LEVELS, rows, LANES), F32)
    wide = pltpu.VMEM((LEVELS, rows, LANES), F32)
    return pl.pallas_call(
        last_kernel,
        in_specs=[VMEM] * 14,
        out_specs=[HBM] * 5,
        out_shape=[out3] * 4 + [jax.ShapeDtypeStruct((rows, LANES), F32)],
        scratch_shapes=[big] * 5
        + [flat]
        + [big] * 7
        + [flat]
        + [high, high, flat]
        + [short] * 3
        + [wide] * 4
        + [short, pltpu.SemaphoreType.DMA((3 + 2 * LAST_CHUNKS,))],
        compiler_params=params(24),
        name="last",
    )(c, m0, m1, t, s, w, e, un, vel, me, mn, face, slope, place)


def swaps():
    lon, lat = lax.axis_size("lon"), lax.axis_size("lat")

    def device(o, a):
        return o % lon * lat + a

    lat_first, lat_second, lon_first, lon_second = [], [], [], []
    for o in range(lon):
        for a in range(lat):
            lat_first.append((device(o, a), device(o, a ^ 1)))
            if a == lat - 1:
                lat_second.append((device(o, a), device(lon - 1 - o, a)))
            elif a > 0:
                lat_second.append((device(o, a), device(o, a + 1 if a % 2 else a - 1)))
            else:
                lat_second.append((device(o, a), device(o ^ 1, a)))
            lon_first.append((device(o, a), device(o ^ 1, a)))
            lon_second.append((device(o, a), device(o + 1 if o % 2 else o - 1, a)))
    return lat_first, lat_second, lon_first, lon_second


def on_device(
    heat_anomaly,
    saltiness_anomaly,
    zonal_current,
    meridional_current,
    free_elevation,
    ocean_indicator,
    floor_layer_index,
):
    lat_first, lat_second, lon_first, lon_second = swaps()
    send = functools.partial(lax.ppermute, axis_name=("lon", "lat"))
    fields = (heat_anomaly, saltiness_anomaly, zonal_current, meridional_current, ocean_indicator)
    a, b = row_pack(fields, free_elevation)
    a = send(a, perm=lat_first)
    b = send(b, perm=lat_second)
    *arrays, face, slope, place = column_pack(fields, free_elevation)
    t, s, u, v, w, e, p, c, m0, m1 = ghosts(a, b, arrays)
    m0 = send(m0, perm=lon_first)
    m1 = send(m1, perm=lon_second)
    un, vel, me, mn = new_velocities(u, v, w, p, free_elevation.shape[0])
    return tuple(last(c, m0, m1, t, s, w, e, un, vel, me, mn, face, slope, place))


def solution(mesh):
    return jax.shard_map(
        on_device,
        mesh=mesh,
        in_specs=(
            P(None, "lat", "lon"),
            P(None, "lat", "lon"),
            P(None, "lat", "lon"),
            P(None, "lat", "lon"),
            P("lat", "lon"),
            P(None, "lat", "lon"),
            P("lat", "lon"),
        ),
        out_specs=(
            P(None, "lat", "lon"),
            P(None, "lat", "lon"),
            P(None, "lat", "lon"),
            P(None, "lat", "lon"),
            P("lat", "lon"),
        ),
        check_vma=False,
    )
```

```python
import functools

import jax
import jax.numpy as jnp
from jax import lax
from jax.experimental import pallas as pl
from jax.experimental.pallas import tpu as pltpu
from jax.sharding import PartitionSpec as P

F32 = jnp.float32
BF16 = jnp.bfloat16
LEVELS = 8
LANES = 128
FIELDS = 5
PLANES = FIELDS * LEVELS + 1
ROW_MSG = 2 * FIELDS * LEVELS + 8
BASE = 16
PACK_ROWS = 96
REST_ROWS = 32
REST_LANES = 2 * LEVELS + 2
MAIN_BLOCKS = 1

time_step = 0.2
viscosity = 0.5
diffusivity = 0.3
press_scale = 0.25
gravity = 1.0
drag_coef = 1.0
coriolis_max = 0.5

HBM = pl.BlockSpec(memory_space=pltpu.HBM)
VMEM = pl.BlockSpec(memory_space=pltpu.VMEM)


def params(mib):
    return pltpu.CompilerParams(vmem_limit_bytes=int(mib * 1024 * 1024))


def lanes(rows=8):
    return lax.broadcasted_iota(jnp.int32, (rows, LANES), 1)


def east(x):
    return pltpu.roll(x, LANES - 1, 1)


def west(x):
    return pltpu.roll(x, 1, 1)


def gather(x, index):
    return jnp.take_along_axis(x, index, axis=1)


def strip_layout(rows):
    lane = lanes(rows)
    return lane, lane // 16, lane % 16


def own_strips(packed, rows):
    _, level, slot = strip_layout(rows)
    own = jnp.where(slot < 4, slot, jnp.where((slot >= 8) & (slot < 12), slot - 4, 0))
    out = [gather(packed[f // 2], 8 * level + own + 64 * (f % 2)) for f in range(FIELDS)]
    return out + [gather(packed[2], own + 64)]


def split(x):
    high = x.astype(BF16)
    rest = x - high.astype(F32)
    middle = rest.astype(BF16)
    return high, middle, (rest - middle.astype(F32)).astype(BF16)


def face_matrix():
    step = lane_step()
    face = jnp.where(step < 2, 7.0, jnp.where((step == 2) | (step == LANES - 1), -1.0, 0.0))
    slope = jnp.where(step == 1, 1.0, jnp.where(step == 0, -1.0, 0.0))
    return jnp.concatenate([face, slope], axis=1).astype(BF16)


def product(x, matrix):
    return sum(jnp.dot(part, matrix, preferred_element_type=F32) for part in split(x)[::-1])


def lane_step():
    row = lax.broadcasted_iota(jnp.int32, (LANES, LANES), 0)
    return lax.rem(row - lax.broadcasted_iota(jnp.int32, (LANES, LANES), 1) + LANES, LANES)


def neighbour_matrix():
    step = lane_step()
    return jnp.concatenate([jnp.where(step == 1, 1.0, 0.0), jnp.where(step == LANES - 1, 1.0, 0.0)], axis=1).astype(BF16)


def difference_matrix():
    step = lane_step()
    return jnp.where(step == 1, 1.0, jnp.where(step == LANES - 1, -1.0, 0.0)).astype(BF16)


def place_matrix(level):
    lane, row = (lax.broadcasted_iota(jnp.int32, (LANES, LANES), n) for n in (1, 0))
    slot = jnp.where(lane < 2, lane + 8, jnp.where(lane >= LANES - 2, lane - (LANES - 4), -LANES))
    return jnp.where(row == 16 * level + slot, 1.0, 0.0).astype(BF16)


def is_even(axis):
    return lax.rem(lax.axis_index(axis), 2) == 0


def row_pack_kernel(*refs):
    ins, (a_ref, b_ref), tiles, sems = refs[:6], refs[6:8], refs[8:20], refs[20]
    rows = ins[5].shape[0]
    copies = []
    for n, x in enumerate(ins):
        for side, start in enumerate((0, rows - 8)):
            src = x.at[:, pl.ds(start, 8), :] if n < FIELDS else x.at[pl.ds(start, 8), :]
            copies.append(pltpu.make_async_copy(src, tiles[2 * n + side], sems.at[2 * n + side]))
            copies[-1].start()
    for x in copies:
        x.wait()
    even = is_even("lat")
    for r in range(2):
        for f in range(FIELDS):
            low, high = tiles[2 * f : 2 * f + 2]
            bottom = low.reshape(LEVELS * 8, LANES)[pl.ds(r, LEVELS, stride=8), :].astype(F32)
            top = high.reshape(LEVELS * 8, LANES)[pl.ds(6 + r, LEVELS, stride=8), :].astype(F32)
            place = pl.ds((r * FIELDS + f) * LEVELS, LEVELS)
            a_ref[place, :] = jnp.where(even, top, bottom)
            b_ref[place, :] = jnp.where(even, bottom, top)
    place = pl.ds(2 * FIELDS * LEVELS, 8)
    low, high = tiles[10][...], tiles[11][...]
    a_ref[place, :] = jnp.where(even, high, low)
    b_ref[place, :] = jnp.where(even, low, high)


def row_pack(fields, surface):
    scratch = [pltpu.VMEM((LEVELS, 8, LANES), x.dtype) for x in fields for _ in range(2)]
    scratch += [pltpu.VMEM((8, LANES), F32)] * 2 + [pltpu.SemaphoreType.DMA((12,))]
    return pl.pallas_call(
        row_pack_kernel,
        in_specs=[HBM] * 6,
        out_specs=[VMEM] * 2,
        out_shape=[pltpu.VMEM((ROW_MSG, LANES), F32)] * 2,
        scratch_shapes=scratch,
        compiler_params=params(60),
        name="row_pack",
    )(*fields, surface)


def pack_columns(plane, rows):
    lane = lanes(rows)
    packed = []
    for first in range(0, PLANES, 16):
        group = None
        for p in range(first, min(first + 16, PLANES)):
            q = p - first
            moved = pltpu.roll(plane(p), (8 * q + 4) % LANES, 1)
            group = moved if group is None else jnp.where(lane >= 8 * q, moved, group)
        packed.append(group)
    return packed


def column_messages(packed, even, rows):
    lane = lanes(rows)
    base = 8 * ((lane // 2) % 16) + lane % 2
    messages = []
    for first in (True, False):
        eastern = even if first else jnp.logical_not(even)
        index = base + jnp.where(eastern, 2, 4)
        c0, c1, c2 = [gather(c, index) for c in packed]
        messages.append(jnp.where(lane < 32, c0, jnp.where(lane < 64, c1, c2)))
    return messages


def message_rows(rows):
    half = (rows + 8 + 15) // 16 * 8
    return half, half + REST_ROWS


def compact(message, rows):
    half, _ = message_rows(rows)
    lane = lanes(half)
    second = jnp.concatenate([message[half:rows, :], jnp.zeros((2 * half - rows, LANES), F32)], axis=0)
    main = jnp.where(lane < 64, message[:half, :], pltpu.roll(second, 64, 1))
    lane = lanes(REST_ROWS)
    rest = jnp.zeros((REST_ROWS, LANES), F32)
    for g in range(rows // REST_ROWS):
        part = pltpu.roll(message[g * REST_ROWS : (g + 1) * REST_ROWS, :], (REST_LANES * g - 64) % LANES, 1)
        rest = jnp.where((lane >= REST_LANES * g) & (lane < REST_LANES * (g + 1)), part, rest)
    return main, rest


def column_pack_kernel(t_in, s_in, u_in, v_in, w_in, e_in, t, s, u, v, w, e, p, c_ref, m0_ref, m1_ref, face, slope, place, m0_wide, m1_wide):
    rows = e_in.shape[0]
    even = is_even("lon")
    matrix = face_matrix()
    for k in range(LEVELS):
        place[:, k * LANES : (k + 1) * LANES] = place_matrix(k)

    def step(i, _):
        out = pl.ds(pl.multiple_of(i * PACK_ROWS, 8), PACK_ROWS)
        here = pl.ds(pl.multiple_of(BASE + i * PACK_ROWS, 8), PACK_ROWS)
        for x, y in ((t_in, t), (s_in, s), (u_in, u), (v_in, v), (w_in, w)):
            for k in range(LEVELS):
                y[k, here, :] = x[k, out, :].astype(F32)
        e[here, :] = e_in[out, :]

        def plane(q):
            if q == PLANES - 1:
                return e_in[out, :]
            return (t_in, s_in, u_in, v_in, w_in)[q // LEVELS][q % LEVELS, out, :].astype(F32)

        packed = pack_columns(plane, PACK_ROWS)
        for n, x in enumerate(own_strips(packed, PACK_ROWS)):
            c_ref[n, out, :] = x
        m0_wide[out, :], m1_wide[out, :] = column_messages(packed, even, PACK_ROWS)
        total = (gravity * 0.5 * time_step) * e_in[out, :]
        for k in range(LEVELS):
            h = density_half(t_in[k, out, :], s_in[k, out, :])
            at = total + h
            p[k, here, :] = at
            total = at + h
        for n, x in enumerate((t_in, s_in)):
            for k in range(LEVELS):
                both = product(x[k, out, :], matrix)
                face[n * LEVELS + k, out, :] = both[:, :LANES]
                slope[n * LEVELS + k, out, :] = both[:, LANES:]
        return 0

    lax.fori_loop(0, rows // PACK_ROWS, step, 0)
    half, _ = message_rows(rows)
    for wide, out in ((m0_wide, m0_ref), (m1_wide, m1_ref)):
        main, rest = compact(wide[...], rows)
        out[:half, :] = main
        out[half:, :] = rest


def column_pack(fields, surface):
    rows = surface.shape[0]
    tall = rows + BASE + 16
    big = pltpu.VMEM((LEVELS, tall, LANES), F32)
    return pl.pallas_call(
        column_pack_kernel,
        in_specs=[VMEM] * 6,
        out_specs=[VMEM] * 13,
        out_shape=[big] * 5
        + [pltpu.VMEM((tall, LANES), F32), big]
        + [pltpu.VMEM((FIELDS + 1, rows + 8, LANES), F32)]
        + [pltpu.VMEM((message_rows(rows)[1], LANES), F32)] * 2
        + [pltpu.VMEM((2 * LEVELS, rows, LANES), F32)] * 2
        + [pltpu.VMEM((LANES, LEVELS * LANES), BF16)],
        scratch_shapes=[pltpu.VMEM((rows, LANES), F32)] * 2,
        compiler_params=params(16),
        cost_estimate=pl.CostEstimate(flops=10_000_000, bytes_accessed=6_000_000, transcendentals=0),
        name="column_pack",
    )(*fields, surface)


def ghost_kernel(a_ref, b_ref, *refs):
    face, slope = refs[10:12]
    t, s, u, v, w, e, p, c_ref, m0_ref, m1_ref = refs[12:22]
    outs, g_ref, scratch = refs[22:27], refs[27], refs[28:]
    rows = c_ref.shape[1] - 8
    even = is_even("lat")
    fold = lax.axis_index("lat") == lax.axis_size("lat") - 1
    mirror = LANES - 1 - lanes()
    flat = g_ref.reshape(PLANES * 8, LANES)
    g_ref[...] = jnp.zeros_like(g_ref)

    southmost = lax.axis_index("lat") == 0

    def both(start):
        a, b = a_ref[pl.ds(start, 8), :], b_ref[pl.ds(start, 8), :]
        return jnp.where(even, a, b), jnp.where(southmost, 0.0, jnp.where(even, b, a))

    for f in range(FIELDS):
        sign = -1.0 if f in (2, 3) else 1.0
        north0, south0 = both(f * LEVELS)
        north1, south1 = both((FIELDS + f) * LEVELS)
        first = jnp.where(fold, sign * gather(north1, mirror), north0)
        second = jnp.where(fold, sign * gather(north0, mirror), north1)
        for row, value in ((0, first), (1, second), (6, south0), (7, south1)):
            flat[pl.ds(f * LEVELS * 8 + row, LEVELS, stride=8), :] = value
    north, south = both(2 * FIELDS * LEVELS)
    turned = gather(north, mirror)
    row = lax.broadcasted_iota(jnp.int32, (8, LANES), 0)
    folded = jnp.where(row == 0, pltpu.roll(turned, 1, 0), pltpu.roll(turned, 3, 0))
    g_ref[PLANES - 1] = jnp.where(row < 2, jnp.where(fold, folded, north), jnp.where(row >= 6, south, 0.0))
    packed = pack_columns(lambda q: g_ref[q], 8)
    last = pl.ds(rows, 8)
    for n, x in enumerate(own_strips(packed, 8)):
        c_ref[n, last, :] = x
    half, _ = message_rows(rows)
    lane = lanes()
    first = REST_LANES * (rows // REST_ROWS)
    for out, message in zip((m0_ref, m1_ref), column_messages(packed, is_even("lon"), 8)):
        place = pl.ds(rows - half, 8)
        out[place, :] = jnp.where(lane < 64, out[place, :], pltpu.roll(message, 64, 1))
        place = pl.ds(half, 8)
        moved = pltpu.roll(message, (first - 64) % LANES, 1)
        out[place, :] = jnp.where((lane >= first) & (lane < first + REST_LANES), moved, out[place, :])
    for side in (pl.ds(BASE - 8, 8), pl.ds(BASE + rows, 8)):
        for f, x in enumerate((t, s, u, v, w)):
            for k in range(LEVELS):
                x[k, side, :] = g_ref[f * LEVELS + k]
        e[side, :] = g_ref[PLANES - 1]
        pressure(side, t, s, e, p)

    @pl.when(waits_for_seam())
    def _():
        interior(t, s, u, v, w, e, p, face, slope, *outs, *scratch)


def ghosts(a, b, arrays, face, slope):
    rows, tall = face.shape[1], arrays[0].shape[1]
    return pl.pallas_call(
        ghost_kernel,
        in_specs=[VMEM] * 14,
        out_specs=[VMEM] * 15,
        out_shape=[pltpu.VMEM(x.shape, F32) for x in arrays] + interior_outputs(rows),
        scratch_shapes=[pltpu.VMEM((PLANES, 8, LANES), F32)] + interior_scratch(tall),
        input_output_aliases={n + 2: n for n in range(10)},
        compiler_params=params(16),
        name="ghosts",
    )(a, b, *arrays, face, slope)


def density_half(t, s):
    k = 0.5 * press_scale * 0.5 * time_step
    return t * (-0.2 * k + (-0.05 * k) * t + (0.02 * k) * s) + (0.8 * k) * s


def pressure(here, t, s, e, p):
    total = (gravity * 0.5 * time_step) * e[here, :]
    for k in range(LEVELS):
        h = density_half(t[k, here, :], s[k, here, :])
        at = total + h
        p[k, here, :] = at
        total = at + h


def coriolis_rows(start, count, rows):
    total = rows * lax.axis_size("lat")
    row = lax.broadcasted_iota(jnp.int32, (count, LANES), 0) + (start - BASE + lax.axis_index("lat") * rows)
    row = jnp.minimum(row, total - 1).astype(F32)
    return (time_step * coriolis_max) * (2.0 * (row + 0.5) / total - 1.0)


def velocity_trial(k, r, n, spin, u, v, w, p, m_east, m_north, matrices=None):
    here, up, down = pl.ds(r, n), pl.ds(r + 1, n), pl.ds(r - 1, n)
    wet = w[k, here, :]
    pc = p[k, here, :]
    if matrices is None:
        wet_east, wet_west, slope = east(wet), west(wet), east(pc) - west(pc)
    else:
        both = jnp.dot(wet.astype(BF16), matrices[0], preferred_element_type=F32)
        wet_east, wet_west, slope = both[:, :LANES], both[:, LANES:], product(pc, matrices[1])
    me = wet * wet_east
    mw = wet * wet_west
    mn = wet * w[k, up, :]
    ms = wet * w[k, down, :]
    m_east[k, here, :] = me
    m_north[k, here, :] = mn

    def lap(q_ref, q):
        return me * (east(q) - q) + mw * (west(q) - q) + (mn * (q_ref[k, up, :] - q) + ms * (q_ref[k, down, :] - q))

    un, vn = u[k, here, :], v[k, here, :]
    u_trial = un + (spin * vn - slope + (time_step * viscosity) * lap(u, un))
    v_trial = vn + ((time_step * viscosity) * lap(v, vn) - spin * un - (p[k, up, :] - p[k, down, :]))
    return wet, u_trial, v_trial


def damping(u, v):
    return 1.0 / (1.0 + drag_coef * jnp.sqrt(u * u + v * v))


FLUX = time_step * 0.5 / 12.0
HEIGHT = time_step / LEVELS * 0.5 / FLUX


def flux(q0, q1, qm, qp, tr, md):
    return tr * (7.0 * (q0 + q1) - (qm + qp)) - md * (q1 - q0)


def north_flux(k, r, n, vel, m_north, tracers, g_refs):
    here, up = pl.ds(r, n), pl.ds(r + 1, n)
    mn = m_north[k, here, :]
    tr = (FLUX * mn) * (vel[k, here, :] + vel[k, up, :])
    md = (time_step * diffusivity) * mn
    out = []
    for q, g in zip(tracers, g_refs):
        gy = flux(q[k, here, :], q[k, up, :], q[k, pl.ds(r - 1, n), :], q[k, pl.ds(r + 2, n), :], tr, md)
        g[k, here, :] = gy
        out.append(gy)
    return tr, out


def east_flux(k, r, n, u_next, m_east, tracers):
    here = pl.ds(r, n)
    me = m_east[k, here, :]
    tr = (FLUX * me) * (u_next + east(u_next))
    md = (time_step * diffusivity) * me
    out = []
    for q_ref in tracers:
        q = q_ref[k, here, :]
        out.append((q, flux(q, east(q), west(q), pltpu.roll(q, LANES - 2, 1), tr, md)))
    return tr, out


def interior(t, s, u, v, w, e, p, face, slope, t_out, s_out, u_out, v_out, h_out, me, mn, vel, gt, gs, hy):
    rows = h_out.shape[0]
    matrices = neighbour_matrix(), difference_matrix()

    def velocities(r, n, store):
        here = pl.ds(r, n)
        spin = coriolis_rows(r, n, rows)
        on_unit = matrices if n % 16 == 0 else None
        trial = [velocity_trial(k, r, n, spin, u, v, w, p, me, mn, on_unit) for k in range(LEVELS)]
        at_floor = [trial[k][0] > (trial[k + 1][0] if k + 1 < LEVELS else 0.0) for k in range(LEVELS)]
        u_floor, v_floor = trial[0][1], trial[0][2]
        for k in range(1, LEVELS):
            u_floor = jnp.where(at_floor[k], trial[k][1], u_floor)
            v_floor = jnp.where(at_floor[k], trial[k][2], v_floor)
        damp = damping(u_floor, v_floor)
        for k in range(LEVELS):
            factor = jnp.where(at_floor[k], damp, trial[k][0])
            v_next = factor * trial[k][2]
            vel[k, here, :] = v_next
            if store:
                out = pl.ds(r - BASE, n)
                u_out[k, out, :] = factor * trial[k][1]
                v_out[k, out, :] = v_next

    def tracers(r, n):
        here, down = pl.ds(r, n), pl.ds(r - 1, n)
        out = pl.ds(r - BASE, n)
        total_x = total_y = 0.0
        for k in range(LEVELS):
            tr_y, (gy_t, gy_s) = north_flux(k, r, n, vel, mn, (t, s), (gt, gs))
            u_next = u_out[k, out, :]
            mask = me[k, here, :]
            tr_x = (FLUX * mask) * (u_next + east(u_next))
            md = (time_step * diffusivity) * mask
            gx_t = tr_x * face[k, out, :] - md * slope[k, out, :]
            gx_s = tr_x * face[LEVELS + k, out, :] - md * slope[LEVELS + k, out, :]
            total_x, total_y = total_x + tr_x, total_y + tr_y
            wet = w[k, here, :]
            t_out[k, out, :] = wet * (t[k, here, :] - (gx_t - west(gx_t) + (gy_t - gt[k, down, :])))
            s_out[k, out, :] = wet * (s[k, here, :] - (gx_s - west(gx_s) + (gy_s - gs[k, down, :])))
        hy[here, :] = total_y
        h_out[out, :] = e[here, :] - HEIGHT * (total_x - west(total_x) + (total_y - hy[down, :]))

    velocities(BASE - 8, 8, False)
    velocities(BASE + rows, 8, False)
    velocities(BASE, rows, True)
    total = 0.0
    for k in range(LEVELS):
        total = total + north_flux(k, BASE - 8, 8, vel, mn, (t, s), (gt, gs))[0]
    hy[pl.ds(BASE - 8, 8), :] = total
    block = rows // MAIN_BLOCKS
    for n in range(MAIN_BLOCKS):
        tracers(BASE + n * block, block)


def interior_outputs(rows):
    return [pltpu.VMEM((LEVELS, rows, LANES), F32)] * 4 + [pltpu.VMEM((rows, LANES), F32)]


def interior_scratch(tall):
    return [pltpu.VMEM((LEVELS, tall, LANES), F32)] * 5 + [pltpu.VMEM((tall, LANES), F32)]


def waits_for_seam():
    return lax.axis_index("lon") == 0


def main_kernel(*refs):
    ins, outs, scratch = refs[:9], refs[14:19], refs[19:]

    @pl.when(jnp.logical_not(waits_for_seam()))
    def _():
        interior(*ins, *outs, *scratch)


def main(arrays, outs):
    rows, tall = outs[4].shape[0], arrays[0].shape[1]
    return pl.pallas_call(
        main_kernel,
        in_specs=[VMEM] * 14,
        out_specs=[VMEM] * 5,
        out_shape=interior_outputs(rows),
        scratch_shapes=interior_scratch(tall),
        input_output_aliases={n + 9: n for n in range(5)},
        compiler_params=params(16),
        cost_estimate=pl.CostEstimate(flops=40_000_000, bytes_accessed=8_000_000, transcendentals=100_000),
        name="main",
    )(*arrays, *outs)


def last_kernel(c_ref, m0_ref, m1_ref, place, mt, ms, mu, mv, mh, t_hbm, s_hbm, u_hbm, v_hbm, h_hbm,
                t, s, u, v, w, e, p, me, mn, un, vel, gt, gs, hy, st, ss, sh, ot, os, ou, ov, oh, sems):
    rows = oh.shape[0]
    even = is_even("lon")

    def complete():
        n = rows + 8
        half, _ = message_rows(rows)
        m0, m1 = m0_ref[...], m1_ref[...]
        m_east, m_west = jnp.where(even, m0, m1), jnp.where(even, m1, m0)
        low = jnp.where(lanes(half) < 64, m_east[:half, :], pltpu.roll(m_west[:half, :], 64, 1))
        high = jnp.where(lanes(n - half) < 64, pltpu.roll(m_east[: n - half, :], 64, 1), m_west[: n - half, :])
        four = jnp.concatenate([low, high], axis=0)
        rest_east, rest_west = m_east[half:, :], pltpu.roll(m_west[half:, :], 64, 1)

        def slots(count):
            _, level, slot = strip_layout(count)
            west_side = jnp.where(slot >= 6, 64, 0)
            return level, (slot >= 4) & (slot < 8), west_side + jnp.where(slot % 2 == 1, 1, 0)

        level, ghost, at = slots(n)
        here = pl.ds(BASE, n)
        for f, x in enumerate((t, s, u, v)):
            x[0, here, :] = jnp.where(ghost, gather(four, 2 * LEVELS * f + 2 * level + at), c_ref[f])
        for g in range(-(-n // REST_ROWS)):
            count = min(REST_ROWS, n - g * REST_ROWS)
            level, ghost, at = slots(count)
            lane = lanes(count)
            mine = (lane >= REST_LANES * g) & (lane < REST_LANES * (g + 1))
            rest = jnp.where(mine, rest_east[:count, :], rest_west[:count, :])
            src, dst = pl.ds(g * REST_ROWS, count), pl.ds(BASE + g * REST_ROWS, count)
            index = (REST_LANES * g + 2 * level + at) % LANES
            w[0, dst, :] = jnp.where(ghost, gather(rest, index), c_ref[FIELDS - 1, src, :])
            index = (REST_LANES * g + 2 * LEVELS + at) % LANES
            e[dst, :] = jnp.where(ghost, gather(rest, index), c_ref[FIELDS, src, :])

    def strip_pressure(r, n):
        here = pl.ds(r, n)
        lane = lanes(n)
        h = density_half(t[0, here, :], s[0, here, :])
        total = h
        for step in (16, 32, 64):
            total = total + jnp.where(lane >= step, pltpu.roll(total, step, 1), 0.0)
        p[0, here, :] = (gravity * 0.5 * time_step) * e[here, :] + (2.0 * total - h)

    def strip_velocities(r, n):
        here = pl.ds(r, n)
        lane = lanes(n)
        wet, u_trial, v_trial = velocity_trial(0, r, n, coriolis_rows(r, n, rows), u, v, w, p, me, mn)
        below = jnp.where(lane < LANES - 16, pltpu.roll(wet, LANES - 16, 1), 0.0)
        factor = jnp.where(wet > below, damping(u_trial, v_trial), wet)
        un[0, here, :] = factor * u_trial
        vel[0, here, :] = factor * v_trial

    def on_edge(n):
        lane = lanes(n)
        return (lane < 2) | (lane >= LANES - 2)

    def placed(strip, levels=LEVELS):
        out = []
        for k in range(0, levels, 2):
            both = product(strip, place[:, k * LANES : (k + 2) * LANES])
            out += [both[:, :LANES], both[:, LANES:]]
        return out

    def strip_tracers(r, n):
        here, down = pl.ds(r, n), pl.ds(r - 1, n)
        out = pl.ds(r - BASE, n)
        tr_y, (gy_t, gy_s) = north_flux(0, r, n, vel, mn, (t, s), (gt, gs))
        tr_x, ((tc, gx_t), (sc, gx_s)) = east_flux(0, r, n, un[0, here, :], me, (t, s))
        wet = w[0, here, :]
        hy[here, :] = tr_y
        st[out, :] = wet * (tc - (gx_t - west(gx_t) + (gy_t - gt[0, down, :])))
        ss[out, :] = wet * (sc - (gx_s - west(gx_s) + (gy_s - gs[0, down, :])))
        inflow = tr_x - west(tr_x) + (tr_y - hy[down, :])
        for step in (16, 32, 64):
            inflow = inflow + pltpu.roll(inflow, step, 1)
        sh[out, :] = e[here, :] - HEIGHT * inflow

    copies = []

    def send(x, y):
        copies.append(pltpu.make_async_copy(x, y, sems.at[len(copies)]))
        copies[-1].start()

    complete()
    strip_pressure(BASE, rows + 8)
    for x in (t, s, u, v, w, p):
        x[0, pl.ds(BASE - 8, 8), :] = x[0, pl.ds(BASE + rows, 8), :]
    e[pl.ds(BASE - 8, 8), :] = e[pl.ds(BASE + rows, 8), :]
    strip_velocities(BASE - 8, rows + 16)
    hy[pl.ds(BASE - 8, 8), :] = north_flux(0, BASE - 8, 8, vel, mn, (t, s), (gt, gs))[0]
    whole = pl.ds(BASE, rows)

    def merge(out, strip, inner):
        edge = on_edge(strip.shape[0])
        for k, value in enumerate(placed(strip)):
            out[k] = jnp.where(edge, value, inner[k])

    merge(ou, un[0, whole, :], mu)
    merge(ov, vel[0, whole, :], mv)
    send(ou, u_hbm)
    send(ov, v_hbm)
    strip_tracers(BASE, rows)
    merge(ot, st[...], mt)
    send(ot, t_hbm)
    oh[...] = jnp.where(on_edge(rows), placed(sh[...], 2)[0], mh[...])
    send(oh, h_hbm)
    merge(os, ss[...], ms)
    send(os, s_hbm)
    for x in copies:
        x.wait()


def last(c, m0, m1, place, outs):
    rows = outs[4].shape[0]
    tall = rows + BASE + 16
    big = pltpu.VMEM((1, tall, LANES), F32)
    flat = pltpu.VMEM((tall, LANES), F32)
    short = pltpu.VMEM((rows, LANES), F32)
    out3 = jax.ShapeDtypeStruct((LEVELS, rows, LANES), F32)
    wide = pltpu.VMEM((LEVELS, rows, LANES), F32)
    return pl.pallas_call(
        last_kernel,
        in_specs=[VMEM] * 9,
        out_specs=[HBM] * 5,
        out_shape=[out3] * 4 + [jax.ShapeDtypeStruct((rows, LANES), F32)],
        scratch_shapes=[big] * 5
        + [flat]
        + [big] * 7
        + [flat]
        + [short] * 3
        + [wide] * 4
        + [short, pltpu.SemaphoreType.DMA((5,))],
        compiler_params=params(24),
        name="last",
    )(c, m0, m1, place, *outs)


def swaps():
    lon, lat = lax.axis_size("lon"), lax.axis_size("lat")

    def device(o, a):
        return o % lon * lat + a

    lat_first, lat_second, lon_first, lon_second = [], [], [], []
    for o in range(lon):
        for a in range(lat):
            lat_first.append((device(o, a), device(o, a ^ 1)))
            if a == lat - 1:
                lat_second.append((device(o, a), device(lon - 1 - o, a)))
            elif a > 0:
                lat_second.append((device(o, a), device(o, a + 1 if a % 2 else a - 1)))
            else:
                lat_second.append((device(o, a), device(o ^ 1, a)))
            lon_first.append((device(o, a), device(o ^ 1, a)))
            lon_second.append((device(o, a), device(o + 1 if o % 2 else o - 1, a)))
    return lat_first, lat_second, lon_first, lon_second


def on_device(
    heat_anomaly,
    saltiness_anomaly,
    zonal_current,
    meridional_current,
    free_elevation,
    ocean_indicator,
    floor_layer_index,
):
    lat_first, lat_second, lon_first, lon_second = swaps()
    send = functools.partial(lax.ppermute, axis_name=("lon", "lat"))
    fields = (heat_anomaly, saltiness_anomaly, zonal_current, meridional_current, ocean_indicator)
    a, b = row_pack(fields, free_elevation)
    a = send(a, perm=lat_first)
    b = send(b, perm=lat_second)
    *arrays, face, slope, place = column_pack(fields, free_elevation)
    *arrays, c, m0, m1, t, s, u, v, h = ghosts(a, b, arrays, face, slope)
    m0 = send(m0, perm=lon_first)
    m1 = send(m1, perm=lon_second)
    outs = main((*arrays, face, slope), (t, s, u, v, h))
    return tuple(last(c, m0, m1, place, outs))


def solution(mesh):
    return jax.shard_map(
        on_device,
        mesh=mesh,
        in_specs=(
            P(None, "lat", "lon"),
            P(None, "lat", "lon"),
            P(None, "lat", "lon"),
            P(None, "lat", "lon"),
            P("lat", "lon"),
            P(None, "lat", "lon"),
            P("lat", "lon"),
        ),
        out_specs=(
            P(None, "lat", "lon"),
            P(None, "lat", "lon"),
            P(None, "lat", "lon"),
            P(None, "lat", "lon"),
            P("lat", "lon"),
        ),
        check_vma=False,
    )
```

```python
import functools

import jax
import jax.numpy as jnp
from jax import lax
from jax.experimental import pallas as pl
from jax.experimental.pallas import tpu as pltpu
from jax.sharding import PartitionSpec as P

F32 = jnp.float32
BF16 = jnp.bfloat16
LEVELS = 8
LANES = 128
FIELDS = 5
PLANES = FIELDS * LEVELS + 1
ROW_MSG = 2 * FIELDS * LEVELS + 8
BASE = 16
PACK_ROWS = 96
REST_ROWS = 32
REST_LANES = 2 * LEVELS + 2
MAIN_BLOCKS = 1

time_step = 0.2
viscosity = 0.5
diffusivity = 0.3
press_scale = 0.25
gravity = 1.0
drag_coef = 1.0
coriolis_max = 0.5

HBM = pl.BlockSpec(memory_space=pltpu.HBM)
VMEM = pl.BlockSpec(memory_space=pltpu.VMEM)


def params(mib):
    return pltpu.CompilerParams(vmem_limit_bytes=int(mib * 1024 * 1024))


def lanes(rows=8):
    return lax.broadcasted_iota(jnp.int32, (rows, LANES), 1)


def east(x):
    return pltpu.roll(x, LANES - 1, 1)


def west(x):
    return pltpu.roll(x, 1, 1)


def gather(x, index):
    return jnp.take_along_axis(x, index, axis=1)


def strip_layout(rows):
    lane = lanes(rows)
    return lane, lane // 16, lane % 16


def own_strips(packed, rows):
    _, level, slot = strip_layout(rows)
    own = jnp.where(slot < 4, slot, jnp.where((slot >= 8) & (slot < 12), slot - 4, 0))
    out = [gather(packed[f // 2], 8 * level + own + 64 * (f % 2)) for f in range(FIELDS)]
    return out + [gather(packed[2], own + 64)]


def split(x):
    high = x.astype(BF16)
    rest = x - high.astype(F32)
    middle = rest.astype(BF16)
    return high, middle, (rest - middle.astype(F32)).astype(BF16)


def face_matrix():
    step = lane_step()
    face = jnp.where(step < 2, 7.0, jnp.where((step == 2) | (step == LANES - 1), -1.0, 0.0))
    slope = jnp.where(step == 1, 1.0, jnp.where(step == 0, -1.0, 0.0))
    return jnp.concatenate([face, slope], axis=1).astype(BF16)


def product(x, matrix):
    return sum(jnp.dot(part, matrix, preferred_element_type=F32) for part in split(x)[::-1])


def lane_step():
    row = lax.broadcasted_iota(jnp.int32, (LANES, LANES), 0)
    return lax.rem(row - lax.broadcasted_iota(jnp.int32, (LANES, LANES), 1) + LANES, LANES)


def neighbour_matrix():
    step = lane_step()
    return jnp.concatenate([jnp.where(step == 1, 1.0, 0.0), jnp.where(step == LANES - 1, 1.0, 0.0)], axis=1).astype(BF16)


def difference_matrix():
    step = lane_step()
    return jnp.where(step == 1, 1.0, jnp.where(step == LANES - 1, -1.0, 0.0)).astype(BF16)


def place_matrix(level):
    lane, row = (lax.broadcasted_iota(jnp.int32, (LANES, LANES), n) for n in (1, 0))
    slot = jnp.where(lane < 2, lane + 8, jnp.where(lane >= LANES - 2, lane - (LANES - 4), -LANES))
    return jnp.where(row == 16 * level + slot, 1.0, 0.0).astype(BF16)


def is_even(axis):
    return lax.rem(lax.axis_index(axis), 2) == 0


def row_pack_kernel(*refs):
    ins, (a_ref, b_ref), tiles, sems = refs[:6], refs[6:8], refs[8:20], refs[20]
    rows = ins[5].shape[0]
    copies = []
    for n, x in enumerate(ins):
        for side, start in enumerate((0, rows - 8)):
            src = x.at[:, pl.ds(start, 8), :] if n < FIELDS else x.at[pl.ds(start, 8), :]
            copies.append(pltpu.make_async_copy(src, tiles[2 * n + side], sems.at[2 * n + side]))
            copies[-1].start()
    for x in copies:
        x.wait()
    even = is_even("lat")
    for r in range(2):
        for f in range(FIELDS):
            low, high = tiles[2 * f : 2 * f + 2]
            bottom = low.reshape(LEVELS * 8, LANES)[pl.ds(r, LEVELS, stride=8), :].astype(F32)
            top = high.reshape(LEVELS * 8, LANES)[pl.ds(6 + r, LEVELS, stride=8), :].astype(F32)
            place = pl.ds((r * FIELDS + f) * LEVELS, LEVELS)
            a_ref[place, :] = jnp.where(even, top, bottom)
            b_ref[place, :] = jnp.where(even, bottom, top)
    place = pl.ds(2 * FIELDS * LEVELS, 8)
    low, high = tiles[10][...], tiles[11][...]
    a_ref[place, :] = jnp.where(even, high, low)
    b_ref[place, :] = jnp.where(even, low, high)


def row_pack(fields, surface):
    scratch = [pltpu.VMEM((LEVELS, 8, LANES), x.dtype) for x in fields for _ in range(2)]
    scratch += [pltpu.VMEM((8, LANES), F32)] * 2 + [pltpu.SemaphoreType.DMA((12,))]
    return pl.pallas_call(
        row_pack_kernel,
        in_specs=[HBM] * 6,
        out_specs=[VMEM] * 2,
        out_shape=[pltpu.VMEM((ROW_MSG, LANES), F32)] * 2,
        scratch_shapes=scratch,
        compiler_params=params(60),
        name="row_pack",
    )(*fields, surface)


def pack_columns(plane, rows):
    lane = lanes(rows)
    packed = []
    for first in range(0, PLANES, 16):
        group = None
        for p in range(first, min(first + 16, PLANES)):
            q = p - first
            moved = pltpu.roll(plane(p), (8 * q + 4) % LANES, 1)
            group = moved if group is None else jnp.where(lane >= 8 * q, moved, group)
        packed.append(group)
    return packed


def column_messages(packed, even, rows):
    lane = lanes(rows)
    base = 8 * ((lane // 2) % 16) + lane % 2
    messages = []
    for first in (True, False):
        eastern = even if first else jnp.logical_not(even)
        index = base + jnp.where(eastern, 2, 4)
        c0, c1, c2 = [gather(c, index) for c in packed]
        messages.append(jnp.where(lane < 32, c0, jnp.where(lane < 64, c1, c2)))
    return messages


def message_rows(rows):
    half = (rows + 8 + 15) // 16 * 8
    return half, half + REST_ROWS


def compact(message, rows):
    half, _ = message_rows(rows)
    lane = lanes(half)
    second = jnp.concatenate([message[half:rows, :], jnp.zeros((2 * half - rows, LANES), F32)], axis=0)
    main = jnp.where(lane < 64, message[:half, :], pltpu.roll(second, 64, 1))
    lane = lanes(REST_ROWS)
    rest = jnp.zeros((REST_ROWS, LANES), F32)
    for g in range(rows // REST_ROWS):
        part = pltpu.roll(message[g * REST_ROWS : (g + 1) * REST_ROWS, :], (REST_LANES * g - 64) % LANES, 1)
        rest = jnp.where((lane >= REST_LANES * g) & (lane < REST_LANES * (g + 1)), part, rest)
    return main, rest


def column_pack_kernel(t_in, s_in, u_in, v_in, w_in, e_in, t, s, u, v, w, e, p, c_ref, m0_ref, m1_ref, face, slope, place, m0_wide, m1_wide):
    rows = e_in.shape[0]
    even = is_even("lon")
    matrix = face_matrix()
    for k in range(LEVELS):
        place[:LANES, k * LANES : (k + 1) * LANES] = place_matrix(k)
        place[LANES:, k * LANES : (k + 1) * LANES] = place_matrix(k)

    def step(i, _):
        out = pl.ds(pl.multiple_of(i * PACK_ROWS, 8), PACK_ROWS)
        here = pl.ds(pl.multiple_of(BASE + i * PACK_ROWS, 8), PACK_ROWS)
        for x, y in ((t_in, t), (s_in, s), (u_in, u), (v_in, v), (w_in, w)):
            for k in range(LEVELS):
                y[k, here, :] = x[k, out, :].astype(F32)
        e[here, :] = e_in[out, :]

        def plane(q):
            if q == PLANES - 1:
                return e_in[out, :]
            return (t_in, s_in, u_in, v_in, w_in)[q // LEVELS][q % LEVELS, out, :].astype(F32)

        packed = pack_columns(plane, PACK_ROWS)
        for n, x in enumerate(own_strips(packed, PACK_ROWS)):
            c_ref[n, out, :] = x
        m0_wide[out, :], m1_wide[out, :] = column_messages(packed, even, PACK_ROWS)
        total = (gravity * 0.5 * time_step) * e_in[out, :]
        for k in range(LEVELS):
            h = density_half(t_in[k, out, :], s_in[k, out, :])
            at = total + h
            p[k, here, :] = at
            total = at + h
        for n, x in enumerate((t_in, s_in)):
            for k in range(LEVELS):
                both = product(x[k, out, :], matrix)
                face[n * LEVELS + k, out, :] = both[:, :LANES]
                slope[n * LEVELS + k, out, :] = both[:, LANES:]
        return 0

    lax.fori_loop(0, rows // PACK_ROWS, step, 0)
    half, _ = message_rows(rows)
    for wide, out in ((m0_wide, m0_ref), (m1_wide, m1_ref)):
        main, rest = compact(wide[...], rows)
        out[:half, :] = main
        out[half:, :] = rest


def column_pack(fields, surface):
    rows = surface.shape[0]
    tall = rows + BASE + 16
    big = pltpu.VMEM((LEVELS, tall, LANES), F32)
    return pl.pallas_call(
        column_pack_kernel,
        in_specs=[VMEM] * 6,
        out_specs=[VMEM] * 13,
        out_shape=[big] * 5
        + [pltpu.VMEM((tall, LANES), F32), big]
        + [pltpu.VMEM((FIELDS + 1, rows + 8, LANES), F32)]
        + [pltpu.VMEM((message_rows(rows)[1], LANES), F32)] * 2
        + [pltpu.VMEM((2 * LEVELS, rows, LANES), F32)] * 2
        + [pltpu.VMEM((2 * LANES, LEVELS * LANES), BF16)],
        scratch_shapes=[pltpu.VMEM((rows, LANES), F32)] * 2,
        compiler_params=params(16),
        cost_estimate=pl.CostEstimate(flops=10_000_000, bytes_accessed=6_000_000, transcendentals=0),
        name="column_pack",
    )(*fields, surface)


def ghost_kernel(a_ref, b_ref, *refs):
    t, s, u, v, w, e, p, c_ref, m0_ref, m1_ref, g_ref = refs[10:]
    rows = c_ref.shape[1] - 8
    even = is_even("lat")
    fold = lax.axis_index("lat") == lax.axis_size("lat") - 1
    mirror = LANES - 1 - lanes()
    flat = g_ref.reshape(PLANES * 8, LANES)
    g_ref[...] = jnp.zeros_like(g_ref)

    southmost = lax.axis_index("lat") == 0

    def both(start):
        a, b = a_ref[pl.ds(start, 8), :], b_ref[pl.ds(start, 8), :]
        return jnp.where(even, a, b), jnp.where(southmost, 0.0, jnp.where(even, b, a))

    for f in range(FIELDS):
        sign = -1.0 if f in (2, 3) else 1.0
        north0, south0 = both(f * LEVELS)
        north1, south1 = both((FIELDS + f) * LEVELS)
        first = jnp.where(fold, sign * gather(north1, mirror), north0)
        second = jnp.where(fold, sign * gather(north0, mirror), north1)
        for row, value in ((0, first), (1, second), (6, south0), (7, south1)):
            flat[pl.ds(f * LEVELS * 8 + row, LEVELS, stride=8), :] = value
    north, south = both(2 * FIELDS * LEVELS)
    turned = gather(north, mirror)
    row = lax.broadcasted_iota(jnp.int32, (8, LANES), 0)
    folded = jnp.where(row == 0, pltpu.roll(turned, 1, 0), pltpu.roll(turned, 3, 0))
    g_ref[PLANES - 1] = jnp.where(row < 2, jnp.where(fold, folded, north), jnp.where(row >= 6, south, 0.0))
    packed = pack_columns(lambda q: g_ref[q], 8)
    last = pl.ds(rows, 8)
    for n, x in enumerate(own_strips(packed, 8)):
        c_ref[n, last, :] = x
    half, _ = message_rows(rows)
    lane = lanes()
    first = REST_LANES * (rows // REST_ROWS)
    for out, message in zip((m0_ref, m1_ref), column_messages(packed, is_even("lon"), 8)):
        place = pl.ds(rows - half, 8)
        out[place, :] = jnp.where(lane < 64, out[place, :], pltpu.roll(message, 64, 1))
        place = pl.ds(half, 8)
        moved = pltpu.roll(message, (first - 64) % LANES, 1)
        out[place, :] = jnp.where((lane >= first) & (lane < first + REST_LANES), moved, out[place, :])
    for side in (pl.ds(BASE - 8, 8), pl.ds(BASE + rows, 8)):
        for f, x in enumerate((t, s, u, v, w)):
            for k in range(LEVELS):
                x[k, side, :] = g_ref[f * LEVELS + k]
        e[side, :] = g_ref[PLANES - 1]
        pressure(side, t, s, e, p)


def ghosts(a, b, arrays):
    return pl.pallas_call(
        ghost_kernel,
        in_specs=[VMEM] * 12,
        out_specs=[VMEM] * 10,
        out_shape=[pltpu.VMEM(x.shape, F32) for x in arrays],
        scratch_shapes=[pltpu.VMEM((PLANES, 8, LANES), F32)],
        input_output_aliases={n + 2: n for n in range(10)},
        compiler_params=params(8),
        name="ghosts",
    )(a, b, *arrays)


def density_half(t, s):
    k = 0.5 * press_scale * 0.5 * time_step
    return t * (-0.2 * k + (-0.05 * k) * t + (0.02 * k) * s) + (0.8 * k) * s


def pressure(here, t, s, e, p):
    total = (gravity * 0.5 * time_step) * e[here, :]
    for k in range(LEVELS):
        h = density_half(t[k, here, :], s[k, here, :])
        at = total + h
        p[k, here, :] = at
        total = at + h


def coriolis_rows(start, count, rows):
    total = rows * lax.axis_size("lat")
    row = lax.broadcasted_iota(jnp.int32, (count, LANES), 0) + (start - BASE + lax.axis_index("lat") * rows)
    row = jnp.minimum(row, total - 1).astype(F32)
    return (time_step * coriolis_max) * (2.0 * (row + 0.5) / total - 1.0)


def velocity_trial(k, r, n, spin, u, v, w, p, m_east, m_north, matrices=None):
    here, up, down = pl.ds(r, n), pl.ds(r + 1, n), pl.ds(r - 1, n)
    wet = w[k, here, :]
    pc = p[k, here, :]
    if matrices is None:
        wet_east, wet_west, slope = east(wet), west(wet), east(pc) - west(pc)
    else:
        both = jnp.dot(wet.astype(BF16), matrices[0], preferred_element_type=F32)
        wet_east, wet_west, slope = both[:, :LANES], both[:, LANES:], product(pc, matrices[1])
    me = wet * wet_east
    mw = wet * wet_west
    mn = wet * w[k, up, :]
    ms = wet * w[k, down, :]
    m_east[k, here, :] = me
    m_north[k, here, :] = mn

    def lap(q_ref, q):
        return me * (east(q) - q) + mw * (west(q) - q) + (mn * (q_ref[k, up, :] - q) + ms * (q_ref[k, down, :] - q))

    un, vn = u[k, here, :], v[k, here, :]
    u_trial = un + (spin * vn - slope + (time_step * viscosity) * lap(u, un))
    v_trial = vn + ((time_step * viscosity) * lap(v, vn) - spin * un - (p[k, up, :] - p[k, down, :]))
    return wet, u_trial, v_trial


def damping(u, v):
    return 1.0 / (1.0 + drag_coef * jnp.sqrt(u * u + v * v))


FLUX = time_step * 0.5 / 12.0
HEIGHT = time_step / LEVELS * 0.5 / FLUX


def flux(q0, q1, qm, qp, tr, md):
    return tr * (7.0 * (q0 + q1) - (qm + qp)) - md * (q1 - q0)


def north_flux(k, r, n, vel, m_north, tracers, g_refs):
    here, up = pl.ds(r, n), pl.ds(r + 1, n)
    mn = m_north[k, here, :]
    tr = (FLUX * mn) * (vel[k, here, :] + vel[k, up, :])
    md = (time_step * diffusivity) * mn
    out = []
    for q, g in zip(tracers, g_refs):
        gy = flux(q[k, here, :], q[k, up, :], q[k, pl.ds(r - 1, n), :], q[k, pl.ds(r + 2, n), :], tr, md)
        g[k, here, :] = gy
        out.append(gy)
    return tr, out


def east_flux(k, r, n, u_next, m_east, tracers):
    here = pl.ds(r, n)
    me = m_east[k, here, :]
    tr = (FLUX * me) * (u_next + east(u_next))
    md = (time_step * diffusivity) * me
    out = []
    for q_ref in tracers:
        q = q_ref[k, here, :]
        out.append((q, flux(q, east(q), west(q), pltpu.roll(q, LANES - 2, 1), tr, md)))
    return tr, out


def interior(t, s, u, v, w, e, p, face, slope, t_out, s_out, u_out, v_out, h_out, me, mn, vel, gt, gs, hy):
    rows = h_out.shape[0]
    matrices = neighbour_matrix(), difference_matrix()

    def velocities(r, n, store):
        here = pl.ds(r, n)
        spin = coriolis_rows(r, n, rows)
        on_unit = matrices if n % 16 == 0 else None
        trial = [velocity_trial(k, r, n, spin, u, v, w, p, me, mn, on_unit) for k in range(LEVELS)]
        at_floor = [trial[k][0] > (trial[k + 1][0] if k + 1 < LEVELS else 0.0) for k in range(LEVELS)]
        u_floor, v_floor = trial[0][1], trial[0][2]
        for k in range(1, LEVELS):
            u_floor = jnp.where(at_floor[k], trial[k][1], u_floor)
            v_floor = jnp.where(at_floor[k], trial[k][2], v_floor)
        damp = damping(u_floor, v_floor)
        for k in range(LEVELS):
            factor = jnp.where(at_floor[k], damp, trial[k][0])
            v_next = factor * trial[k][2]
            vel[k, here, :] = v_next
            if store:
                out = pl.ds(r - BASE, n)
                u_out[k, out, :] = factor * trial[k][1]
                v_out[k, out, :] = v_next

    def tracers(r, n):
        here, down = pl.ds(r, n), pl.ds(r - 1, n)
        out = pl.ds(r - BASE, n)
        total_x = total_y = 0.0
        for k in range(LEVELS):
            tr_y, (gy_t, gy_s) = north_flux(k, r, n, vel, mn, (t, s), (gt, gs))
            u_next = u_out[k, out, :]
            mask = me[k, here, :]
            tr_x = (FLUX * mask) * (u_next + east(u_next))
            md = (time_step * diffusivity) * mask
            gx_t = tr_x * face[k, out, :] - md * slope[k, out, :]
            gx_s = tr_x * face[LEVELS + k, out, :] - md * slope[LEVELS + k, out, :]
            total_x, total_y = total_x + tr_x, total_y + tr_y
            wet = w[k, here, :]
            t_out[k, out, :] = wet * (t[k, here, :] - (gx_t - west(gx_t) + (gy_t - gt[k, down, :])))
            s_out[k, out, :] = wet * (s[k, here, :] - (gx_s - west(gx_s) + (gy_s - gs[k, down, :])))
        hy[here, :] = total_y
        h_out[out, :] = e[here, :] - HEIGHT * (total_x - west(total_x) + (total_y - hy[down, :]))

    velocities(BASE - 8, 8, False)
    velocities(BASE + rows, 8, False)
    velocities(BASE, rows, True)
    total = 0.0
    for k in range(LEVELS):
        total = total + north_flux(k, BASE - 8, 8, vel, mn, (t, s), (gt, gs))[0]
    hy[pl.ds(BASE - 8, 8), :] = total
    block = rows // MAIN_BLOCKS
    for n in range(MAIN_BLOCKS):
        tracers(BASE + n * block, block)


def interior_outputs(rows):
    return [pltpu.VMEM((LEVELS, rows, LANES), F32)] * 4 + [pltpu.VMEM((rows, LANES), F32)]


def interior_scratch(tall):
    return [pltpu.VMEM((LEVELS, tall, LANES), F32)] * 5 + [pltpu.VMEM((tall, LANES), F32)]


def waits_for_seam():
    return lax.axis_index("lon") == 0


def early_kernel(*refs):
    ins, outs, scratch = refs[:9], refs[11:16], refs[16:]

    @pl.when(waits_for_seam())
    def _():
        interior(*ins, *outs, *scratch)


def early(arrays, message):
    rows, tall = arrays[-1].shape[1], arrays[0].shape[1]
    return pl.pallas_call(
        early_kernel,
        in_specs=[VMEM] * 10,
        out_specs=[VMEM] * 6,
        out_shape=[pltpu.VMEM(message.shape, F32)] + interior_outputs(rows),
        scratch_shapes=interior_scratch(tall),
        input_output_aliases={9: 0},
        compiler_params=params(16),
        name="early",
    )(*arrays, message)


def main_kernel(*refs):
    ins, outs, scratch = refs[:9], refs[14:19], refs[19:]

    @pl.when(jnp.logical_not(waits_for_seam()))
    def _():
        interior(*ins, *outs, *scratch)


def main(arrays, outs):
    rows, tall = arrays[-1].shape[1], arrays[0].shape[1]
    return pl.pallas_call(
        main_kernel,
        in_specs=[VMEM] * 14,
        out_specs=[VMEM] * 5,
        out_shape=interior_outputs(rows),
        scratch_shapes=interior_scratch(tall),
        input_output_aliases={n + 9: n for n in range(5)},
        compiler_params=params(16),
        cost_estimate=pl.CostEstimate(flops=40_000_000, bytes_accessed=8_000_000, transcendentals=100_000),
        name="main",
    )(*arrays, *outs)


def last_kernel(c_ref, m0_ref, m1_ref, place, mt, ms, mu, mv, mh, t_hbm, s_hbm, u_hbm, v_hbm, h_hbm,
                t, s, u, v, w, e, p, me, mn, un, vel, gt, gs, hy, st, ss, sh, ot, os, ou, ov, oh, sems):
    rows = oh.shape[0]
    even = is_even("lon")

    def complete():
        n = rows + 8
        half, _ = message_rows(rows)
        m0, m1 = m0_ref[...], m1_ref[...]
        m_east, m_west = jnp.where(even, m0, m1), jnp.where(even, m1, m0)
        low = jnp.where(lanes(half) < 64, m_east[:half, :], pltpu.roll(m_west[:half, :], 64, 1))
        high = jnp.where(lanes(n - half) < 64, pltpu.roll(m_east[: n - half, :], 64, 1), m_west[: n - half, :])
        four = jnp.concatenate([low, high], axis=0)
        rest_east, rest_west = m_east[half:, :], pltpu.roll(m_west[half:, :], 64, 1)

        def slots(count):
            _, level, slot = strip_layout(count)
            west_side = jnp.where(slot >= 6, 64, 0)
            return level, (slot >= 4) & (slot < 8), west_side + jnp.where(slot % 2 == 1, 1, 0)

        level, ghost, at = slots(n)
        here = pl.ds(BASE, n)
        for f, x in enumerate((t, s, u, v)):
            x[0, here, :] = jnp.where(ghost, gather(four, 2 * LEVELS * f + 2 * level + at), c_ref[f])
        for g in range(-(-n // REST_ROWS)):
            count = min(REST_ROWS, n - g * REST_ROWS)
            level, ghost, at = slots(count)
            lane = lanes(count)
            mine = (lane >= REST_LANES * g) & (lane < REST_LANES * (g + 1))
            rest = jnp.where(mine, rest_east[:count, :], rest_west[:count, :])
            src, dst = pl.ds(g * REST_ROWS, count), pl.ds(BASE + g * REST_ROWS, count)
            index = (REST_LANES * g + 2 * level + at) % LANES
            w[0, dst, :] = jnp.where(ghost, gather(rest, index), c_ref[FIELDS - 1, src, :])
            index = (REST_LANES * g + 2 * LEVELS + at) % LANES
            e[dst, :] = jnp.where(ghost, gather(rest, index), c_ref[FIELDS, src, :])

    def strip_pressure(r, n):
        here = pl.ds(r, n)
        lane = lanes(n)
        h = density_half(t[0, here, :], s[0, here, :])
        total = h
        for step in (16, 32, 64):
            total = total + jnp.where(lane >= step, pltpu.roll(total, step, 1), 0.0)
        p[0, here, :] = (gravity * 0.5 * time_step) * e[here, :] + (2.0 * total - h)

    def strip_velocities(r, n):
        here = pl.ds(r, n)
        lane = lanes(n)
        wet, u_trial, v_trial = velocity_trial(0, r, n, coriolis_rows(r, n, rows), u, v, w, p, me, mn)
        below = jnp.where(lane < LANES - 16, pltpu.roll(wet, LANES - 16, 1), 0.0)
        factor = jnp.where(wet > below, damping(u_trial, v_trial), wet)
        un[0, here, :] = factor * u_trial
        vel[0, here, :] = factor * v_trial

    def on_edge(n):
        lane = lanes(n)
        return (lane < 2) | (lane >= LANES - 2)

    def placed(strip, levels=LEVELS):
        out = []
        high, middle, low = split(strip)
        top = jnp.concatenate([high, middle], axis=1)
        for k in range(0, levels, 2):
            at = slice(k * LANES, (k + 2) * LANES)
            both = jnp.dot(low, place[:LANES, at], preferred_element_type=F32)
            both = both + jnp.dot(top, place[:, at], preferred_element_type=F32)
            out += [both[:, :LANES], both[:, LANES:]]
        return out

    def strip_tracers(r, n):
        here, down = pl.ds(r, n), pl.ds(r - 1, n)
        out = pl.ds(r - BASE, n)
        tr_y, (gy_t, gy_s) = north_flux(0, r, n, vel, mn, (t, s), (gt, gs))
        tr_x, ((tc, gx_t), (sc, gx_s)) = east_flux(0, r, n, un[0, here, :], me, (t, s))
        wet = w[0, here, :]
        hy[here, :] = tr_y
        st[out, :] = wet * (tc - (gx_t - west(gx_t) + (gy_t - gt[0, down, :])))
        ss[out, :] = wet * (sc - (gx_s - west(gx_s) + (gy_s - gs[0, down, :])))
        inflow = tr_x - west(tr_x) + (tr_y - hy[down, :])
        for step in (16, 32, 64):
            inflow = inflow + pltpu.roll(inflow, step, 1)
        sh[out, :] = e[here, :] - HEIGHT * inflow

    copies = []

    def send(x, y):
        copies.append(pltpu.make_async_copy(x, y, sems.at[len(copies)]))
        copies[-1].start()

    complete()
    strip_pressure(BASE, rows + 8)
    for x in (t, s, u, v, w, p):
        x[0, pl.ds(BASE - 8, 8), :] = x[0, pl.ds(BASE + rows, 8), :]
    e[pl.ds(BASE - 8, 8), :] = e[pl.ds(BASE + rows, 8), :]
    strip_velocities(BASE - 8, rows + 16)
    hy[pl.ds(BASE - 8, 8), :] = north_flux(0, BASE - 8, 8, vel, mn, (t, s), (gt, gs))[0]
    whole = pl.ds(BASE, rows)

    def merge(out, strip, inner):
        edge = on_edge(strip.shape[0])
        for k, value in enumerate(placed(strip)):
            out[k] = jnp.where(edge, value, inner[k])

    merge(ou, un[0, whole, :], mu)
    merge(ov, vel[0, whole, :], mv)
    send(ou, u_hbm)
    send(ov, v_hbm)
    strip_tracers(BASE, rows)
    merge(ot, st[...], mt)
    send(ot, t_hbm)
    oh[...] = jnp.where(on_edge(rows), placed(sh[...], 2)[0], mh[...])
    send(oh, h_hbm)
    merge(os, ss[...], ms)
    send(os, s_hbm)
    for x in copies:
        x.wait()


def last(c, m0, m1, place, outs):
    rows = outs[4].shape[0]
    tall = rows + BASE + 16
    big = pltpu.VMEM((1, tall, LANES), F32)
    flat = pltpu.VMEM((tall, LANES), F32)
    short = pltpu.VMEM((rows, LANES), F32)
    out3 = jax.ShapeDtypeStruct((LEVELS, rows, LANES), F32)
    wide = pltpu.VMEM((LEVELS, rows, LANES), F32)
    return pl.pallas_call(
        last_kernel,
        in_specs=[VMEM] * 9,
        out_specs=[HBM] * 5,
        out_shape=[out3] * 4 + [jax.ShapeDtypeStruct((rows, LANES), F32)],
        scratch_shapes=[big] * 5
        + [flat]
        + [big] * 7
        + [flat]
        + [short] * 3
        + [wide] * 4
        + [short, pltpu.SemaphoreType.DMA((5,))],
        compiler_params=params(24),
        name="last",
    )(c, m0, m1, place, *outs)


def swaps():
    lon, lat = lax.axis_size("lon"), lax.axis_size("lat")

    def device(o, a):
        return o % lon * lat + a

    lat_first, lat_second, lon_first, lon_second = [], [], [], []
    for o in range(lon):
        for a in range(lat):
            lat_first.append((device(o, a), device(o, a ^ 1)))
            if a == lat - 1:
                lat_second.append((device(o, a), device(lon - 1 - o, a)))
            elif a > 0:
                lat_second.append((device(o, a), device(o, a + 1 if a % 2 else a - 1)))
            else:
                lat_second.append((device(o, a), device(o ^ 1, a)))
            lon_first.append((device(o, a), device(o ^ 1, a)))
            lon_second.append((device(o, a), device(o + 1 if o % 2 else o - 1, a)))
    return lat_first, lat_second, lon_first, lon_second


def on_device(
    heat_anomaly,
    saltiness_anomaly,
    zonal_current,
    meridional_current,
    free_elevation,
    ocean_indicator,
    floor_layer_index,
):
    lat_first, lat_second, lon_first, lon_second = swaps()
    send = functools.partial(lax.ppermute, axis_name=("lon", "lat"))
    fields = (heat_anomaly, saltiness_anomaly, zonal_current, meridional_current, ocean_indicator)
    a, b = row_pack(fields, free_elevation)
    a = send(a, perm=lat_first)
    b = send(b, perm=lat_second)
    *arrays, face, slope, place = column_pack(fields, free_elevation)
    *arrays, c, m0, m1 = ghosts(a, b, arrays)
    arrays += [face, slope]
    m0 = send(m0, perm=lon_first)
    m1, *outs = early(arrays, m1)
    m1 = send(m1, perm=lon_second)
    outs = main(arrays, outs)
    return tuple(last(c, m0, m1, place, outs))


def solution(mesh):
    return jax.shard_map(
        on_device,
        mesh=mesh,
        in_specs=(
            P(None, "lat", "lon"),
            P(None, "lat", "lon"),
            P(None, "lat", "lon"),
            P(None, "lat", "lon"),
            P("lat", "lon"),
            P(None, "lat", "lon"),
            P("lat", "lon"),
        ),
        out_specs=(
            P(None, "lat", "lon"),
            P(None, "lat", "lon"),
            P(None, "lat", "lon"),
            P(None, "lat", "lon"),
            P("lat", "lon"),
        ),
        check_vma=False,
    )
```

```python
import functools

import jax
import jax.numpy as jnp
from jax import lax
from jax.experimental import pallas as pl
from jax.experimental.pallas import tpu as pltpu
from jax.sharding import PartitionSpec as P

F32 = jnp.float32
BF16 = jnp.bfloat16
LEVELS = 8
LANES = 128
FIELDS = 5
PLANES = FIELDS * LEVELS + 1
ROW_MSG = 2 * FIELDS * LEVELS + 8
BASE = 16
PACK_ROWS = 96
REST_ROWS = 32
REST_LANES = 2 * LEVELS + 2
MAIN_BLOCKS = 1

time_step = 0.2
viscosity = 0.5
diffusivity = 0.3
press_scale = 0.25
gravity = 1.0
drag_coef = 1.0
coriolis_max = 0.5

HBM = pl.BlockSpec(memory_space=pltpu.HBM)
VMEM = pl.BlockSpec(memory_space=pltpu.VMEM)


def params(mib):
    return pltpu.CompilerParams(vmem_limit_bytes=int(mib * 1024 * 1024))


def lanes(rows=8):
    return lax.broadcasted_iota(jnp.int32, (rows, LANES), 1)


def east(x):
    return pltpu.roll(x, LANES - 1, 1)


def west(x):
    return pltpu.roll(x, 1, 1)


def gather(x, index):
    return jnp.take_along_axis(x, index, axis=1)


def strip_layout(rows):
    lane = lanes(rows)
    return lane, lane // 16, lane % 16


def own_strips(packed, rows):
    _, level, slot = strip_layout(rows)
    own = jnp.where(slot < 4, slot, jnp.where((slot >= 8) & (slot < 12), slot - 4, 0))
    out = [gather(packed[f // 2], 8 * level + own + 64 * (f % 2)) for f in range(FIELDS)]
    return out + [gather(packed[2], own + 64)]


def split(x):
    high = x.astype(BF16)
    rest = x - high.astype(F32)
    middle = rest.astype(BF16)
    return high, middle, (rest - middle.astype(F32)).astype(BF16)


def face_matrix():
    step = lane_step()
    face = jnp.where(step < 2, 7.0, jnp.where((step == 2) | (step == LANES - 1), -1.0, 0.0))
    slope = jnp.where(step == 1, 1.0, jnp.where(step == 0, -1.0, 0.0))
    return jnp.concatenate([face, slope], axis=1).astype(BF16)


def product(x, matrix):
    return sum(jnp.dot(part, matrix, preferred_element_type=F32) for part in split(x)[::-1])


def lane_step():
    row = lax.broadcasted_iota(jnp.int32, (LANES, LANES), 0)
    return lax.rem(row - lax.broadcasted_iota(jnp.int32, (LANES, LANES), 1) + LANES, LANES)


def neighbour_matrix():
    step = lane_step()
    return jnp.concatenate([jnp.where(step == 1, 1.0, 0.0), jnp.where(step == LANES - 1, 1.0, 0.0)], axis=1).astype(BF16)


def difference_matrix():
    step = lane_step()
    return jnp.where(step == 1, 1.0, jnp.where(step == LANES - 1, -1.0, 0.0)).astype(BF16)


def place_matrix(level):
    lane, row = (lax.broadcasted_iota(jnp.int32, (LANES, LANES), n) for n in (1, 0))
    slot = jnp.where(lane < 2, lane + 8, jnp.where(lane >= LANES - 2, lane - (LANES - 4), -LANES))
    return jnp.where(row == 16 * level + slot, 1.0, 0.0).astype(BF16)


def is_even(axis):
    return lax.rem(lax.axis_index(axis), 2) == 0


def row_pack_kernel(*refs):
    ins, (a_ref, b_ref), tiles, sems = refs[:6], refs[6:8], refs[8:20], refs[20]
    rows = ins[5].shape[0]
    copies = []
    for n, x in enumerate(ins):
        for side, start in enumerate((0, rows - 8)):
            src = x.at[:, pl.ds(start, 8), :] if n < FIELDS else x.at[pl.ds(start, 8), :]
            copies.append(pltpu.make_async_copy(src, tiles[2 * n + side], sems.at[2 * n + side]))
            copies[-1].start()
    for x in copies:
        x.wait()
    even = is_even("lat")
    for r in range(2):
        for f in range(FIELDS):
            low, high = tiles[2 * f : 2 * f + 2]
            bottom = low.reshape(LEVELS * 8, LANES)[pl.ds(r, LEVELS, stride=8), :].astype(F32)
            top = high.reshape(LEVELS * 8, LANES)[pl.ds(6 + r, LEVELS, stride=8), :].astype(F32)
            place = pl.ds((r * FIELDS + f) * LEVELS, LEVELS)
            a_ref[place, :] = jnp.where(even, top, bottom)
            b_ref[place, :] = jnp.where(even, bottom, top)
    place = pl.ds(2 * FIELDS * LEVELS, 8)
    low, high = tiles[10][...], tiles[11][...]
    a_ref[place, :] = jnp.where(even, high, low)
    b_ref[place, :] = jnp.where(even, low, high)


def row_pack(fields, surface):
    scratch = [pltpu.VMEM((LEVELS, 8, LANES), x.dtype) for x in fields for _ in range(2)]
    scratch += [pltpu.VMEM((8, LANES), F32)] * 2 + [pltpu.SemaphoreType.DMA((12,))]
    return pl.pallas_call(
        row_pack_kernel,
        in_specs=[HBM] * 6,
        out_specs=[VMEM] * 2,
        out_shape=[pltpu.VMEM((ROW_MSG, LANES), F32)] * 2,
        scratch_shapes=scratch,
        compiler_params=params(60),
        name="row_pack",
    )(*fields, surface)


def pack_columns(plane, rows):
    lane = lanes(rows)
    packed = []
    for first in range(0, PLANES, 16):
        group = None
        for p in range(first, min(first + 16, PLANES)):
            q = p - first
            moved = pltpu.roll(plane(p), (8 * q + 4) % LANES, 1)
            group = moved if group is None else jnp.where(lane >= 8 * q, moved, group)
        packed.append(group)
    return packed


def column_messages(packed, even, rows):
    lane = lanes(rows)
    base = 8 * ((lane // 2) % 16) + lane % 2
    messages = []
    for first in (True, False):
        eastern = even if first else jnp.logical_not(even)
        index = base + jnp.where(eastern, 2, 4)
        c0, c1, c2 = [gather(c, index) for c in packed]
        messages.append(jnp.where(lane < 32, c0, jnp.where(lane < 64, c1, c2)))
    return messages


def message_rows(rows):
    half = (rows + 8 + 15) // 16 * 8
    return half, half + REST_ROWS


def compact(message, rows):
    half, _ = message_rows(rows)
    lane = lanes(half)
    second = jnp.concatenate([message[half:rows, :], jnp.zeros((2 * half - rows, LANES), F32)], axis=0)
    main = jnp.where(lane < 64, message[:half, :], pltpu.roll(second, 64, 1))
    lane = lanes(REST_ROWS)
    rest = jnp.zeros((REST_ROWS, LANES), F32)
    for g in range(rows // REST_ROWS):
        part = pltpu.roll(message[g * REST_ROWS : (g + 1) * REST_ROWS, :], (REST_LANES * g - 64) % LANES, 1)
        rest = jnp.where((lane >= REST_LANES * g) & (lane < REST_LANES * (g + 1)), part, rest)
    return main, rest


def column_pack_kernel(t_in, s_in, u_in, v_in, w_in, e_in, t, s, u, v, w, e, p, c_ref, m0_ref, m1_ref, face, slope, xu, xv, me, place, m0_wide, m1_wide):
    rows = e_in.shape[0]
    even = is_even("lon")
    matrix, neighbours, difference = face_matrix(), neighbour_matrix(), difference_matrix()
    for k in range(LEVELS):
        place[:LANES, k * LANES : (k + 1) * LANES] = place_matrix(k)
        place[LANES:, k * LANES : (k + 1) * LANES] = place_matrix(k)

    def step(i, _):
        out = pl.ds(pl.multiple_of(i * PACK_ROWS, 8), PACK_ROWS)
        here = pl.ds(pl.multiple_of(BASE + i * PACK_ROWS, 8), PACK_ROWS)
        for x, y in ((t_in, t), (s_in, s), (u_in, u), (v_in, v), (w_in, w)):
            for k in range(LEVELS):
                y[k, here, :] = x[k, out, :].astype(F32)
        e[here, :] = e_in[out, :]

        def plane(q):
            if q == PLANES - 1:
                return e_in[out, :]
            return (t_in, s_in, u_in, v_in, w_in)[q // LEVELS][q % LEVELS, out, :].astype(F32)

        packed = pack_columns(plane, PACK_ROWS)
        for n, x in enumerate(own_strips(packed, PACK_ROWS)):
            c_ref[n, out, :] = x
        m0_wide[out, :], m1_wide[out, :] = column_messages(packed, even, PACK_ROWS)
        total = (gravity * 0.5 * time_step) * e_in[out, :]
        for k in range(LEVELS):
            h = density_half(t_in[k, out, :], s_in[k, out, :])
            at = total + h
            p[k, here, :] = at
            total = at + h
            wet = w_in[k, out, :].astype(F32)
            both = jnp.dot(wet.astype(BF16), neighbours, preferred_element_type=F32)
            m_east, m_west = wet * both[:, :LANES], wet * both[:, LANES:]
            me[k, out, :] = m_east
            for x, y, gradient in ((u_in, xu, product(at, difference)), (v_in, xv, 0.0)):
                q = x[k, out, :]
                spread = m_east * (east(q) - q) + m_west * (west(q) - q)
                y[k, out, :] = q - gradient + (time_step * viscosity) * spread
        for n, x in enumerate((t_in, s_in)):
            for k in range(LEVELS):
                both = product(x[k, out, :], matrix)
                face[n * LEVELS + k, out, :] = both[:, :LANES]
                slope[n * LEVELS + k, out, :] = both[:, LANES:]
        return 0

    lax.fori_loop(0, rows // PACK_ROWS, step, 0)
    half, _ = message_rows(rows)
    for wide, out in ((m0_wide, m0_ref), (m1_wide, m1_ref)):
        main, rest = compact(wide[...], rows)
        out[:half, :] = main
        out[half:, :] = rest


def column_pack(fields, surface):
    rows = surface.shape[0]
    tall = rows + BASE + 16
    big = pltpu.VMEM((LEVELS, tall, LANES), F32)
    return pl.pallas_call(
        column_pack_kernel,
        in_specs=[VMEM] * 6,
        out_specs=[VMEM] * 16,
        out_shape=[big] * 5
        + [pltpu.VMEM((tall, LANES), F32), big]
        + [pltpu.VMEM((FIELDS + 1, rows + 8, LANES), F32)]
        + [pltpu.VMEM((message_rows(rows)[1], LANES), F32)] * 2
        + [pltpu.VMEM((2 * LEVELS, rows, LANES), F32)] * 2
        + [pltpu.VMEM((LEVELS, rows, LANES), F32)] * 3
        + [pltpu.VMEM((2 * LANES, LEVELS * LANES), BF16)],
        scratch_shapes=[pltpu.VMEM((rows, LANES), F32)] * 2,
        compiler_params=params(16),
        cost_estimate=pl.CostEstimate(flops=10_000_000, bytes_accessed=6_000_000, transcendentals=0),
        name="column_pack",
    )(*fields, surface)


def ghost_kernel(a_ref, b_ref, *refs):
    t, s, u, v, w, e, p, c_ref, m0_ref, m1_ref, g_ref = refs[10:]
    rows = c_ref.shape[1] - 8
    even = is_even("lat")
    fold = lax.axis_index("lat") == lax.axis_size("lat") - 1
    mirror = LANES - 1 - lanes()
    flat = g_ref.reshape(PLANES * 8, LANES)
    g_ref[...] = jnp.zeros_like(g_ref)

    southmost = lax.axis_index("lat") == 0

    def both(start):
        a, b = a_ref[pl.ds(start, 8), :], b_ref[pl.ds(start, 8), :]
        return jnp.where(even, a, b), jnp.where(southmost, 0.0, jnp.where(even, b, a))

    for f in range(FIELDS):
        sign = -1.0 if f in (2, 3) else 1.0
        north0, south0 = both(f * LEVELS)
        north1, south1 = both((FIELDS + f) * LEVELS)
        first = jnp.where(fold, sign * gather(north1, mirror), north0)
        second = jnp.where(fold, sign * gather(north0, mirror), north1)
        for row, value in ((0, first), (1, second), (6, south0), (7, south1)):
            flat[pl.ds(f * LEVELS * 8 + row, LEVELS, stride=8), :] = value
    north, south = both(2 * FIELDS * LEVELS)
    turned = gather(north, mirror)
    row = lax.broadcasted_iota(jnp.int32, (8, LANES), 0)
    folded = jnp.where(row == 0, pltpu.roll(turned, 1, 0), pltpu.roll(turned, 3, 0))
    g_ref[PLANES - 1] = jnp.where(row < 2, jnp.where(fold, folded, north), jnp.where(row >= 6, south, 0.0))
    packed = pack_columns(lambda q: g_ref[q], 8)
    last = pl.ds(rows, 8)
    for n, x in enumerate(own_strips(packed, 8)):
        c_ref[n, last, :] = x
    half, _ = message_rows(rows)
    lane = lanes()
    first = REST_LANES * (rows // REST_ROWS)
    for out, message in zip((m0_ref, m1_ref), column_messages(packed, is_even("lon"), 8)):
        place = pl.ds(rows - half, 8)
        out[place, :] = jnp.where(lane < 64, out[place, :], pltpu.roll(message, 64, 1))
        place = pl.ds(half, 8)
        moved = pltpu.roll(message, (first - 64) % LANES, 1)
        out[place, :] = jnp.where((lane >= first) & (lane < first + REST_LANES), moved, out[place, :])
    for side in (pl.ds(BASE - 8, 8), pl.ds(BASE + rows, 8)):
        for f, x in enumerate((t, s, u, v, w)):
            for k in range(LEVELS):
                x[k, side, :] = g_ref[f * LEVELS + k]
        e[side, :] = g_ref[PLANES - 1]
        pressure(side, t, s, e, p)


def ghosts(a, b, arrays):
    return pl.pallas_call(
        ghost_kernel,
        in_specs=[VMEM] * 12,
        out_specs=[VMEM] * 10,
        out_shape=[pltpu.VMEM(x.shape, F32) for x in arrays],
        scratch_shapes=[pltpu.VMEM((PLANES, 8, LANES), F32)],
        input_output_aliases={n + 2: n for n in range(10)},
        compiler_params=params(8),
        name="ghosts",
    )(a, b, *arrays)


def density_half(t, s):
    k = 0.5 * press_scale * 0.5 * time_step
    return t * (-0.2 * k + (-0.05 * k) * t + (0.02 * k) * s) + (0.8 * k) * s


def pressure(here, t, s, e, p):
    total = (gravity * 0.5 * time_step) * e[here, :]
    for k in range(LEVELS):
        h = density_half(t[k, here, :], s[k, here, :])
        at = total + h
        p[k, here, :] = at
        total = at + h


def coriolis_rows(start, count, rows):
    total = rows * lax.axis_size("lat")
    row = lax.broadcasted_iota(jnp.int32, (count, LANES), 0) + (start - BASE + lax.axis_index("lat") * rows)
    row = jnp.minimum(row, total - 1).astype(F32)
    return (time_step * coriolis_max) * (2.0 * (row + 0.5) / total - 1.0)


def velocity_trial(k, r, n, spin, u, v, w, p, m_east, m_north):
    here, up, down = pl.ds(r, n), pl.ds(r + 1, n), pl.ds(r - 1, n)
    wet = w[k, here, :]
    me = wet * east(wet)
    mw = wet * west(wet)
    mn = wet * w[k, up, :]
    ms = wet * w[k, down, :]
    if m_east is not None:
        m_east[k, here, :] = me
    m_north[k, here, :] = mn

    def lap(q_ref, q):
        return me * (east(q) - q) + mw * (west(q) - q) + (mn * (q_ref[k, up, :] - q) + ms * (q_ref[k, down, :] - q))

    un, vn = u[k, here, :], v[k, here, :]
    pc = p[k, here, :]
    u_trial = un + (spin * vn - (east(pc) - west(pc)) + (time_step * viscosity) * lap(u, un))
    v_trial = vn + ((time_step * viscosity) * lap(v, vn) - spin * un - (p[k, up, :] - p[k, down, :]))
    return wet, u_trial, v_trial


def velocity_trial_y(k, r, n, spin, u, v, w, p, xu, xv, m_north):
    here, up, down = pl.ds(r, n), pl.ds(r + 1, n), pl.ds(r - 1, n)
    out = pl.ds(r - BASE, n)
    wet = w[k, here, :]
    mn = wet * w[k, up, :]
    ms = wet * w[k, down, :]
    m_north[k, here, :] = mn

    def lap(q_ref, q):
        return (time_step * viscosity) * (mn * (q_ref[k, up, :] - q) + ms * (q_ref[k, down, :] - q))

    un, vn = u[k, here, :], v[k, here, :]
    u_trial = xu[k, out, :] + (spin * vn + lap(u, un))
    v_trial = xv[k, out, :] + (lap(v, vn) - spin * un - (p[k, up, :] - p[k, down, :]))
    return wet, u_trial, v_trial


def damping(u, v):
    return 1.0 / (1.0 + drag_coef * jnp.sqrt(u * u + v * v))


FLUX = time_step * 0.5 / 12.0
HEIGHT = time_step / LEVELS * 0.5 / FLUX


def flux(q0, q1, qm, qp, tr, md):
    return tr * (7.0 * (q0 + q1) - (qm + qp)) - md * (q1 - q0)


def north_flux(k, r, n, vel, m_north, tracers, g_refs):
    here, up = pl.ds(r, n), pl.ds(r + 1, n)
    mn = m_north[k, here, :]
    tr = (FLUX * mn) * (vel[k, here, :] + vel[k, up, :])
    md = (time_step * diffusivity) * mn
    out = []
    for q, g in zip(tracers, g_refs):
        gy = flux(q[k, here, :], q[k, up, :], q[k, pl.ds(r - 1, n), :], q[k, pl.ds(r + 2, n), :], tr, md)
        g[k, here, :] = gy
        out.append(gy)
    return tr, out


def east_flux(k, r, n, u_next, m_east, tracers):
    here = pl.ds(r, n)
    me = m_east[k, here, :]
    tr = (FLUX * me) * (u_next + east(u_next))
    md = (time_step * diffusivity) * me
    out = []
    for q_ref in tracers:
        q = q_ref[k, here, :]
        out.append((q, flux(q, east(q), west(q), pltpu.roll(q, LANES - 2, 1), tr, md)))
    return tr, out


def new_velocities(u, v, w, p, xu, xv, u_out, v_out, vel, mn):
    rows = u_out.shape[1]

    def velocities(r, n, store):
        here = pl.ds(r, n)
        spin = coriolis_rows(r, n, rows)
        if store:
            trial = [velocity_trial_y(k, r, n, spin, u, v, w, p, xu, xv, mn) for k in range(LEVELS)]
        else:
            trial = [velocity_trial(k, r, n, spin, u, v, w, p, None, mn) for k in range(LEVELS)]
        at_floor = [trial[k][0] > (trial[k + 1][0] if k + 1 < LEVELS else 0.0) for k in range(LEVELS)]
        u_floor, v_floor = trial[0][1], trial[0][2]
        for k in range(1, LEVELS):
            u_floor = jnp.where(at_floor[k], trial[k][1], u_floor)
            v_floor = jnp.where(at_floor[k], trial[k][2], v_floor)
        damp = damping(u_floor, v_floor)
        for k in range(LEVELS):
            factor = jnp.where(at_floor[k], damp, trial[k][0])
            v_next = factor * trial[k][2]
            vel[k, here, :] = v_next
            if store:
                out = pl.ds(r - BASE, n)
                u_out[k, out, :] = factor * trial[k][1]
                v_out[k, out, :] = v_next

    velocities(BASE - 8, 8, False)
    velocities(BASE + rows, 8, False)
    for n in range(MAIN_BLOCKS):
        velocities(BASE + n * (rows // MAIN_BLOCKS), rows // MAIN_BLOCKS, True)


def new_tracers(t, s, w, e, face, slope, me, u_out, vel, mn, t_out, s_out, h_out, gt, gs, hy):
    rows = h_out.shape[0]
    total = 0.0
    for k in range(LEVELS):
        total = total + north_flux(k, BASE - 8, 8, vel, mn, (t, s), (gt, gs))[0]
    hy[pl.ds(BASE - 8, 8), :] = total
    here, down = pl.ds(BASE, rows), pl.ds(BASE - 1, rows)
    total_x = total_y = 0.0
    for k in range(LEVELS):
        tr_y, (gy_t, gy_s) = north_flux(k, BASE, rows, vel, mn, (t, s), (gt, gs))
        u_next = u_out[k]
        mask = me[k]
        tr_x = (FLUX * mask) * (u_next + east(u_next))
        md = (time_step * diffusivity) * mask
        gx_t = tr_x * face[k] - md * slope[k]
        gx_s = tr_x * face[LEVELS + k] - md * slope[LEVELS + k]
        total_x, total_y = total_x + tr_x, total_y + tr_y
        wet = w[k, here, :]
        t_out[k] = wet * (t[k, here, :] - (gx_t - west(gx_t) + (gy_t - gt[k, down, :])))
        s_out[k] = wet * (s[k, here, :] - (gx_s - west(gx_s) + (gy_s - gs[k, down, :])))
    hy[here, :] = total_y
    h_out[...] = e[here, :] - HEIGHT * (total_x - west(total_x) + (total_y - hy[down, :]))


def waits_for_seam():
    return (lax.axis_index("lon") == 0) & (lax.axis_index("lat") < lax.axis_size("lat") - 1)


def early_kernel(*refs):
    ins, outs = refs[:6], refs[8:]

    @pl.when(waits_for_seam())
    def _():
        new_velocities(*ins, *outs)


def early(u, v, w, p, xu, xv, message):
    wide, high = pltpu.VMEM(xu.shape, F32), pltpu.VMEM(u.shape, F32)
    return pl.pallas_call(
        early_kernel,
        in_specs=[VMEM] * 7,
        out_specs=[VMEM] * 5,
        out_shape=[pltpu.VMEM(message.shape, F32), wide, wide, high, high],
        input_output_aliases={6: 0},
        compiler_params=params(16),
        name="early",
    )(u, v, w, p, xu, xv, message)


def main_kernel(*refs):
    (t, s, u, v, w, e, p, face, slope, xu, xv, me), outs, scratch = refs[:12], refs[16:23], refs[23:]
    u_out, v_out, vel, mn, t_out, s_out, h_out = outs

    @pl.when(jnp.logical_not(waits_for_seam()))
    def _():
        new_velocities(u, v, w, p, xu, xv, u_out, v_out, vel, mn)

    new_tracers(t, s, w, e, face, slope, me, u_out, vel, mn, t_out, s_out, h_out, *scratch)


def main(arrays, velocities):
    rows, tall = arrays[-1].shape[1], arrays[0].shape[1]
    wide, high = pltpu.VMEM((LEVELS, rows, LANES), F32), pltpu.VMEM((LEVELS, tall, LANES), F32)
    return pl.pallas_call(
        main_kernel,
        in_specs=[VMEM] * 16,
        out_specs=[VMEM] * 7,
        out_shape=[wide, wide, high, high, wide, wide, pltpu.VMEM((rows, LANES), F32)],
        scratch_shapes=[high, high, pltpu.VMEM((tall, LANES), F32)],
        input_output_aliases={n + 12: n for n in range(4)},
        compiler_params=params(16),
        cost_estimate=pl.CostEstimate(flops=40_000_000, bytes_accessed=8_000_000, transcendentals=100_000),
        name="main",
    )(*arrays, *velocities)


def last_kernel(c_ref, m0_ref, m1_ref, place, mt, ms, mu, mv, mh, t_hbm, s_hbm, u_hbm, v_hbm, h_hbm,
                t, s, u, v, w, e, p, me, mn, un, vel, gt, gs, hy, st, ss, sh, ot, os, ou, ov, oh, sems):
    rows = oh.shape[0]
    even = is_even("lon")

    def complete():
        n = rows + 8
        half, _ = message_rows(rows)
        m0, m1 = m0_ref[...], m1_ref[...]
        m_east, m_west = jnp.where(even, m0, m1), jnp.where(even, m1, m0)
        low = jnp.where(lanes(half) < 64, m_east[:half, :], pltpu.roll(m_west[:half, :], 64, 1))
        high = jnp.where(lanes(n - half) < 64, pltpu.roll(m_east[: n - half, :], 64, 1), m_west[: n - half, :])
        four = jnp.concatenate([low, high], axis=0)
        rest_east, rest_west = m_east[half:, :], pltpu.roll(m_west[half:, :], 64, 1)

        def slots(count):
            _, level, slot = strip_layout(count)
            west_side = jnp.where(slot >= 6, 64, 0)
            return level, (slot >= 4) & (slot < 8), west_side + jnp.where(slot % 2 == 1, 1, 0)

        level, ghost, at = slots(n)
        here = pl.ds(BASE, n)
        for f, x in enumerate((t, s, u, v)):
            x[0, here, :] = jnp.where(ghost, gather(four, 2 * LEVELS * f + 2 * level + at), c_ref[f])
        for g in range(-(-n // REST_ROWS)):
            count = min(REST_ROWS, n - g * REST_ROWS)
            level, ghost, at = slots(count)
            lane = lanes(count)
            mine = (lane >= REST_LANES * g) & (lane < REST_LANES * (g + 1))
            rest = jnp.where(mine, rest_east[:count, :], rest_west[:count, :])
            src, dst = pl.ds(g * REST_ROWS, count), pl.ds(BASE + g * REST_ROWS, count)
            index = (REST_LANES * g + 2 * level + at) % LANES
            w[0, dst, :] = jnp.where(ghost, gather(rest, index), c_ref[FIELDS - 1, src, :])
            index = (REST_LANES * g + 2 * LEVELS + at) % LANES
            e[dst, :] = jnp.where(ghost, gather(rest, index), c_ref[FIELDS, src, :])

    def strip_pressure(r, n):
        here = pl.ds(r, n)
        lane = lanes(n)
        h = density_half(t[0, here, :], s[0, here, :])
        total = h
        for step in (16, 32, 64):
            total = total + jnp.where(lane >= step, pltpu.roll(total, step, 1), 0.0)
        p[0, here, :] = (gravity * 0.5 * time_step) * e[here, :] + (2.0 * total - h)

    def strip_velocities(r, n):
        here = pl.ds(r, n)
        lane = lanes(n)
        wet, u_trial, v_trial = velocity_trial(0, r, n, coriolis_rows(r, n, rows), u, v, w, p, me, mn)
        below = jnp.where(lane < LANES - 16, pltpu.roll(wet, LANES - 16, 1), 0.0)
        factor = jnp.where(wet > below, damping(u_trial, v_trial), wet)
        un[0, here, :] = factor * u_trial
        vel[0, here, :] = factor * v_trial

    def on_edge(n):
        lane = lanes(n)
        return (lane < 2) | (lane >= LANES - 2)

    def placed(strip, levels=LEVELS):
        out = []
        high, middle, low = split(strip)
        top = jnp.concatenate([high, middle], axis=1)
        for k in range(0, levels, 2):
            at = slice(k * LANES, (k + 2) * LANES)
            both = jnp.dot(low, place[:LANES, at], preferred_element_type=F32)
            both = both + jnp.dot(top, place[:, at], preferred_element_type=F32)
            out += [both[:, :LANES], both[:, LANES:]]
        return out

    def strip_tracers(r, n):
        here, down = pl.ds(r, n), pl.ds(r - 1, n)
        out = pl.ds(r - BASE, n)
        tr_y, (gy_t, gy_s) = north_flux(0, r, n, vel, mn, (t, s), (gt, gs))
        tr_x, ((tc, gx_t), (sc, gx_s)) = east_flux(0, r, n, un[0, here, :], me, (t, s))
        wet = w[0, here, :]
        hy[here, :] = tr_y
        st[out, :] = wet * (tc - (gx_t - west(gx_t) + (gy_t - gt[0, down, :])))
        ss[out, :] = wet * (sc - (gx_s - west(gx_s) + (gy_s - gs[0, down, :])))
        inflow = tr_x - west(tr_x) + (tr_y - hy[down, :])
        for step in (16, 32, 64):
            inflow = inflow + pltpu.roll(inflow, step, 1)
        sh[out, :] = e[here, :] - HEIGHT * inflow

    copies = []

    def send(x, y):
        copies.append(pltpu.make_async_copy(x, y, sems.at[len(copies)]))
        copies[-1].start()

    complete()
    strip_pressure(BASE, rows + 8)
    for x in (t, s, u, v, w, p):
        x[0, pl.ds(BASE - 8, 8), :] = x[0, pl.ds(BASE + rows, 8), :]
    e[pl.ds(BASE - 8, 8), :] = e[pl.ds(BASE + rows, 8), :]
    strip_velocities(BASE - 8, rows + 16)
    hy[pl.ds(BASE - 8, 8), :] = north_flux(0, BASE - 8, 8, vel, mn, (t, s), (gt, gs))[0]
    whole = pl.ds(BASE, rows)

    def merge(out, strip, inner):
        edge = on_edge(strip.shape[0])
        for k, value in enumerate(placed(strip)):
            out[k] = jnp.where(edge, value, inner[k])

    merge(ou, un[0, whole, :], mu)
    merge(ov, vel[0, whole, :], mv)
    send(ou, u_hbm)
    send(ov, v_hbm)
    strip_tracers(BASE, rows)
    merge(ot, st[...], mt)
    send(ot, t_hbm)
    oh[...] = jnp.where(on_edge(rows), placed(sh[...], 2)[0], mh[...])
    send(oh, h_hbm)
    merge(os, ss[...], ms)
    send(os, s_hbm)
    for x in copies:
        x.wait()


def last(c, m0, m1, place, outs):
    rows = outs[4].shape[0]
    tall = rows + BASE + 16
    big = pltpu.VMEM((1, tall, LANES), F32)
    flat = pltpu.VMEM((tall, LANES), F32)
    short = pltpu.VMEM((rows, LANES), F32)
    out3 = jax.ShapeDtypeStruct((LEVELS, rows, LANES), F32)
    wide = pltpu.VMEM((LEVELS, rows, LANES), F32)
    return pl.pallas_call(
        last_kernel,
        in_specs=[VMEM] * 9,
        out_specs=[HBM] * 5,
        out_shape=[out3] * 4 + [jax.ShapeDtypeStruct((rows, LANES), F32)],
        scratch_shapes=[big] * 5
        + [flat]
        + [big] * 7
        + [flat]
        + [short] * 3
        + [wide] * 4
        + [short, pltpu.SemaphoreType.DMA((5,))],
        compiler_params=params(24),
        name="last",
    )(c, m0, m1, place, *outs)


def swaps():
    lon, lat = lax.axis_size("lon"), lax.axis_size("lat")

    def device(o, a):
        return o % lon * lat + a

    lat_first, lat_second, lon_first, lon_second = [], [], [], []
    for o in range(lon):
        for a in range(lat):
            lat_first.append((device(o, a), device(o, a ^ 1)))
            if a == lat - 1:
                lat_second.append((device(o, a), device(lon - 1 - o, a)))
            elif a > 0:
                lat_second.append((device(o, a), device(o, a + 1 if a % 2 else a - 1)))
            else:
                lat_second.append((device(o, a), device(o ^ 1, a)))
            lon_first.append((device(o, a), device(o ^ 1, a)))
            lon_second.append((device(o, a), device(o + 1 if o % 2 else o - 1, a)))
    return lat_first, lat_second, lon_first, lon_second


def on_device(
    heat_anomaly,
    saltiness_anomaly,
    zonal_current,
    meridional_current,
    free_elevation,
    ocean_indicator,
    floor_layer_index,
):
    lat_first, lat_second, lon_first, lon_second = swaps()
    send = functools.partial(lax.ppermute, axis_name=("lon", "lat"))
    fields = (heat_anomaly, saltiness_anomaly, zonal_current, meridional_current, ocean_indicator)
    a, b = row_pack(fields, free_elevation)
    a = send(a, perm=lat_first)
    b = send(b, perm=lat_second)
    *arrays, face, slope, xu, xv, me, place = column_pack(fields, free_elevation)
    t, s, u, v, w, e, p, c, m0, m1 = ghosts(a, b, arrays)
    m0 = send(m0, perm=lon_first)
    m1, *velocities = early(u, v, w, p, xu, xv, m1)
    m1 = send(m1, perm=lon_second)
    u_next, v_next, _, _, *tracers = main((t, s, u, v, w, e, p, face, slope, xu, xv, me), velocities)
    return tuple(last(c, m0, m1, place, (*tracers[:2], u_next, v_next, tracers[2])))


def solution(mesh):
    return jax.shard_map(
        on_device,
        mesh=mesh,
        in_specs=(
            P(None, "lat", "lon"),
            P(None, "lat", "lon"),
            P(None, "lat", "lon"),
            P(None, "lat", "lon"),
            P("lat", "lon"),
            P(None, "lat", "lon"),
            P("lat", "lon"),
        ),
        out_specs=(
            P(None, "lat", "lon"),
            P(None, "lat", "lon"),
            P(None, "lat", "lon"),
            P(None, "lat", "lon"),
            P("lat", "lon"),
        ),
        check_vma=False,
    )
```

```python
import functools

import jax
import jax.numpy as jnp
from jax import lax
from jax.experimental import pallas as pl
from jax.experimental.pallas import tpu as pltpu
from jax.sharding import PartitionSpec as P

F32 = jnp.float32
BF16 = jnp.bfloat16
LEVELS = 8
LANES = 128
FIELDS = 5
PLANES = FIELDS * LEVELS + 1
ROW_MSG = 2 * FIELDS * LEVELS + 8
BASE = 16
PACK_ROWS = 96
REST_ROWS = 32
REST_LANES = 2 * LEVELS + 2
MAIN_BLOCKS = 1

time_step = 0.2
viscosity = 0.5
diffusivity = 0.3
press_scale = 0.25
gravity = 1.0
drag_coef = 1.0
coriolis_max = 0.5

HBM = pl.BlockSpec(memory_space=pltpu.HBM)
VMEM = pl.BlockSpec(memory_space=pltpu.VMEM)


def params(mib):
    return pltpu.CompilerParams(vmem_limit_bytes=int(mib * 1024 * 1024))


def lanes(rows=8):
    return lax.broadcasted_iota(jnp.int32, (rows, LANES), 1)


def east(x):
    return pltpu.roll(x, LANES - 1, 1)


def west(x):
    return pltpu.roll(x, 1, 1)


def gather(x, index):
    return jnp.take_along_axis(x, index, axis=1)


def strip_layout(rows):
    lane = lanes(rows)
    return lane, lane // 16, lane % 16


def own_strips(packed, rows):
    _, level, slot = strip_layout(rows)
    own = jnp.where(slot < 4, slot, jnp.where((slot >= 8) & (slot < 12), slot - 4, 0))
    out = [gather(packed[f // 2], 8 * level + own + 64 * (f % 2)) for f in range(FIELDS)]
    return out + [gather(packed[2], own + 64)]


def split(x):
    high = x.astype(BF16)
    rest = x - high.astype(F32)
    middle = rest.astype(BF16)
    return high, middle, (rest - middle.astype(F32)).astype(BF16)


def face_matrix():
    step = lane_step()
    face = jnp.where(step < 2, 7.0, jnp.where((step == 2) | (step == LANES - 1), -1.0, 0.0))
    slope = jnp.where(step == 1, 1.0, jnp.where(step == 0, -1.0, 0.0))
    return jnp.concatenate([face, slope], axis=1).astype(BF16)


def product(x, matrix):
    return sum(jnp.dot(part, matrix, preferred_element_type=F32) for part in split(x)[::-1])


def lane_step():
    row = lax.broadcasted_iota(jnp.int32, (LANES, LANES), 0)
    return lax.rem(row - lax.broadcasted_iota(jnp.int32, (LANES, LANES), 1) + LANES, LANES)


def neighbour_matrix():
    step = lane_step()
    return jnp.concatenate([jnp.where(step == 1, 1.0, 0.0), jnp.where(step == LANES - 1, 1.0, 0.0)], axis=1).astype(BF16)


def difference_matrix():
    step = lane_step()
    return jnp.where(step == 1, 1.0, jnp.where(step == LANES - 1, -1.0, 0.0)).astype(BF16)


def place_matrix(level):
    lane, row = (lax.broadcasted_iota(jnp.int32, (LANES, LANES), n) for n in (1, 0))
    slot = jnp.where(lane < 2, lane + 8, jnp.where(lane >= LANES - 2, lane - (LANES - 4), -LANES))
    return jnp.where(row == 16 * level + slot, 1.0, 0.0).astype(BF16)


def is_even(axis):
    return lax.rem(lax.axis_index(axis), 2) == 0


def row_pack_kernel(*refs):
    ins, (a_ref, b_ref), tiles, sems = refs[:6], refs[6:8], refs[8:20], refs[20]
    rows = ins[5].shape[0]
    copies = []
    for n, x in enumerate(ins):
        for side, start in enumerate((0, rows - 8)):
            src = x.at[:, pl.ds(start, 8), :] if n < FIELDS else x.at[pl.ds(start, 8), :]
            copies.append(pltpu.make_async_copy(src, tiles[2 * n + side], sems.at[2 * n + side]))
            copies[-1].start()
    for x in copies:
        x.wait()
    even = is_even("lat")
    for r in range(2):
        for f in range(FIELDS):
            low, high = tiles[2 * f : 2 * f + 2]
            bottom = low.reshape(LEVELS * 8, LANES)[pl.ds(r, LEVELS, stride=8), :].astype(F32)
            top = high.reshape(LEVELS * 8, LANES)[pl.ds(6 + r, LEVELS, stride=8), :].astype(F32)
            place = pl.ds((r * FIELDS + f) * LEVELS, LEVELS)
            a_ref[place, :] = jnp.where(even, top, bottom)
            b_ref[place, :] = jnp.where(even, bottom, top)
    place = pl.ds(2 * FIELDS * LEVELS, 8)
    low, high = tiles[10][...], tiles[11][...]
    a_ref[place, :] = jnp.where(even, high, low)
    b_ref[place, :] = jnp.where(even, low, high)


def row_pack(fields, surface):
    scratch = [pltpu.VMEM((LEVELS, 8, LANES), x.dtype) for x in fields for _ in range(2)]
    scratch += [pltpu.VMEM((8, LANES), F32)] * 2 + [pltpu.SemaphoreType.DMA((12,))]
    return pl.pallas_call(
        row_pack_kernel,
        in_specs=[HBM] * 6,
        out_specs=[VMEM] * 2,
        out_shape=[pltpu.VMEM((ROW_MSG, LANES), F32)] * 2,
        scratch_shapes=scratch,
        compiler_params=params(60),
        name="row_pack",
    )(*fields, surface)


def pack_columns(plane, rows):
    lane = lanes(rows)
    packed = []
    for first in range(0, PLANES, 16):
        group = None
        for p in range(first, min(first + 16, PLANES)):
            q = p - first
            moved = pltpu.roll(plane(p), (8 * q + 4) % LANES, 1)
            group = moved if group is None else jnp.where(lane >= 8 * q, moved, group)
        packed.append(group)
    return packed


def column_messages(packed, even, rows):
    lane = lanes(rows)
    base = 8 * ((lane // 2) % 16) + lane % 2
    messages = []
    for first in (True, False):
        eastern = even if first else jnp.logical_not(even)
        index = base + jnp.where(eastern, 2, 4)
        c0, c1, c2 = [gather(c, index) for c in packed]
        messages.append(jnp.where(lane < 32, c0, jnp.where(lane < 64, c1, c2)))
    return messages


def message_rows(rows):
    half = (rows + 8 + 15) // 16 * 8
    return half, half + REST_ROWS


def compact(message, rows):
    half, _ = message_rows(rows)
    lane = lanes(half)
    second = jnp.concatenate([message[half:rows, :], jnp.zeros((2 * half - rows, LANES), F32)], axis=0)
    main = jnp.where(lane < 64, message[:half, :], pltpu.roll(second, 64, 1))
    lane = lanes(REST_ROWS)
    rest = jnp.zeros((REST_ROWS, LANES), F32)
    for g in range(rows // REST_ROWS):
        part = pltpu.roll(message[g * REST_ROWS : (g + 1) * REST_ROWS, :], (REST_LANES * g - 64) % LANES, 1)
        rest = jnp.where((lane >= REST_LANES * g) & (lane < REST_LANES * (g + 1)), part, rest)
    return main, rest


def column_pack_kernel(t_in, s_in, u_in, v_in, w_in, e_in, t, s, u, v, w, e, p, c_ref, m0_ref, m1_ref, face, slope, xu, xv, me, place, m0_wide, m1_wide):
    rows = e_in.shape[0]
    even = is_even("lon")
    matrix, neighbours, difference = face_matrix(), neighbour_matrix(), difference_matrix()
    for k in range(LEVELS):
        place[:LANES, k * LANES : (k + 1) * LANES] = place_matrix(k)
        place[LANES:, k * LANES : (k + 1) * LANES] = place_matrix(k)

    def step(i, _):
        out = pl.ds(pl.multiple_of(i * PACK_ROWS, 8), PACK_ROWS)
        here = pl.ds(pl.multiple_of(BASE + i * PACK_ROWS, 8), PACK_ROWS)
        for x, y in ((t_in, t), (s_in, s), (u_in, u), (v_in, v), (w_in, w)):
            for k in range(LEVELS):
                y[k, here, :] = x[k, out, :].astype(F32)
        e[here, :] = e_in[out, :]

        def plane(q):
            if q == PLANES - 1:
                return e_in[out, :]
            return (t_in, s_in, u_in, v_in, w_in)[q // LEVELS][q % LEVELS, out, :].astype(F32)

        packed = pack_columns(plane, PACK_ROWS)
        for n, x in enumerate(own_strips(packed, PACK_ROWS)):
            c_ref[n, out, :] = x
        m0_wide[out, :], m1_wide[out, :] = column_messages(packed, even, PACK_ROWS)
        total = (gravity * 0.5 * time_step) * e_in[out, :]
        for k in range(LEVELS):
            h = density_half(t_in[k, out, :], s_in[k, out, :])
            at = total + h
            p[k, here, :] = at
            total = at + h
            wet = w_in[k, out, :].astype(F32)
            both = jnp.dot(wet.astype(BF16), neighbours, preferred_element_type=F32)
            m_east, m_west = wet * both[:, :LANES], wet * both[:, LANES:]
            me[k, out, :] = m_east
            for x, y, gradient in ((u_in, xu, product(at, difference)), (v_in, xv, 0.0)):
                q = x[k, out, :]
                spread = m_east * (east(q) - q) + m_west * (west(q) - q)
                y[k, out, :] = q - gradient + (time_step * viscosity) * spread
        for n, x in enumerate((t_in, s_in)):
            for k in range(LEVELS):
                both = product(x[k, out, :], matrix)
                face[n * LEVELS + k, out, :] = both[:, :LANES]
                slope[n * LEVELS + k, out, :] = both[:, LANES:]
        return 0

    lax.fori_loop(0, rows // PACK_ROWS, step, 0)
    half, _ = message_rows(rows)
    for wide, out in ((m0_wide, m0_ref), (m1_wide, m1_ref)):
        main, rest = compact(wide[...], rows)
        out[:half, :] = main
        out[half:, :] = rest


def column_pack(fields, surface):
    rows = surface.shape[0]
    tall = rows + BASE + 16
    big = pltpu.VMEM((LEVELS, tall, LANES), F32)
    return pl.pallas_call(
        column_pack_kernel,
        in_specs=[VMEM] * 6,
        out_specs=[VMEM] * 16,
        out_shape=[big] * 5
        + [pltpu.VMEM((tall, LANES), F32), big]
        + [pltpu.VMEM((FIELDS + 1, rows + 8, LANES), F32)]
        + [pltpu.VMEM((message_rows(rows)[1], LANES), F32)] * 2
        + [pltpu.VMEM((2 * LEVELS, rows, LANES), F32)] * 2
        + [pltpu.VMEM((LEVELS, rows, LANES), F32)] * 3
        + [pltpu.VMEM((2 * LANES, LEVELS * LANES), BF16)],
        scratch_shapes=[pltpu.VMEM((rows, LANES), F32)] * 2,
        compiler_params=params(16),
        cost_estimate=pl.CostEstimate(flops=10_000_000, bytes_accessed=6_000_000, transcendentals=0),
        name="column_pack",
    )(*fields, surface)


def ghost_kernel(a_ref, b_ref, *refs):
    t, s, u, v, w, e, p, c_ref, m0_ref, m1_ref, g_ref = refs[10:]
    rows = c_ref.shape[1] - 8
    even = is_even("lat")
    fold = lax.axis_index("lat") == lax.axis_size("lat") - 1
    mirror = LANES - 1 - lanes()
    flat = g_ref.reshape(PLANES * 8, LANES)
    g_ref[...] = jnp.zeros_like(g_ref)

    southmost = lax.axis_index("lat") == 0

    def both(start):
        a, b = a_ref[pl.ds(start, 8), :], b_ref[pl.ds(start, 8), :]
        return jnp.where(even, a, b), jnp.where(southmost, 0.0, jnp.where(even, b, a))

    for f in range(FIELDS):
        sign = -1.0 if f in (2, 3) else 1.0
        north0, south0 = both(f * LEVELS)
        north1, south1 = both((FIELDS + f) * LEVELS)
        first = jnp.where(fold, sign * gather(north1, mirror), north0)
        second = jnp.where(fold, sign * gather(north0, mirror), north1)
        for row, value in ((0, first), (1, second), (6, south0), (7, south1)):
            flat[pl.ds(f * LEVELS * 8 + row, LEVELS, stride=8), :] = value
    north, south = both(2 * FIELDS * LEVELS)
    turned = gather(north, mirror)
    row = lax.broadcasted_iota(jnp.int32, (8, LANES), 0)
    folded = jnp.where(row == 0, pltpu.roll(turned, 1, 0), pltpu.roll(turned, 3, 0))
    g_ref[PLANES - 1] = jnp.where(row < 2, jnp.where(fold, folded, north), jnp.where(row >= 6, south, 0.0))
    packed = pack_columns(lambda q: g_ref[q], 8)
    last = pl.ds(rows, 8)
    for n, x in enumerate(own_strips(packed, 8)):
        c_ref[n, last, :] = x
    half, _ = message_rows(rows)
    lane = lanes()
    first = REST_LANES * (rows // REST_ROWS)
    for out, message in zip((m0_ref, m1_ref), column_messages(packed, is_even("lon"), 8)):
        place = pl.ds(rows - half, 8)
        out[place, :] = jnp.where(lane < 64, out[place, :], pltpu.roll(message, 64, 1))
        place = pl.ds(half, 8)
        moved = pltpu.roll(message, (first - 64) % LANES, 1)
        out[place, :] = jnp.where((lane >= first) & (lane < first + REST_LANES), moved, out[place, :])
    for side in (pl.ds(BASE - 8, 8), pl.ds(BASE + rows, 8)):
        for f, x in enumerate((t, s, u, v, w)):
            for k in range(LEVELS):
                x[k, side, :] = g_ref[f * LEVELS + k]
        e[side, :] = g_ref[PLANES - 1]
        pressure(side, t, s, e, p)


def ghosts(a, b, arrays):
    return pl.pallas_call(
        ghost_kernel,
        in_specs=[VMEM] * 12,
        out_specs=[VMEM] * 10,
        out_shape=[pltpu.VMEM(x.shape, F32) for x in arrays],
        scratch_shapes=[pltpu.VMEM((PLANES, 8, LANES), F32)],
        input_output_aliases={n + 2: n for n in range(10)},
        compiler_params=params(8),
        name="ghosts",
    )(a, b, *arrays)


def density_half(t, s):
    k = 0.5 * press_scale * 0.5 * time_step
    return t * (-0.2 * k + (-0.05 * k) * t + (0.02 * k) * s) + (0.8 * k) * s


def pressure(here, t, s, e, p):
    total = (gravity * 0.5 * time_step) * e[here, :]
    for k in range(LEVELS):
        h = density_half(t[k, here, :], s[k, here, :])
        at = total + h
        p[k, here, :] = at
        total = at + h


def coriolis_rows(start, count, rows):
    total = rows * lax.axis_size("lat")
    row = lax.broadcasted_iota(jnp.int32, (count, LANES), 0) + (start - BASE + lax.axis_index("lat") * rows)
    row = jnp.minimum(row, total - 1).astype(F32)
    return (time_step * coriolis_max) * (2.0 * (row + 0.5) / total - 1.0)


def velocity_trial(k, r, n, spin, u, v, w, p, m_east, m_north):
    here, up, down = pl.ds(r, n), pl.ds(r + 1, n), pl.ds(r - 1, n)
    wet = w[k, here, :]
    me = wet * east(wet)
    mw = wet * west(wet)
    mn = wet * w[k, up, :]
    ms = wet * w[k, down, :]
    if m_east is not None:
        m_east[k, here, :] = me
    m_north[k, here, :] = mn

    def lap(q_ref, q):
        return me * (east(q) - q) + mw * (west(q) - q) + (mn * (q_ref[k, up, :] - q) + ms * (q_ref[k, down, :] - q))

    un, vn = u[k, here, :], v[k, here, :]
    pc = p[k, here, :]
    u_trial = un + (spin * vn - (east(pc) - west(pc)) + (time_step * viscosity) * lap(u, un))
    v_trial = vn + ((time_step * viscosity) * lap(v, vn) - spin * un - (p[k, up, :] - p[k, down, :]))
    return wet, u_trial, v_trial


def velocity_trial_y(k, r, n, spin, u, v, w, p, xu, xv, m_north):
    here, up, down = pl.ds(r, n), pl.ds(r + 1, n), pl.ds(r - 1, n)
    out = pl.ds(r - BASE, n)
    wet = w[k, here, :]
    mn = wet * w[k, up, :]
    ms = wet * w[k, down, :]
    m_north[k, here, :] = mn

    def lap(q_ref, q):
        return (time_step * viscosity) * (mn * (q_ref[k, up, :] - q) + ms * (q_ref[k, down, :] - q))

    un, vn = u[k, here, :], v[k, here, :]
    u_trial = xu[k, out, :] + (spin * vn + lap(u, un))
    v_trial = xv[k, out, :] + (lap(v, vn) - spin * un - (p[k, up, :] - p[k, down, :]))
    return wet, u_trial, v_trial


def damping(u, v):
    return 1.0 / (1.0 + drag_coef * jnp.sqrt(u * u + v * v))


FLUX = time_step * 0.5 / 12.0
HEIGHT = time_step / LEVELS * 0.5 / FLUX


def flux(q0, q1, qm, qp, tr, md):
    return tr * (7.0 * (q0 + q1) - (qm + qp)) - md * (q1 - q0)


def north_flux(k, r, n, vel, m_north, tracers, g_refs):
    here, up = pl.ds(r, n), pl.ds(r + 1, n)
    mn = m_north[k, here, :]
    tr = (FLUX * mn) * (vel[k, here, :] + vel[k, up, :])
    md = (time_step * diffusivity) * mn
    out = []
    for q, g in zip(tracers, g_refs):
        gy = flux(q[k, here, :], q[k, up, :], q[k, pl.ds(r - 1, n), :], q[k, pl.ds(r + 2, n), :], tr, md)
        g[k, here, :] = gy
        out.append(gy)
    return tr, out


def east_flux(k, r, n, u_next, m_east, tracers):
    here = pl.ds(r, n)
    me = m_east[k, here, :]
    tr = (FLUX * me) * (u_next + east(u_next))
    md = (time_step * diffusivity) * me
    out = []
    for q_ref in tracers:
        q = q_ref[k, here, :]
        out.append((q, flux(q, east(q), west(q), pltpu.roll(q, LANES - 2, 1), tr, md)))
    return tr, out


def new_velocities(u, v, w, p, xu, xv, u_out, v_out, vel, mn):
    rows = u_out.shape[1]

    def velocities(r, n, store):
        here = pl.ds(r, n)
        spin = coriolis_rows(r, n, rows)
        if store:
            trial = [velocity_trial_y(k, r, n, spin, u, v, w, p, xu, xv, mn) for k in range(LEVELS)]
        else:
            trial = [velocity_trial(k, r, n, spin, u, v, w, p, None, mn) for k in range(LEVELS)]
        at_floor = [trial[k][0] > (trial[k + 1][0] if k + 1 < LEVELS else 0.0) for k in range(LEVELS)]
        u_floor, v_floor = trial[0][1], trial[0][2]
        for k in range(1, LEVELS):
            u_floor = jnp.where(at_floor[k], trial[k][1], u_floor)
            v_floor = jnp.where(at_floor[k], trial[k][2], v_floor)
        damp = damping(u_floor, v_floor)
        for k in range(LEVELS):
            factor = jnp.where(at_floor[k], damp, trial[k][0])
            v_next = factor * trial[k][2]
            vel[k, here, :] = v_next
            if store:
                out = pl.ds(r - BASE, n)
                u_out[k, out, :] = factor * trial[k][1]
                v_out[k, out, :] = v_next

    velocities(BASE - 8, 8, False)
    velocities(BASE + rows, 8, False)
    for n in range(MAIN_BLOCKS):
        velocities(BASE + n * (rows // MAIN_BLOCKS), rows // MAIN_BLOCKS, True)


def new_tracers(t, s, w, e, face, slope, me, u_out, vel, mn, t_out, s_out, h_out, gt, gs, hy):
    rows = h_out.shape[0]
    total = 0.0
    for k in range(LEVELS):
        total = total + north_flux(k, BASE - 8, 8, vel, mn, (t, s), (gt, gs))[0]
    hy[pl.ds(BASE - 8, 8), :] = total
    here, down = pl.ds(BASE, rows), pl.ds(BASE - 1, rows)
    total_x = total_y = 0.0
    for k in range(LEVELS):
        tr_y, (gy_t, gy_s) = north_flux(k, BASE, rows, vel, mn, (t, s), (gt, gs))
        u_next = u_out[k]
        mask = me[k]
        tr_x = (FLUX * mask) * (u_next + east(u_next))
        md = (time_step * diffusivity) * mask
        gx_t = tr_x * face[k] - md * slope[k]
        gx_s = tr_x * face[LEVELS + k] - md * slope[LEVELS + k]
        total_x, total_y = total_x + tr_x, total_y + tr_y
        wet = w[k, here, :]
        t_out[k] = wet * (t[k, here, :] - (gx_t - west(gx_t) + (gy_t - gt[k, down, :])))
        s_out[k] = wet * (s[k, here, :] - (gx_s - west(gx_s) + (gy_s - gs[k, down, :])))
    hy[here, :] = total_y
    h_out[...] = e[here, :] - HEIGHT * (total_x - west(total_x) + (total_y - hy[down, :]))


def waits_for_seam():
    return (lax.axis_index("lon") == 0) & (lax.axis_index("lat") < lax.axis_size("lat") - 1)


def early_kernel(*refs):
    ins, outs = refs[:6], refs[8:]

    @pl.when(waits_for_seam())
    def _():
        new_velocities(*ins, *outs)


def early(u, v, w, p, xu, xv, message):
    wide, high = pltpu.VMEM(xu.shape, F32), pltpu.VMEM(u.shape, F32)
    return pl.pallas_call(
        early_kernel,
        in_specs=[VMEM] * 7,
        out_specs=[VMEM] * 5,
        out_shape=[pltpu.VMEM(message.shape, F32), wide, wide, high, high],
        input_output_aliases={6: 0},
        compiler_params=params(16),
        name="early",
    )(u, v, w, p, xu, xv, message)


def main_kernel(*refs):
    (t, s, u, v, w, e, p, face, slope, xu, xv, me), outs, scratch = refs[:12], refs[16:23], refs[23:]
    u_out, v_out, vel, mn, t_out, s_out, h_out = outs

    @pl.when(jnp.logical_not(waits_for_seam()))
    def _():
        new_velocities(u, v, w, p, xu, xv, u_out, v_out, vel, mn)

    new_tracers(t, s, w, e, face, slope, me, u_out, vel, mn, t_out, s_out, h_out, *scratch)


def main(arrays, velocities):
    rows, tall = arrays[-1].shape[1], arrays[0].shape[1]
    wide, high = pltpu.VMEM((LEVELS, rows, LANES), F32), pltpu.VMEM((LEVELS, tall, LANES), F32)
    return pl.pallas_call(
        main_kernel,
        in_specs=[VMEM] * 16,
        out_specs=[VMEM] * 7,
        out_shape=[wide, wide, high, high, wide, wide, pltpu.VMEM((rows, LANES), F32)],
        scratch_shapes=[high, high, pltpu.VMEM((tall, LANES), F32)],
        input_output_aliases={n + 12: n for n in range(4)},
        compiler_params=params(16),
        cost_estimate=pl.CostEstimate(flops=40_000_000, bytes_accessed=8_000_000, transcendentals=100_000),
        name="main",
    )(*arrays, *velocities)


def last_kernel(c_ref, m0_ref, m1_ref, place, mt, ms, mu, mv, mh, t_hbm, s_hbm, u_hbm, v_hbm, h_hbm,
                t, s, u, v, w, e, p, me, mn, un, vel, gt, gs, hy, st, ss, sh, ot, os, ou, ov, oh, sems):
    rows = oh.shape[0]
    even = is_even("lon")

    def complete():
        n = rows + 8
        half, _ = message_rows(rows)
        m0, m1 = m0_ref[...], m1_ref[...]
        m_east, m_west = jnp.where(even, m0, m1), jnp.where(even, m1, m0)
        low = jnp.where(lanes(half) < 64, m_east[:half, :], pltpu.roll(m_west[:half, :], 64, 1))
        high = jnp.where(lanes(n - half) < 64, pltpu.roll(m_east[: n - half, :], 64, 1), m_west[: n - half, :])
        four = jnp.concatenate([low, high], axis=0)
        rest_east, rest_west = m_east[half:, :], pltpu.roll(m_west[half:, :], 64, 1)

        def slots(count):
            _, level, slot = strip_layout(count)
            west_side = jnp.where(slot >= 6, 64, 0)
            return level, (slot >= 4) & (slot < 8), west_side + jnp.where(slot % 2 == 1, 1, 0)

        level, ghost, at = slots(n)
        here = pl.ds(BASE, n)
        for f, x in enumerate((t, s, u, v)):
            x[0, here, :] = jnp.where(ghost, gather(four, 2 * LEVELS * f + 2 * level + at), c_ref[f])
        for g in range(-(-n // REST_ROWS)):
            count = min(REST_ROWS, n - g * REST_ROWS)
            level, ghost, at = slots(count)
            lane = lanes(count)
            mine = (lane >= REST_LANES * g) & (lane < REST_LANES * (g + 1))
            rest = jnp.where(mine, rest_east[:count, :], rest_west[:count, :])
            src, dst = pl.ds(g * REST_ROWS, count), pl.ds(BASE + g * REST_ROWS, count)
            index = (REST_LANES * g + 2 * level + at) % LANES
            w[0, dst, :] = jnp.where(ghost, gather(rest, index), c_ref[FIELDS - 1, src, :])
            index = (REST_LANES * g + 2 * LEVELS + at) % LANES
            e[dst, :] = jnp.where(ghost, gather(rest, index), c_ref[FIELDS, src, :])

    def strip_pressure(r, n):
        here = pl.ds(r, n)
        lane = lanes(n)
        h = density_half(t[0, here, :], s[0, here, :])
        total = h
        for step in (16, 32, 64):
            total = total + jnp.where(lane >= step, pltpu.roll(total, step, 1), 0.0)
        p[0, here, :] = (gravity * 0.5 * time_step) * e[here, :] + (2.0 * total - h)

    def strip_velocities(r, n):
        here = pl.ds(r, n)
        lane = lanes(n)
        wet, u_trial, v_trial = velocity_trial(0, r, n, coriolis_rows(r, n, rows), u, v, w, p, me, mn)
        below = jnp.where(lane < LANES - 16, pltpu.roll(wet, LANES - 16, 1), 0.0)
        factor = jnp.where(wet > below, damping(u_trial, v_trial), wet)
        un[0, here, :] = factor * u_trial
        vel[0, here, :] = factor * v_trial

    def on_edge(n):
        lane = lanes(n)
        return (lane < 2) | (lane >= LANES - 2)

    def placed(strip, levels=LEVELS):
        out = []
        high, middle, _ = split(strip)
        top = jnp.concatenate([high, middle], axis=1)
        for k in range(0, levels, 2):
            both = jnp.dot(top, place[:, k * LANES : (k + 2) * LANES], preferred_element_type=F32)
            out += [both[:, :LANES], both[:, LANES:]]
        return out

    def strip_tracers(r, n):
        here, down = pl.ds(r, n), pl.ds(r - 1, n)
        out = pl.ds(r - BASE, n)
        tr_y, (gy_t, gy_s) = north_flux(0, r, n, vel, mn, (t, s), (gt, gs))
        tr_x, ((tc, gx_t), (sc, gx_s)) = east_flux(0, r, n, un[0, here, :], me, (t, s))
        wet = w[0, here, :]
        hy[here, :] = tr_y
        st[out, :] = wet * (tc - (gx_t - west(gx_t) + (gy_t - gt[0, down, :])))
        ss[out, :] = wet * (sc - (gx_s - west(gx_s) + (gy_s - gs[0, down, :])))
        inflow = tr_x - west(tr_x) + (tr_y - hy[down, :])
        for step in (16, 32, 64):
            inflow = inflow + pltpu.roll(inflow, step, 1)
        sh[out, :] = e[here, :] - HEIGHT * inflow

    copies = []

    def send(x, y):
        copies.append(pltpu.make_async_copy(x, y, sems.at[len(copies)]))
        copies[-1].start()

    complete()
    strip_pressure(BASE, rows + 8)
    for x in (t, s, u, v, w, p):
        x[0, pl.ds(BASE - 8, 8), :] = x[0, pl.ds(BASE + rows, 8), :]
    e[pl.ds(BASE - 8, 8), :] = e[pl.ds(BASE + rows, 8), :]
    strip_velocities(BASE - 8, rows + 16)
    hy[pl.ds(BASE - 8, 8), :] = north_flux(0, BASE - 8, 8, vel, mn, (t, s), (gt, gs))[0]
    whole = pl.ds(BASE, rows)

    def merge(out, strip, inner):
        edge = on_edge(strip.shape[0])
        for k, value in enumerate(placed(strip)):
            out[k] = jnp.where(edge, value, inner[k])

    merge(ou, un[0, whole, :], mu)
    send(ou, u_hbm)
    merge(ov, vel[0, whole, :], mv)
    send(ov, v_hbm)
    strip_tracers(BASE, rows)
    merge(ot, st[...], mt)
    send(ot, t_hbm)
    oh[...] = jnp.where(on_edge(rows), placed(sh[...], 2)[0], mh[...])
    send(oh, h_hbm)
    merge(os, ss[...], ms)
    send(os, s_hbm)
    for x in copies:
        x.wait()


def last(c, m0, m1, place, outs):
    rows = outs[4].shape[0]
    tall = rows + BASE + 16
    big = pltpu.VMEM((1, tall, LANES), F32)
    flat = pltpu.VMEM((tall, LANES), F32)
    short = pltpu.VMEM((rows, LANES), F32)
    out3 = jax.ShapeDtypeStruct((LEVELS, rows, LANES), F32)
    wide = pltpu.VMEM((LEVELS, rows, LANES), F32)
    return pl.pallas_call(
        last_kernel,
        in_specs=[VMEM] * 9,
        out_specs=[HBM] * 5,
        out_shape=[out3] * 4 + [jax.ShapeDtypeStruct((rows, LANES), F32)],
        scratch_shapes=[big] * 5
        + [flat]
        + [big] * 7
        + [flat]
        + [short] * 3
        + [wide] * 4
        + [short, pltpu.SemaphoreType.DMA((5,))],
        compiler_params=params(24),
        name="last",
    )(c, m0, m1, place, *outs)


def swaps():
    lon, lat = lax.axis_size("lon"), lax.axis_size("lat")

    def device(o, a):
        return o % lon * lat + a

    lat_first, lat_second, lon_first, lon_second = [], [], [], []
    for o in range(lon):
        for a in range(lat):
            lat_first.append((device(o, a), device(o, a ^ 1)))
            if a == lat - 1:
                lat_second.append((device(o, a), device(lon - 1 - o, a)))
            elif a > 0:
                lat_second.append((device(o, a), device(o, a + 1 if a % 2 else a - 1)))
            else:
                lat_second.append((device(o, a), device(o ^ 1, a)))
            lon_first.append((device(o, a), device(o ^ 1, a)))
            lon_second.append((device(o, a), device(o + 1 if o % 2 else o - 1, a)))
    return lat_first, lat_second, lon_first, lon_second


def on_device(
    heat_anomaly,
    saltiness_anomaly,
    zonal_current,
    meridional_current,
    free_elevation,
    ocean_indicator,
    floor_layer_index,
):
    lat_first, lat_second, lon_first, lon_second = swaps()
    send = functools.partial(lax.ppermute, axis_name=("lon", "lat"))
    fields = (heat_anomaly, saltiness_anomaly, zonal_current, meridional_current, ocean_indicator)
    a, b = row_pack(fields, free_elevation)
    a = send(a, perm=lat_first)
    b = send(b, perm=lat_second)
    *arrays, face, slope, xu, xv, me, place = column_pack(fields, free_elevation)
    t, s, u, v, w, e, p, c, m0, m1 = ghosts(a, b, arrays)
    m0 = send(m0, perm=lon_first)
    m1, *velocities = early(u, v, w, p, xu, xv, m1)
    m1 = send(m1, perm=lon_second)
    u_next, v_next, _, _, *tracers = main((t, s, u, v, w, e, p, face, slope, xu, xv, me), velocities)
    return tuple(last(c, m0, m1, place, (*tracers[:2], u_next, v_next, tracers[2])))


def solution(mesh):
    return jax.shard_map(
        on_device,
        mesh=mesh,
        in_specs=(
            P(None, "lat", "lon"),
            P(None, "lat", "lon"),
            P(None, "lat", "lon"),
            P(None, "lat", "lon"),
            P("lat", "lon"),
            P(None, "lat", "lon"),
            P("lat", "lon"),
        ),
        out_specs=(
            P(None, "lat", "lon"),
            P(None, "lat", "lon"),
            P(None, "lat", "lon"),
            P(None, "lat", "lon"),
            P("lat", "lon"),
        ),
        check_vma=False,
    )
```

```python
import functools

import jax
import jax.numpy as jnp
from jax import lax
from jax.experimental import pallas as pl
from jax.experimental.pallas import tpu as pltpu
from jax.sharding import PartitionSpec as P

F32 = jnp.float32
BF16 = jnp.bfloat16
LEVELS = 8
LANES = 128
FIELDS = 5
PLANES = FIELDS * LEVELS + 1
ROW_MSG = 2 * FIELDS * LEVELS + 8
BASE = 16
PACK_ROWS = 96
REST_ROWS = 32
REST_LANES = 2 * LEVELS + 2
MAIN_BLOCKS = 1
TRACER_BLOCKS = 2

time_step = 0.2
viscosity = 0.5
diffusivity = 0.3
press_scale = 0.25
gravity = 1.0
drag_coef = 1.0
coriolis_max = 0.5

HBM = pl.BlockSpec(memory_space=pltpu.HBM)
VMEM = pl.BlockSpec(memory_space=pltpu.VMEM)


def params(mib):
    return pltpu.CompilerParams(vmem_limit_bytes=int(mib * 1024 * 1024))


def lanes(rows=8):
    return lax.broadcasted_iota(jnp.int32, (rows, LANES), 1)


def east(x):
    return pltpu.roll(x, LANES - 1, 1)


def west(x):
    return pltpu.roll(x, 1, 1)


def gather(x, index):
    return jnp.take_along_axis(x, index, axis=1)


def strip_layout(rows):
    lane = lanes(rows)
    return lane, lane // 16, lane % 16


def own_strips(packed, rows):
    _, level, slot = strip_layout(rows)
    own = jnp.where(slot < 4, slot, jnp.where((slot >= 8) & (slot < 12), slot - 4, 0))
    out = [gather(packed[f // 2], 8 * level + own + 64 * (f % 2)) for f in range(FIELDS)]
    return out + [gather(packed[2], own + 64)]


def split(x):
    high = x.astype(BF16)
    rest = x - high.astype(F32)
    middle = rest.astype(BF16)
    return high, middle, (rest - middle.astype(F32)).astype(BF16)


def face_matrix():
    step = lane_step()
    face = jnp.where(step < 2, 7.0, jnp.where((step == 2) | (step == LANES - 1), -1.0, 0.0))
    slope = jnp.where(step == 1, 1.0, jnp.where(step == 0, -1.0, 0.0))
    return jnp.concatenate([face, slope], axis=1).astype(BF16)


def product(x, matrix):
    return sum(jnp.dot(part, matrix, preferred_element_type=F32) for part in split(x)[::-1])


def lane_step():
    row = lax.broadcasted_iota(jnp.int32, (LANES, LANES), 0)
    return lax.rem(row - lax.broadcasted_iota(jnp.int32, (LANES, LANES), 1) + LANES, LANES)


def neighbour_matrix():
    step = lane_step()
    return jnp.concatenate([jnp.where(step == 1, 1.0, 0.0), jnp.where(step == LANES - 1, 1.0, 0.0)], axis=1).astype(BF16)


def difference_matrix():
    step = lane_step()
    return jnp.where(step == 1, 1.0, jnp.where(step == LANES - 1, -1.0, 0.0)).astype(BF16)


def place_matrix(level):
    lane, row = (lax.broadcasted_iota(jnp.int32, (LANES, LANES), n) for n in (1, 0))
    slot = jnp.where(lane < 2, lane + 8, jnp.where(lane >= LANES - 2, lane - (LANES - 4), -LANES))
    return jnp.where(row == 16 * level + slot, 1.0, 0.0).astype(BF16)


def is_even(axis):
    return lax.rem(lax.axis_index(axis), 2) == 0


def row_pack_kernel(*refs):
    ins, (a_ref, b_ref), tiles, sems = refs[:6], refs[6:8], refs[8:20], refs[20]
    rows = ins[5].shape[0]
    copies = []
    for n, x in enumerate(ins):
        for side, start in enumerate((0, rows - 8)):
            src = x.at[:, pl.ds(start, 8), :] if n < FIELDS else x.at[pl.ds(start, 8), :]
            copies.append(pltpu.make_async_copy(src, tiles[2 * n + side], sems.at[2 * n + side]))
            copies[-1].start()
    for x in copies:
        x.wait()
    even = is_even("lat")
    for r in range(2):
        for f in range(FIELDS):
            low, high = tiles[2 * f : 2 * f + 2]
            bottom = low.reshape(LEVELS * 8, LANES)[pl.ds(r, LEVELS, stride=8), :].astype(F32)
            top = high.reshape(LEVELS * 8, LANES)[pl.ds(6 + r, LEVELS, stride=8), :].astype(F32)
            place = pl.ds((r * FIELDS + f) * LEVELS, LEVELS)
            a_ref[place, :] = jnp.where(even, top, bottom)
            b_ref[place, :] = jnp.where(even, bottom, top)
    place = pl.ds(2 * FIELDS * LEVELS, 8)
    low, high = tiles[10][...], tiles[11][...]
    a_ref[place, :] = jnp.where(even, high, low)
    b_ref[place, :] = jnp.where(even, low, high)


def row_pack(fields, surface):
    scratch = [pltpu.VMEM((LEVELS, 8, LANES), x.dtype) for x in fields for _ in range(2)]
    scratch += [pltpu.VMEM((8, LANES), F32)] * 2 + [pltpu.SemaphoreType.DMA((12,))]
    return pl.pallas_call(
        row_pack_kernel,
        in_specs=[HBM] * 6,
        out_specs=[VMEM] * 2,
        out_shape=[pltpu.VMEM((ROW_MSG, LANES), F32)] * 2,
        scratch_shapes=scratch,
        compiler_params=params(60),
        name="row_pack",
    )(*fields, surface)


def pack_columns(plane, rows):
    lane = lanes(rows)
    packed = []
    for first in range(0, PLANES, 16):
        group = None
        for p in range(first, min(first + 16, PLANES)):
            q = p - first
            moved = pltpu.roll(plane(p), (8 * q + 4) % LANES, 1)
            group = moved if group is None else jnp.where(lane >= 8 * q, moved, group)
        packed.append(group)
    return packed


def column_messages(packed, even, rows):
    lane = lanes(rows)
    base = 8 * ((lane // 2) % 16) + lane % 2
    messages = []
    for first in (True, False):
        eastern = even if first else jnp.logical_not(even)
        index = base + jnp.where(eastern, 2, 4)
        c0, c1, c2 = [gather(c, index) for c in packed]
        messages.append(jnp.where(lane < 32, c0, jnp.where(lane < 64, c1, c2)))
    return messages


def message_rows(rows):
    half = (rows + 8 + 15) // 16 * 8
    return half, half + REST_ROWS


def compact(message, rows):
    half, _ = message_rows(rows)
    lane = lanes(half)
    second = jnp.concatenate([message[half:rows, :], jnp.zeros((2 * half - rows, LANES), F32)], axis=0)
    main = jnp.where(lane < 64, message[:half, :], pltpu.roll(second, 64, 1))
    lane = lanes(REST_ROWS)
    rest = jnp.zeros((REST_ROWS, LANES), F32)
    for g in range(rows // REST_ROWS):
        part = pltpu.roll(message[g * REST_ROWS : (g + 1) * REST_ROWS, :], (REST_LANES * g - 64) % LANES, 1)
        rest = jnp.where((lane >= REST_LANES * g) & (lane < REST_LANES * (g + 1)), part, rest)
    return main, rest


def column_pack_kernel(t_in, s_in, u_in, v_in, w_in, e_in, t, s, u, v, w, e, p, c_ref, m0_ref, m1_ref, face, slope, xu, xv, me, place, m0_wide, m1_wide):
    rows = e_in.shape[0]
    even = is_even("lon")
    matrix, neighbours, difference = face_matrix(), neighbour_matrix(), difference_matrix()
    for k in range(LEVELS):
        place[:LANES, k * LANES : (k + 1) * LANES] = place_matrix(k)
        place[LANES:, k * LANES : (k + 1) * LANES] = place_matrix(k)

    def step(i, _):
        out = pl.ds(pl.multiple_of(i * PACK_ROWS, 8), PACK_ROWS)
        here = pl.ds(pl.multiple_of(BASE + i * PACK_ROWS, 8), PACK_ROWS)
        for x, y in ((t_in, t), (s_in, s), (u_in, u), (v_in, v), (w_in, w)):
            for k in range(LEVELS):
                y[k, here, :] = x[k, out, :].astype(F32)
        e[here, :] = e_in[out, :]

        def plane(q):
            if q == PLANES - 1:
                return e_in[out, :]
            return (t_in, s_in, u_in, v_in, w_in)[q // LEVELS][q % LEVELS, out, :].astype(F32)

        packed = pack_columns(plane, PACK_ROWS)
        for n, x in enumerate(own_strips(packed, PACK_ROWS)):
            c_ref[n, out, :] = x
        m0_wide[out, :], m1_wide[out, :] = column_messages(packed, even, PACK_ROWS)
        total = (gravity * 0.5 * time_step) * e_in[out, :]
        for k in range(LEVELS):
            h = density_half(t_in[k, out, :], s_in[k, out, :])
            at = total + h
            p[k, here, :] = at
            total = at + h
            wet = w_in[k, out, :].astype(F32)
            both = jnp.dot(wet.astype(BF16), neighbours, preferred_element_type=F32)
            m_east, m_west = wet * both[:, :LANES], wet * both[:, LANES:]
            me[k, out, :] = m_east
            for x, y, gradient in ((u_in, xu, product(at, difference)), (v_in, xv, 0.0)):
                q = x[k, out, :]
                spread = m_east * (east(q) - q) + m_west * (west(q) - q)
                y[k, out, :] = q - gradient + (time_step * viscosity) * spread
        for n, x in enumerate((t_in, s_in)):
            for k in range(LEVELS):
                both = product(x[k, out, :], matrix)
                face[n * LEVELS + k, out, :] = both[:, :LANES]
                slope[n * LEVELS + k, out, :] = both[:, LANES:]
        return 0

    lax.fori_loop(0, rows // PACK_ROWS, step, 0)
    half, _ = message_rows(rows)
    for wide, out in ((m0_wide, m0_ref), (m1_wide, m1_ref)):
        main, rest = compact(wide[...], rows)
        out[:half, :] = main
        out[half:, :] = rest


def column_pack(fields, surface):
    rows = surface.shape[0]
    tall = rows + BASE + 16
    big = pltpu.VMEM((LEVELS, tall, LANES), F32)
    return pl.pallas_call(
        column_pack_kernel,
        in_specs=[VMEM] * 6,
        out_specs=[VMEM] * 16,
        out_shape=[big] * 5
        + [pltpu.VMEM((tall, LANES), F32), big]
        + [pltpu.VMEM((FIELDS + 1, rows + 8, LANES), F32)]
        + [pltpu.VMEM((message_rows(rows)[1], LANES), F32)] * 2
        + [pltpu.VMEM((2 * LEVELS, rows, LANES), F32)] * 2
        + [pltpu.VMEM((LEVELS, rows, LANES), F32)] * 3
        + [pltpu.VMEM((2 * LANES, LEVELS * LANES), BF16)],
        scratch_shapes=[pltpu.VMEM((rows, LANES), F32)] * 2,
        compiler_params=params(16),
        cost_estimate=pl.CostEstimate(flops=10_000_000, bytes_accessed=6_000_000, transcendentals=0),
        name="column_pack",
    )(*fields, surface)


def ghost_kernel(a_ref, b_ref, *refs):
    t, s, u, v, w, e, p, c_ref, m0_ref, m1_ref, g_ref = refs[10:]
    rows = c_ref.shape[1] - 8
    even = is_even("lat")
    fold = lax.axis_index("lat") == lax.axis_size("lat") - 1
    mirror = LANES - 1 - lanes()
    flat = g_ref.reshape(PLANES * 8, LANES)
    g_ref[...] = jnp.zeros_like(g_ref)

    southmost = lax.axis_index("lat") == 0

    def both(start):
        a, b = a_ref[pl.ds(start, 8), :], b_ref[pl.ds(start, 8), :]
        return jnp.where(even, a, b), jnp.where(southmost, 0.0, jnp.where(even, b, a))

    for f in range(FIELDS):
        sign = -1.0 if f in (2, 3) else 1.0
        north0, south0 = both(f * LEVELS)
        north1, south1 = both((FIELDS + f) * LEVELS)
        first = jnp.where(fold, sign * gather(north1, mirror), north0)
        second = jnp.where(fold, sign * gather(north0, mirror), north1)
        for row, value in ((0, first), (1, second), (6, south0), (7, south1)):
            flat[pl.ds(f * LEVELS * 8 + row, LEVELS, stride=8), :] = value
    north, south = both(2 * FIELDS * LEVELS)
    turned = gather(north, mirror)
    row = lax.broadcasted_iota(jnp.int32, (8, LANES), 0)
    folded = jnp.where(row == 0, pltpu.roll(turned, 1, 0), pltpu.roll(turned, 3, 0))
    g_ref[PLANES - 1] = jnp.where(row < 2, jnp.where(fold, folded, north), jnp.where(row >= 6, south, 0.0))
    packed = pack_columns(lambda q: g_ref[q], 8)
    last = pl.ds(rows, 8)
    for n, x in enumerate(own_strips(packed, 8)):
        c_ref[n, last, :] = x
    half, _ = message_rows(rows)
    lane = lanes()
    first = REST_LANES * (rows // REST_ROWS)
    for out, message in zip((m0_ref, m1_ref), column_messages(packed, is_even("lon"), 8)):
        place = pl.ds(rows - half, 8)
        out[place, :] = jnp.where(lane < 64, out[place, :], pltpu.roll(message, 64, 1))
        place = pl.ds(half, 8)
        moved = pltpu.roll(message, (first - 64) % LANES, 1)
        out[place, :] = jnp.where((lane >= first) & (lane < first + REST_LANES), moved, out[place, :])
    for side in (pl.ds(BASE - 8, 8), pl.ds(BASE + rows, 8)):
        for f, x in enumerate((t, s, u, v, w)):
            for k in range(LEVELS):
                x[k, side, :] = g_ref[f * LEVELS + k]
        e[side, :] = g_ref[PLANES - 1]
        pressure(side, t, s, e, p)


def ghosts(a, b, arrays):
    return pl.pallas_call(
        ghost_kernel,
        in_specs=[VMEM] * 12,
        out_specs=[VMEM] * 10,
        out_shape=[pltpu.VMEM(x.shape, F32) for x in arrays],
        scratch_shapes=[pltpu.VMEM((PLANES, 8, LANES), F32)],
        input_output_aliases={n + 2: n for n in range(10)},
        compiler_params=params(8),
        name="ghosts",
    )(a, b, *arrays)


def density_half(t, s):
    k = 0.5 * press_scale * 0.5 * time_step
    return t * (-0.2 * k + (-0.05 * k) * t + (0.02 * k) * s) + (0.8 * k) * s


def pressure(here, t, s, e, p):
    total = (gravity * 0.5 * time_step) * e[here, :]
    for k in range(LEVELS):
        h = density_half(t[k, here, :], s[k, here, :])
        at = total + h
        p[k, here, :] = at
        total = at + h


def coriolis_rows(start, count, rows):
    total = rows * lax.axis_size("lat")
    row = lax.broadcasted_iota(jnp.int32, (count, LANES), 0) + (start - BASE + lax.axis_index("lat") * rows)
    row = jnp.minimum(row, total - 1).astype(F32)
    return (time_step * coriolis_max) * (2.0 * (row + 0.5) / total - 1.0)


def velocity_trial(k, r, n, spin, u, v, w, p, m_east, m_north):
    here, up, down = pl.ds(r, n), pl.ds(r + 1, n), pl.ds(r - 1, n)
    wet = w[k, here, :]
    me = wet * east(wet)
    mw = wet * west(wet)
    mn = wet * w[k, up, :]
    ms = wet * w[k, down, :]
    if m_east is not None:
        m_east[k, here, :] = me
    m_north[k, here, :] = mn

    def lap(q_ref, q):
        return me * (east(q) - q) + mw * (west(q) - q) + (mn * (q_ref[k, up, :] - q) + ms * (q_ref[k, down, :] - q))

    un, vn = u[k, here, :], v[k, here, :]
    pc = p[k, here, :]
    u_trial = un + (spin * vn - (east(pc) - west(pc)) + (time_step * viscosity) * lap(u, un))
    v_trial = vn + ((time_step * viscosity) * lap(v, vn) - spin * un - (p[k, up, :] - p[k, down, :]))
    return wet, u_trial, v_trial


def velocity_trial_y(k, r, n, spin, u, v, w, p, xu, xv, m_north):
    here, up, down = pl.ds(r, n), pl.ds(r + 1, n), pl.ds(r - 1, n)
    out = pl.ds(r - BASE, n)
    wet = w[k, here, :]
    mn = wet * w[k, up, :]
    ms = wet * w[k, down, :]
    m_north[k, here, :] = mn

    def lap(q_ref, q):
        return (time_step * viscosity) * (mn * (q_ref[k, up, :] - q) + ms * (q_ref[k, down, :] - q))

    un, vn = u[k, here, :], v[k, here, :]
    u_trial = xu[k, out, :] + (spin * vn + lap(u, un))
    v_trial = xv[k, out, :] + (lap(v, vn) - spin * un - (p[k, up, :] - p[k, down, :]))
    return wet, u_trial, v_trial


def damping(u, v):
    return 1.0 / (1.0 + drag_coef * jnp.sqrt(u * u + v * v))


FLUX = time_step * 0.5 / 12.0
HEIGHT = time_step / LEVELS * 0.5 / FLUX


def flux(q0, q1, qm, qp, tr, md):
    return tr * (7.0 * (q0 + q1) - (qm + qp)) - md * (q1 - q0)


def north_flux(k, r, n, vel, m_north, tracers, g_refs):
    here, up = pl.ds(r, n), pl.ds(r + 1, n)
    mn = m_north[k, here, :]
    tr = (FLUX * mn) * (vel[k, here, :] + vel[k, up, :])
    md = (time_step * diffusivity) * mn
    out = []
    for q, g in zip(tracers, g_refs):
        gy = flux(q[k, here, :], q[k, up, :], q[k, pl.ds(r - 1, n), :], q[k, pl.ds(r + 2, n), :], tr, md)
        g[k, here, :] = gy
        out.append(gy)
    return tr, out


def east_flux(k, r, n, u_next, m_east, tracers):
    here = pl.ds(r, n)
    me = m_east[k, here, :]
    tr = (FLUX * me) * (u_next + east(u_next))
    md = (time_step * diffusivity) * me
    out = []
    for q_ref in tracers:
        q = q_ref[k, here, :]
        out.append((q, flux(q, east(q), west(q), pltpu.roll(q, LANES - 2, 1), tr, md)))
    return tr, out


def new_velocities(u, v, w, p, xu, xv, u_out, v_out, vel, mn):
    rows = u_out.shape[1]

    def velocities(r, n, store):
        here = pl.ds(r, n)
        spin = coriolis_rows(r, n, rows)
        if store:
            trial = [velocity_trial_y(k, r, n, spin, u, v, w, p, xu, xv, mn) for k in range(LEVELS)]
        else:
            trial = [velocity_trial(k, r, n, spin, u, v, w, p, None, mn) for k in range(LEVELS)]
        at_floor = [trial[k][0] > (trial[k + 1][0] if k + 1 < LEVELS else 0.0) for k in range(LEVELS)]
        u_floor, v_floor = trial[0][1], trial[0][2]
        for k in range(1, LEVELS):
            u_floor = jnp.where(at_floor[k], trial[k][1], u_floor)
            v_floor = jnp.where(at_floor[k], trial[k][2], v_floor)
        damp = damping(u_floor, v_floor)
        for k in range(LEVELS):
            factor = jnp.where(at_floor[k], damp, trial[k][0])
            v_next = factor * trial[k][2]
            vel[k, here, :] = v_next
            if store:
                out = pl.ds(r - BASE, n)
                u_out[k, out, :] = factor * trial[k][1]
                v_out[k, out, :] = v_next

    velocities(BASE - 8, 8, False)
    velocities(BASE + rows, 8, False)
    for n in range(MAIN_BLOCKS):
        velocities(BASE + n * (rows // MAIN_BLOCKS), rows // MAIN_BLOCKS, True)


def new_tracers(t, s, w, e, face, slope, me, u_out, vel, mn, t_out, s_out, h_out, gt, gs, hy):
    rows = h_out.shape[0]
    total = 0.0
    for k in range(LEVELS):
        total = total + north_flux(k, BASE - 8, 8, vel, mn, (t, s), (gt, gs))[0]
    hy[pl.ds(BASE - 8, 8), :] = total
    n = rows // TRACER_BLOCKS
    for first in range(0, rows, n):
        r, out = BASE + first, pl.ds(first, n)
        here, down = pl.ds(r, n), pl.ds(r - 1, n)
        total_x = total_y = 0.0
        for k in range(LEVELS):
            tr_y, (gy_t, gy_s) = north_flux(k, r, n, vel, mn, (t, s), (gt, gs))
            u_next = u_out[k, out, :]
            mask = me[k, out, :]
            tr_x = (FLUX * mask) * (u_next + east(u_next))
            md = (time_step * diffusivity) * mask
            gx_t = tr_x * face[k, out, :] - md * slope[k, out, :]
            gx_s = tr_x * face[LEVELS + k, out, :] - md * slope[LEVELS + k, out, :]
            total_x, total_y = total_x + tr_x, total_y + tr_y
            wet = w[k, here, :]
            t_out[k, out, :] = wet * (t[k, here, :] - (gx_t - west(gx_t) + (gy_t - gt[k, down, :])))
            s_out[k, out, :] = wet * (s[k, here, :] - (gx_s - west(gx_s) + (gy_s - gs[k, down, :])))
        hy[here, :] = total_y
        h_out[out, :] = e[here, :] - HEIGHT * (total_x - west(total_x) + (total_y - hy[down, :]))


def waits_for_seam():
    return (lax.axis_index("lon") == 0) & (lax.axis_index("lat") < lax.axis_size("lat") - 1)


def early_kernel(*refs):
    ins, outs = refs[:6], refs[8:]

    @pl.when(waits_for_seam())
    def _():
        new_velocities(*ins, *outs)


def early(u, v, w, p, xu, xv, message):
    wide, high = pltpu.VMEM(xu.shape, F32), pltpu.VMEM(u.shape, F32)
    return pl.pallas_call(
        early_kernel,
        in_specs=[VMEM] * 7,
        out_specs=[VMEM] * 5,
        out_shape=[pltpu.VMEM(message.shape, F32), wide, wide, high, high],
        input_output_aliases={6: 0},
        compiler_params=params(16),
        name="early",
    )(u, v, w, p, xu, xv, message)


def main_kernel(*refs):
    (t, s, u, v, w, e, p, face, slope, xu, xv, me), outs, scratch = refs[:12], refs[16:23], refs[23:]
    u_out, v_out, vel, mn, t_out, s_out, h_out = outs

    @pl.when(jnp.logical_not(waits_for_seam()))
    def _():
        new_velocities(u, v, w, p, xu, xv, u_out, v_out, vel, mn)

    new_tracers(t, s, w, e, face, slope, me, u_out, vel, mn, t_out, s_out, h_out, *scratch)


def main(arrays, velocities):
    rows, tall = arrays[-1].shape[1], arrays[0].shape[1]
    wide, high = pltpu.VMEM((LEVELS, rows, LANES), F32), pltpu.VMEM((LEVELS, tall, LANES), F32)
    return pl.pallas_call(
        main_kernel,
        in_specs=[VMEM] * 16,
        out_specs=[VMEM] * 7,
        out_shape=[wide, wide, high, high, wide, wide, pltpu.VMEM((rows, LANES), F32)],
        scratch_shapes=[high, high, pltpu.VMEM((tall, LANES), F32)],
        input_output_aliases={n + 12: n for n in range(4)},
        compiler_params=params(16),
        cost_estimate=pl.CostEstimate(flops=40_000_000, bytes_accessed=8_000_000, transcendentals=100_000),
        name="main",
    )(*arrays, *velocities)


def last_kernel(c_ref, m0_ref, m1_ref, place, mt, ms, mu, mv, mh, t_hbm, s_hbm, u_hbm, v_hbm, h_hbm,
                t, s, u, v, w, e, p, me, mn, un, vel, gt, gs, hy, st, ss, sh, ot, os, ou, ov, oh, sems):
    rows = oh.shape[0]
    even = is_even("lon")

    def complete():
        n = rows + 8
        half, _ = message_rows(rows)
        m0, m1 = m0_ref[...], m1_ref[...]
        m_east, m_west = jnp.where(even, m0, m1), jnp.where(even, m1, m0)
        low = jnp.where(lanes(half) < 64, m_east[:half, :], pltpu.roll(m_west[:half, :], 64, 1))
        high = jnp.where(lanes(n - half) < 64, pltpu.roll(m_east[: n - half, :], 64, 1), m_west[: n - half, :])
        four = jnp.concatenate([low, high], axis=0)
        rest_east, rest_west = m_east[half:, :], pltpu.roll(m_west[half:, :], 64, 1)

        def slots(count):
            _, level, slot = strip_layout(count)
            west_side = jnp.where(slot >= 6, 64, 0)
            return level, (slot >= 4) & (slot < 8), west_side + jnp.where(slot % 2 == 1, 1, 0)

        level, ghost, at = slots(n)
        here = pl.ds(BASE, n)
        for f, x in enumerate((t, s, u, v)):
            x[0, here, :] = jnp.where(ghost, gather(four, 2 * LEVELS * f + 2 * level + at), c_ref[f])
        for g in range(-(-n // REST_ROWS)):
            count = min(REST_ROWS, n - g * REST_ROWS)
            level, ghost, at = slots(count)
            lane = lanes(count)
            mine = (lane >= REST_LANES * g) & (lane < REST_LANES * (g + 1))
            rest = jnp.where(mine, rest_east[:count, :], rest_west[:count, :])
            src, dst = pl.ds(g * REST_ROWS, count), pl.ds(BASE + g * REST_ROWS, count)
            index = (REST_LANES * g + 2 * level + at) % LANES
            w[0, dst, :] = jnp.where(ghost, gather(rest, index), c_ref[FIELDS - 1, src, :])
            index = (REST_LANES * g + 2 * LEVELS + at) % LANES
            e[dst, :] = jnp.where(ghost, gather(rest, index), c_ref[FIELDS, src, :])

    def strip_pressure(r, n):
        here = pl.ds(r, n)
        lane = lanes(n)
        h = density_half(t[0, here, :], s[0, here, :])
        total = h
        for step in (16, 32, 64):
            total = total + jnp.where(lane >= step, pltpu.roll(total, step, 1), 0.0)
        p[0, here, :] = (gravity * 0.5 * time_step) * e[here, :] + (2.0 * total - h)

    def strip_velocities(r, n):
        here = pl.ds(r, n)
        lane = lanes(n)
        wet, u_trial, v_trial = velocity_trial(0, r, n, coriolis_rows(r, n, rows), u, v, w, p, me, mn)
        below = jnp.where(lane < LANES - 16, pltpu.roll(wet, LANES - 16, 1), 0.0)
        factor = jnp.where(wet > below, damping(u_trial, v_trial), wet)
        un[0, here, :] = factor * u_trial
        vel[0, here, :] = factor * v_trial

    def on_edge(n):
        lane = lanes(n)
        return (lane < 2) | (lane >= LANES - 2)

    def placed(strip, levels=LEVELS):
        out = []
        high, middle, _ = split(strip)
        top = jnp.concatenate([high, middle], axis=1)
        for k in range(0, levels, 2):
            both = jnp.dot(top, place[:, k * LANES : (k + 2) * LANES], preferred_element_type=F32)
            out += [both[:, :LANES], both[:, LANES:]]
        return out

    def strip_tracers(r, n):
        here, down = pl.ds(r, n), pl.ds(r - 1, n)
        out = pl.ds(r - BASE, n)
        tr_y, (gy_t, gy_s) = north_flux(0, r, n, vel, mn, (t, s), (gt, gs))
        tr_x, ((tc, gx_t), (sc, gx_s)) = east_flux(0, r, n, un[0, here, :], me, (t, s))
        wet = w[0, here, :]
        hy[here, :] = tr_y
        st[out, :] = wet * (tc - (gx_t - west(gx_t) + (gy_t - gt[0, down, :])))
        ss[out, :] = wet * (sc - (gx_s - west(gx_s) + (gy_s - gs[0, down, :])))
        inflow = tr_x - west(tr_x) + (tr_y - hy[down, :])
        for step in (16, 32, 64):
            inflow = inflow + pltpu.roll(inflow, step, 1)
        sh[out, :] = e[here, :] - HEIGHT * inflow

    copies = []

    def send(x, y):
        copies.append(pltpu.make_async_copy(x, y, sems.at[len(copies)]))
        copies[-1].start()

    complete()
    strip_pressure(BASE, rows + 8)
    for x in (t, s, u, v, w, p):
        x[0, pl.ds(BASE - 8, 8), :] = x[0, pl.ds(BASE + rows, 8), :]
    e[pl.ds(BASE - 8, 8), :] = e[pl.ds(BASE + rows, 8), :]
    strip_velocities(BASE - 8, rows + 16)
    hy[pl.ds(BASE - 8, 8), :] = north_flux(0, BASE - 8, 8, vel, mn, (t, s), (gt, gs))[0]
    whole = pl.ds(BASE, rows)

    def merge(out, strip, inner):
        edge = on_edge(strip.shape[0])
        for k, value in enumerate(placed(strip)):
            out[k] = jnp.where(edge, value, inner[k])

    merge(ou, un[0, whole, :], mu)
    send(ou, u_hbm)
    merge(ov, vel[0, whole, :], mv)
    send(ov, v_hbm)
    strip_tracers(BASE, rows)
    merge(ot, st[...], mt)
    send(ot, t_hbm)
    oh[...] = jnp.where(on_edge(rows), placed(sh[...], 2)[0], mh[...])
    send(oh, h_hbm)
    merge(os, ss[...], ms)
    send(os, s_hbm)
    for x in copies:
        x.wait()


def last(c, m0, m1, place, outs):
    rows = outs[4].shape[0]
    tall = rows + BASE + 16
    big = pltpu.VMEM((1, tall, LANES), F32)
    flat = pltpu.VMEM((tall, LANES), F32)
    short = pltpu.VMEM((rows, LANES), F32)
    out3 = jax.ShapeDtypeStruct((LEVELS, rows, LANES), F32)
    wide = pltpu.VMEM((LEVELS, rows, LANES), F32)
    return pl.pallas_call(
        last_kernel,
        in_specs=[VMEM] * 9,
        out_specs=[HBM] * 5,
        out_shape=[out3] * 4 + [jax.ShapeDtypeStruct((rows, LANES), F32)],
        scratch_shapes=[big] * 5
        + [flat]
        + [big] * 7
        + [flat]
        + [short] * 3
        + [wide] * 4
        + [short, pltpu.SemaphoreType.DMA((5,))],
        compiler_params=params(24),
        name="last",
    )(c, m0, m1, place, *outs)


def swaps():
    lon, lat = lax.axis_size("lon"), lax.axis_size("lat")

    def device(o, a):
        return o % lon * lat + a

    lat_first, lat_second, lon_first, lon_second = [], [], [], []
    for o in range(lon):
        for a in range(lat):
            lat_first.append((device(o, a), device(o, a ^ 1)))
            if a == lat - 1:
                lat_second.append((device(o, a), device(lon - 1 - o, a)))
            elif a > 0:
                lat_second.append((device(o, a), device(o, a + 1 if a % 2 else a - 1)))
            else:
                lat_second.append((device(o, a), device(o ^ 1, a)))
            lon_first.append((device(o, a), device(o ^ 1, a)))
            lon_second.append((device(o, a), device(o + 1 if o % 2 else o - 1, a)))
    return lat_first, lat_second, lon_first, lon_second


def on_device(
    heat_anomaly,
    saltiness_anomaly,
    zonal_current,
    meridional_current,
    free_elevation,
    ocean_indicator,
    floor_layer_index,
):
    lat_first, lat_second, lon_first, lon_second = swaps()
    send = functools.partial(lax.ppermute, axis_name=("lon", "lat"))
    fields = (heat_anomaly, saltiness_anomaly, zonal_current, meridional_current, ocean_indicator)
    a, b = row_pack(fields, free_elevation)
    a = send(a, perm=lat_first)
    b = send(b, perm=lat_second)
    *arrays, face, slope, xu, xv, me, place = column_pack(fields, free_elevation)
    t, s, u, v, w, e, p, c, m0, m1 = ghosts(a, b, arrays)
    m0 = send(m0, perm=lon_first)
    m1, *velocities = early(u, v, w, p, xu, xv, m1)
    m1 = send(m1, perm=lon_second)
    u_next, v_next, _, _, *tracers = main((t, s, u, v, w, e, p, face, slope, xu, xv, me), velocities)
    return tuple(last(c, m0, m1, place, (*tracers[:2], u_next, v_next, tracers[2])))


def solution(mesh):
    return jax.shard_map(
        on_device,
        mesh=mesh,
        in_specs=(
            P(None, "lat", "lon"),
            P(None, "lat", "lon"),
            P(None, "lat", "lon"),
            P(None, "lat", "lon"),
            P("lat", "lon"),
            P(None, "lat", "lon"),
            P("lat", "lon"),
        ),
        out_specs=(
            P(None, "lat", "lon"),
            P(None, "lat", "lon"),
            P(None, "lat", "lon"),
            P(None, "lat", "lon"),
            P("lat", "lon"),
        ),
        check_vma=False,
    )
```

```python
import functools

import jax
import jax.numpy as jnp
from jax import lax
from jax.experimental import pallas as pl
from jax.experimental.pallas import tpu as pltpu
from jax.sharding import PartitionSpec as P

F32 = jnp.float32
BF16 = jnp.bfloat16
LEVELS = 8
LANES = 128
FIELDS = 5
PLANES = FIELDS * LEVELS + 1
ROW_MSG = 2 * FIELDS * LEVELS + 8
BASE = 16
PACK_ROWS = 96
REST_ROWS = 32
REST_LANES = 2 * LEVELS + 2
MAIN_BLOCKS = 1

time_step = 0.2
viscosity = 0.5
diffusivity = 0.3
press_scale = 0.25
gravity = 1.0
drag_coef = 1.0
coriolis_max = 0.5

HBM = pl.BlockSpec(memory_space=pltpu.HBM)
VMEM = pl.BlockSpec(memory_space=pltpu.VMEM)


def params(mib):
    return pltpu.CompilerParams(vmem_limit_bytes=int(mib * 1024 * 1024))


def lanes(rows=8):
    return lax.broadcasted_iota(jnp.int32, (rows, LANES), 1)


def east(x):
    return pltpu.roll(x, LANES - 1, 1)


def west(x):
    return pltpu.roll(x, 1, 1)


def gather(x, index):
    return jnp.take_along_axis(x, index, axis=1)


def strip_layout(rows):
    lane = lanes(rows)
    return lane, lane // 16, lane % 16


def own_strips(packed, rows):
    _, level, slot = strip_layout(rows)
    own = jnp.where(slot < 4, slot, jnp.where((slot >= 8) & (slot < 12), slot - 4, 0))
    out = [gather(packed[f // 2], 8 * level + own + 64 * (f % 2)) for f in range(FIELDS)]
    return out + [gather(packed[2], own + 64)]


def split(x):
    high = x.astype(BF16)
    rest = x - high.astype(F32)
    middle = rest.astype(BF16)
    return high, middle, (rest - middle.astype(F32)).astype(BF16)


def face_matrix():
    step = lane_step()
    face = jnp.where(step < 2, 7.0, jnp.where((step == 2) | (step == LANES - 1), -1.0, 0.0))
    slope = jnp.where(step == 1, 1.0, jnp.where(step == 0, -1.0, 0.0))
    return jnp.concatenate([face, slope], axis=1).astype(BF16)


def product(x, matrix):
    return sum(jnp.dot(part, matrix, preferred_element_type=F32) for part in split(x)[::-1])


def lane_step():
    row = lax.broadcasted_iota(jnp.int32, (LANES, LANES), 0)
    return lax.rem(row - lax.broadcasted_iota(jnp.int32, (LANES, LANES), 1) + LANES, LANES)


def neighbour_matrix():
    step = lane_step()
    return jnp.concatenate([jnp.where(step == 1, 1.0, 0.0), jnp.where(step == LANES - 1, 1.0, 0.0)], axis=1).astype(BF16)


def difference_matrix():
    step = lane_step()
    return jnp.where(step == 1, 1.0, jnp.where(step == LANES - 1, -1.0, 0.0)).astype(BF16)


def place_matrix(level):
    lane, row = (lax.broadcasted_iota(jnp.int32, (LANES, LANES), n) for n in (1, 0))
    slot = jnp.where(lane < 2, lane + 8, jnp.where(lane >= LANES - 2, lane - (LANES - 4), -LANES))
    return jnp.where(row == 16 * level + slot, 1.0, 0.0).astype(BF16)


def is_even(axis):
    return lax.rem(lax.axis_index(axis), 2) == 0


def row_pack_kernel(*refs):
    ins, (a_ref, b_ref), tiles, sems = refs[:6], refs[6:8], refs[8:20], refs[20]
    rows = ins[5].shape[0]
    copies = []
    for n, x in enumerate(ins):
        for side, start in enumerate((0, rows - 8)):
            src = x.at[:, pl.ds(start, 8), :] if n < FIELDS else x.at[pl.ds(start, 8), :]
            copies.append(pltpu.make_async_copy(src, tiles[2 * n + side], sems.at[2 * n + side]))
            copies[-1].start()
    for x in copies:
        x.wait()
    even = is_even("lat")
    for r in range(2):
        for f in range(FIELDS):
            low, high = tiles[2 * f : 2 * f + 2]
            bottom = low.reshape(LEVELS * 8, LANES)[pl.ds(r, LEVELS, stride=8), :].astype(F32)
            top = high.reshape(LEVELS * 8, LANES)[pl.ds(6 + r, LEVELS, stride=8), :].astype(F32)
            place = pl.ds((r * FIELDS + f) * LEVELS, LEVELS)
            a_ref[place, :] = jnp.where(even, top, bottom)
            b_ref[place, :] = jnp.where(even, bottom, top)
    place = pl.ds(2 * FIELDS * LEVELS, 8)
    low, high = tiles[10][...], tiles[11][...]
    a_ref[place, :] = jnp.where(even, high, low)
    b_ref[place, :] = jnp.where(even, low, high)


def row_pack(fields, surface):
    scratch = [pltpu.VMEM((LEVELS, 8, LANES), x.dtype) for x in fields for _ in range(2)]
    scratch += [pltpu.VMEM((8, LANES), F32)] * 2 + [pltpu.SemaphoreType.DMA((12,))]
    return pl.pallas_call(
        row_pack_kernel,
        in_specs=[HBM] * 6,
        out_specs=[VMEM] * 2,
        out_shape=[pltpu.VMEM((ROW_MSG, LANES), F32)] * 2,
        scratch_shapes=scratch,
        compiler_params=params(60),
        name="row_pack",
    )(*fields, surface)


def pack_columns(plane, rows):
    lane = lanes(rows)
    packed = []
    for first in range(0, PLANES, 16):
        group = None
        for p in range(first, min(first + 16, PLANES)):
            q = p - first
            moved = pltpu.roll(plane(p), (8 * q + 4) % LANES, 1)
            group = moved if group is None else jnp.where(lane >= 8 * q, moved, group)
        packed.append(group)
    return packed


def column_messages(packed, even, rows):
    lane = lanes(rows)
    base = 8 * ((lane // 2) % 16) + lane % 2
    messages = []
    for first in (True, False):
        eastern = even if first else jnp.logical_not(even)
        index = base + jnp.where(eastern, 2, 4)
        c0, c1, c2 = [gather(c, index) for c in packed]
        messages.append(jnp.where(lane < 32, c0, jnp.where(lane < 64, c1, c2)))
    return messages


def message_rows(rows):
    half = (rows + 8 + 15) // 16 * 8
    return half, half + REST_ROWS


def compact(message, rows):
    half, _ = message_rows(rows)
    lane = lanes(half)
    second = jnp.concatenate([message[half:rows, :], jnp.zeros((2 * half - rows, LANES), F32)], axis=0)
    main = jnp.where(lane < 64, message[:half, :], pltpu.roll(second, 64, 1))
    lane = lanes(REST_ROWS)
    rest = jnp.zeros((REST_ROWS, LANES), F32)
    for g in range(rows // REST_ROWS):
        part = pltpu.roll(message[g * REST_ROWS : (g + 1) * REST_ROWS, :], (REST_LANES * g - 64) % LANES, 1)
        rest = jnp.where((lane >= REST_LANES * g) & (lane < REST_LANES * (g + 1)), part, rest)
    return main, rest


def column_pack_kernel(t_in, s_in, u_in, v_in, w_in, e_in, t, s, u, v, w, e, p, c_ref, m0_ref, m1_ref, face, slope, xu, xv, me, place, m0_wide, m1_wide):
    rows = e_in.shape[0]
    even = is_even("lon")
    matrix, neighbours, difference = face_matrix(), neighbour_matrix(), difference_matrix()
    for k in range(LEVELS):
        place[:LANES, k * LANES : (k + 1) * LANES] = place_matrix(k)
        place[LANES:, k * LANES : (k + 1) * LANES] = place_matrix(k)

    def step(i, _):
        out = pl.ds(pl.multiple_of(i * PACK_ROWS, 8), PACK_ROWS)
        here = pl.ds(pl.multiple_of(BASE + i * PACK_ROWS, 8), PACK_ROWS)
        for x, y in ((t_in, t), (s_in, s), (u_in, u), (v_in, v), (w_in, w)):
            for k in range(LEVELS):
                y[k, here, :] = x[k, out, :].astype(F32)
        e[here, :] = e_in[out, :]

        def plane(q):
            if q == PLANES - 1:
                return e_in[out, :]
            return (t_in, s_in, u_in, v_in, w_in)[q // LEVELS][q % LEVELS, out, :].astype(F32)

        packed = pack_columns(plane, PACK_ROWS)
        for n, x in enumerate(own_strips(packed, PACK_ROWS)):
            c_ref[n, out, :] = x
        m0_wide[out, :], m1_wide[out, :] = column_messages(packed, even, PACK_ROWS)
        total = (gravity * 0.5 * time_step) * e_in[out, :]
        for k in range(LEVELS):
            h = density_half(t_in[k, out, :], s_in[k, out, :])
            at = total + h
            p[k, here, :] = at
            total = at + h
            wet = w_in[k, out, :].astype(F32)
            both = jnp.dot(wet.astype(BF16), neighbours, preferred_element_type=F32)
            m_east, m_west = wet * both[:, :LANES], wet * both[:, LANES:]
            me[k, out, :] = m_east
            for x, y, gradient in ((u_in, xu, product(at, difference)), (v_in, xv, 0.0)):
                q = x[k, out, :]
                spread = m_east * (east(q) - q) + m_west * (west(q) - q)
                y[k, out, :] = q - gradient + (time_step * viscosity) * spread
        for n, x in enumerate((t_in, s_in)):
            for k in range(LEVELS):
                both = product(x[k, out, :], matrix)
                face[n * LEVELS + k, out, :] = both[:, :LANES]
                slope[n * LEVELS + k, out, :] = both[:, LANES:]
        return 0

    lax.fori_loop(0, rows // PACK_ROWS, step, 0)
    half, _ = message_rows(rows)
    for wide, out in ((m0_wide, m0_ref), (m1_wide, m1_ref)):
        main, rest = compact(wide[...], rows)
        out[:half, :] = main
        out[half:, :] = rest


def column_pack(fields, surface):
    rows = surface.shape[0]
    tall = rows + BASE + 16
    big = pltpu.VMEM((LEVELS, tall, LANES), F32)
    return pl.pallas_call(
        column_pack_kernel,
        in_specs=[VMEM] * 6,
        out_specs=[VMEM] * 16,
        out_shape=[big] * 5
        + [pltpu.VMEM((tall, LANES), F32), big]
        + [pltpu.VMEM((FIELDS + 1, rows + 8, LANES), F32)]
        + [pltpu.VMEM((message_rows(rows)[1], LANES), F32)] * 2
        + [pltpu.VMEM((2 * LEVELS, rows, LANES), F32)] * 2
        + [pltpu.VMEM((LEVELS, rows, LANES), F32)] * 3
        + [pltpu.VMEM((2 * LANES, LEVELS * LANES), BF16)],
        scratch_shapes=[pltpu.VMEM((rows, LANES), F32)] * 2,
        compiler_params=params(16),
        cost_estimate=pl.CostEstimate(flops=10_000_000, bytes_accessed=6_000_000, transcendentals=0),
        name="column_pack",
    )(*fields, surface)


def ghost_kernel(a_ref, b_ref, *refs):
    t, s, u, v, w, e, p, c_ref, m0_ref, m1_ref, g_ref = refs[10:]
    rows = c_ref.shape[1] - 8
    even = is_even("lat")
    fold = lax.axis_index("lat") == lax.axis_size("lat") - 1
    mirror = LANES - 1 - lanes()
    flat = g_ref.reshape(PLANES * 8, LANES)
    g_ref[...] = jnp.zeros_like(g_ref)

    southmost = lax.axis_index("lat") == 0

    def both(start):
        a, b = a_ref[pl.ds(start, 8), :], b_ref[pl.ds(start, 8), :]
        return jnp.where(even, a, b), jnp.where(southmost, 0.0, jnp.where(even, b, a))

    for f in range(FIELDS):
        sign = -1.0 if f in (2, 3) else 1.0
        north0, south0 = both(f * LEVELS)
        north1, south1 = both((FIELDS + f) * LEVELS)
        first = jnp.where(fold, sign * gather(north1, mirror), north0)
        second = jnp.where(fold, sign * gather(north0, mirror), north1)
        for row, value in ((0, first), (1, second), (6, south0), (7, south1)):
            flat[pl.ds(f * LEVELS * 8 + row, LEVELS, stride=8), :] = value
    north, south = both(2 * FIELDS * LEVELS)
    turned = gather(north, mirror)
    row = lax.broadcasted_iota(jnp.int32, (8, LANES), 0)
    folded = jnp.where(row == 0, pltpu.roll(turned, 1, 0), pltpu.roll(turned, 3, 0))
    g_ref[PLANES - 1] = jnp.where(row < 2, jnp.where(fold, folded, north), jnp.where(row >= 6, south, 0.0))
    packed = pack_columns(lambda q: g_ref[q], 8)
    last = pl.ds(rows, 8)
    for n, x in enumerate(own_strips(packed, 8)):
        c_ref[n, last, :] = x
    half, _ = message_rows(rows)
    lane = lanes()
    first = REST_LANES * (rows // REST_ROWS)
    for out, message in zip((m0_ref, m1_ref), column_messages(packed, is_even("lon"), 8)):
        place = pl.ds(rows - half, 8)
        out[place, :] = jnp.where(lane < 64, out[place, :], pltpu.roll(message, 64, 1))
        place = pl.ds(half, 8)
        moved = pltpu.roll(message, (first - 64) % LANES, 1)
        out[place, :] = jnp.where((lane >= first) & (lane < first + REST_LANES), moved, out[place, :])
    for side in (pl.ds(BASE - 8, 8), pl.ds(BASE + rows, 8)):
        for f, x in enumerate((t, s, u, v, w)):
            for k in range(LEVELS):
                x[k, side, :] = g_ref[f * LEVELS + k]
        e[side, :] = g_ref[PLANES - 1]
        pressure(side, t, s, e, p)


def ghosts(a, b, arrays):
    return pl.pallas_call(
        ghost_kernel,
        in_specs=[VMEM] * 12,
        out_specs=[VMEM] * 10,
        out_shape=[pltpu.VMEM(x.shape, F32) for x in arrays],
        scratch_shapes=[pltpu.VMEM((PLANES, 8, LANES), F32)],
        input_output_aliases={n + 2: n for n in range(10)},
        compiler_params=params(8),
        name="ghosts",
    )(a, b, *arrays)


def density_half(t, s):
    k = 0.5 * press_scale * 0.5 * time_step
    return t * (-0.2 * k + (-0.05 * k) * t + (0.02 * k) * s) + (0.8 * k) * s


def pressure(here, t, s, e, p):
    total = (gravity * 0.5 * time_step) * e[here, :]
    for k in range(LEVELS):
        h = density_half(t[k, here, :], s[k, here, :])
        at = total + h
        p[k, here, :] = at
        total = at + h


def coriolis_rows(start, count, rows):
    total = rows * lax.axis_size("lat")
    row = lax.broadcasted_iota(jnp.int32, (count, LANES), 0) + (start - BASE + lax.axis_index("lat") * rows)
    row = jnp.minimum(row, total - 1).astype(F32)
    return (time_step * coriolis_max) * (2.0 * (row + 0.5) / total - 1.0)


def velocity_trial(k, r, n, spin, u, v, w, p, m_east, m_north):
    here, up, down = pl.ds(r, n), pl.ds(r + 1, n), pl.ds(r - 1, n)
    wet = w[k, here, :]
    me = wet * east(wet)
    mw = wet * west(wet)
    mn = wet * w[k, up, :]
    ms = wet * w[k, down, :]
    if m_east is not None:
        m_east[k, here, :] = me
    m_north[k, here, :] = mn

    def lap(q_ref, q):
        return me * (east(q) - q) + mw * (west(q) - q) + (mn * (q_ref[k, up, :] - q) + ms * (q_ref[k, down, :] - q))

    un, vn = u[k, here, :], v[k, here, :]
    pc = p[k, here, :]
    u_trial = un + (spin * vn - (east(pc) - west(pc)) + (time_step * viscosity) * lap(u, un))
    v_trial = vn + ((time_step * viscosity) * lap(v, vn) - spin * un - (p[k, up, :] - p[k, down, :]))
    return wet, u_trial, v_trial


def velocity_trial_y(k, r, n, spin, u, v, w, p, xu, xv, m_north):
    here, up, down = pl.ds(r, n), pl.ds(r + 1, n), pl.ds(r - 1, n)
    out = pl.ds(r - BASE, n)
    wet = w[k, here, :]
    mn = wet * w[k, up, :]
    ms = wet * w[k, down, :]
    m_north[k, here, :] = mn

    def lap(q_ref, q):
        return (time_step * viscosity) * (mn * (q_ref[k, up, :] - q) + ms * (q_ref[k, down, :] - q))

    un, vn = u[k, here, :], v[k, here, :]
    u_trial = xu[k, out, :] + (spin * vn + lap(u, un))
    v_trial = xv[k, out, :] + (lap(v, vn) - spin * un - (p[k, up, :] - p[k, down, :]))
    return wet, u_trial, v_trial


def damping(u, v):
    return 1.0 / (1.0 + drag_coef * jnp.sqrt(u * u + v * v))


FLUX = time_step * 0.5 / 12.0
HEIGHT = time_step / LEVELS * 0.5 / FLUX


def flux(q0, q1, qm, qp, tr, md):
    return tr * (7.0 * (q0 + q1) - (qm + qp)) - md * (q1 - q0)


def north_flux(k, r, n, vel, m_north, tracers, g_refs):
    here, up = pl.ds(r, n), pl.ds(r + 1, n)
    mn = m_north[k, here, :]
    tr = (FLUX * mn) * (vel[k, here, :] + vel[k, up, :])
    md = (time_step * diffusivity) * mn
    out = []
    for q, g in zip(tracers, g_refs):
        gy = flux(q[k, here, :], q[k, up, :], q[k, pl.ds(r - 1, n), :], q[k, pl.ds(r + 2, n), :], tr, md)
        g[k, here, :] = gy
        out.append(gy)
    return tr, out


def east_flux(k, r, n, u_next, m_east, tracers):
    here = pl.ds(r, n)
    me = m_east[k, here, :]
    tr = (FLUX * me) * (u_next + east(u_next))
    md = (time_step * diffusivity) * me
    out = []
    for q_ref in tracers:
        q = q_ref[k, here, :]
        out.append((q, flux(q, east(q), west(q), pltpu.roll(q, LANES - 2, 1), tr, md)))
    return tr, out


def new_velocities(u, v, w, p, xu, xv, u_out, v_out, vel, mn):
    rows = u_out.shape[1]

    def velocities(r, n, store):
        here = pl.ds(r, n)
        spin = coriolis_rows(r, n, rows)
        if store:
            trial = [velocity_trial_y(k, r, n, spin, u, v, w, p, xu, xv, mn) for k in range(LEVELS)]
        else:
            trial = [velocity_trial(k, r, n, spin, u, v, w, p, None, mn) for k in range(LEVELS)]
        at_floor = [trial[k][0] > (trial[k + 1][0] if k + 1 < LEVELS else 0.0) for k in range(LEVELS)]
        u_floor, v_floor = trial[0][1], trial[0][2]
        for k in range(1, LEVELS):
            u_floor = jnp.where(at_floor[k], trial[k][1], u_floor)
            v_floor = jnp.where(at_floor[k], trial[k][2], v_floor)
        damp = damping(u_floor, v_floor)
        for k in range(LEVELS):
            factor = jnp.where(at_floor[k], damp, trial[k][0])
            v_next = factor * trial[k][2]
            vel[k, here, :] = v_next
            if store:
                out = pl.ds(r - BASE, n)
                u_out[k, out, :] = factor * trial[k][1]
                v_out[k, out, :] = v_next

    velocities(BASE - 8, 8, False)
    velocities(BASE + rows, 8, False)
    for n in range(MAIN_BLOCKS):
        velocities(BASE + n * (rows // MAIN_BLOCKS), rows // MAIN_BLOCKS, True)


def new_tracers(t, s, w, e, face, slope, me, u_out, vel, mn, t_out, s_out, h_out, gt, gs, hy):
    rows = h_out.shape[0]
    total = 0.0
    for k in range(LEVELS):
        total = total + north_flux(k, BASE - 8, 8, vel, mn, (t, s), (gt, gs))[0]
    hy[pl.ds(BASE - 8, 8), :] = total
    here, down = pl.ds(BASE, rows), pl.ds(BASE - 1, rows)
    total_x = total_y = 0.0
    for k in range(LEVELS):
        tr_y, (gy_t, gy_s) = north_flux(k, BASE, rows, vel, mn, (t, s), (gt, gs))
        u_next = u_out[k]
        mask = me[k]
        tr_x = (FLUX * mask) * (u_next + east(u_next))
        md = (time_step * diffusivity) * mask
        gx_t = tr_x * face[k] - md * slope[k]
        gx_s = tr_x * face[LEVELS + k] - md * slope[LEVELS + k]
        total_x, total_y = total_x + tr_x, total_y + tr_y
        wet = w[k, here, :]
        t_out[k] = wet * (t[k, here, :] - (gx_t - west(gx_t) + (gy_t - gt[k, down, :])))
        s_out[k] = wet * (s[k, here, :] - (gx_s - west(gx_s) + (gy_s - gs[k, down, :])))
    hy[here, :] = total_y
    h_out[...] = e[here, :] - HEIGHT * (total_x - west(total_x) + (total_y - hy[down, :]))


def waits_for_seam():
    return (lax.axis_index("lon") == 0) & (lax.axis_index("lat") < lax.axis_size("lat") - 1)


def early_kernel(*refs):
    ins, outs = refs[:6], refs[8:]

    @pl.when(waits_for_seam())
    def _():
        new_velocities(*ins, *outs)


def early(u, v, w, p, xu, xv, message):
    wide, high = pltpu.VMEM(xu.shape, F32), pltpu.VMEM(u.shape, F32)
    return pl.pallas_call(
        early_kernel,
        in_specs=[VMEM] * 7,
        out_specs=[VMEM] * 5,
        out_shape=[pltpu.VMEM(message.shape, F32), wide, wide, high, high],
        input_output_aliases={6: 0},
        compiler_params=params(16),
        name="early",
    )(u, v, w, p, xu, xv, message)


def main_kernel(*refs):
    (t, s, u, v, w, e, p, face, slope, xu, xv, me), outs, scratch = refs[:12], refs[16:23], refs[23:]
    u_out, v_out, vel, mn, t_out, s_out, h_out = outs

    @pl.when(jnp.logical_not(waits_for_seam()))
    def _():
        new_velocities(u, v, w, p, xu, xv, u_out, v_out, vel, mn)

    new_tracers(t, s, w, e, face, slope, me, u_out, vel, mn, t_out, s_out, h_out, *scratch)


def main(arrays, velocities):
    rows, tall = arrays[-1].shape[1], arrays[0].shape[1]
    wide, high = pltpu.VMEM((LEVELS, rows, LANES), F32), pltpu.VMEM((LEVELS, tall, LANES), F32)
    return pl.pallas_call(
        main_kernel,
        in_specs=[VMEM] * 16,
        out_specs=[VMEM] * 7,
        out_shape=[wide, wide, high, high, wide, wide, pltpu.VMEM((rows, LANES), F32)],
        scratch_shapes=[high, high, pltpu.VMEM((tall, LANES), F32)],
        input_output_aliases={n + 12: n for n in range(4)},
        compiler_params=params(16),
        cost_estimate=pl.CostEstimate(flops=40_000_000, bytes_accessed=8_000_000, transcendentals=100_000),
        name="main",
    )(*arrays, *velocities)


def last_kernel(c_ref, m0_ref, m1_ref, place, mt, ms, mu, mv, mh, t_hbm, s_hbm, u_hbm, v_hbm, h_hbm,
                t, s, u, v, w, e, p, me, mn, un, vel, gt, gs, hy, st, ss, sh, ot, os, ou, ov, oh, sems):
    rows = oh.shape[0]
    even = is_even("lon")

    def complete():
        n = rows + 8
        half, _ = message_rows(rows)
        m0, m1 = m0_ref[...], m1_ref[...]
        m_east, m_west = jnp.where(even, m0, m1), jnp.where(even, m1, m0)
        low = jnp.where(lanes(half) < 64, m_east[:half, :], pltpu.roll(m_west[:half, :], 64, 1))
        high = jnp.where(lanes(n - half) < 64, pltpu.roll(m_east[: n - half, :], 64, 1), m_west[: n - half, :])
        four = jnp.concatenate([low, high], axis=0)
        rest_east, rest_west = m_east[half:, :], pltpu.roll(m_west[half:, :], 64, 1)

        def slots(count):
            _, level, slot = strip_layout(count)
            west_side = jnp.where(slot >= 6, 64, 0)
            return level, (slot >= 4) & (slot < 8), west_side + jnp.where(slot % 2 == 1, 1, 0)

        level, ghost, at = slots(n)
        here = pl.ds(BASE, n)
        for f, x in enumerate((t, s, u, v)):
            x[0, here, :] = jnp.where(ghost, gather(four, 2 * LEVELS * f + 2 * level + at), c_ref[f])
        for g in range(-(-n // REST_ROWS)):
            count = min(REST_ROWS, n - g * REST_ROWS)
            level, ghost, at = slots(count)
            lane = lanes(count)
            mine = (lane >= REST_LANES * g) & (lane < REST_LANES * (g + 1))
            rest = jnp.where(mine, rest_east[:count, :], rest_west[:count, :])
            src, dst = pl.ds(g * REST_ROWS, count), pl.ds(BASE + g * REST_ROWS, count)
            index = (REST_LANES * g + 2 * level + at) % LANES
            w[0, dst, :] = jnp.where(ghost, gather(rest, index), c_ref[FIELDS - 1, src, :])
            index = (REST_LANES * g + 2 * LEVELS + at) % LANES
            e[dst, :] = jnp.where(ghost, gather(rest, index), c_ref[FIELDS, src, :])

    def strip_pressure(r, n):
        here = pl.ds(r, n)
        lane = lanes(n)
        h = density_half(t[0, here, :], s[0, here, :])
        total = h
        for step in (16, 32, 64):
            total = total + jnp.where(lane >= step, pltpu.roll(total, step, 1), 0.0)
        p[0, here, :] = (gravity * 0.5 * time_step) * e[here, :] + (2.0 * total - h)

    def strip_velocities(r, n):
        here = pl.ds(r, n)
        lane = lanes(n)
        wet, u_trial, v_trial = velocity_trial(0, r, n, coriolis_rows(r, n, rows), u, v, w, p, me, mn)
        below = jnp.where(lane < LANES - 16, pltpu.roll(wet, LANES - 16, 1), 0.0)
        factor = jnp.where(wet > below, damping(u_trial, v_trial), wet)
        un[0, here, :] = factor * u_trial
        vel[0, here, :] = factor * v_trial

    def on_edge(n):
        lane = lanes(n)
        return (lane < 2) | (lane >= LANES - 2)

    def placed(strip, levels=LEVELS):
        out = []
        high, middle, _ = split(strip)
        top = jnp.concatenate([high, middle], axis=1)
        for k in range(0, levels, 2):
            both = jnp.dot(top, place[:, k * LANES : (k + 2) * LANES], preferred_element_type=F32)
            out += [both[:, :LANES], both[:, LANES:]]
        return out

    def strip_tracers(r, n):
        here, down = pl.ds(r, n), pl.ds(r - 1, n)
        out = pl.ds(r - BASE, n)
        tr_y, (gy_t, gy_s) = north_flux(0, r, n, vel, mn, (t, s), (gt, gs))
        tr_x, ((tc, gx_t), (sc, gx_s)) = east_flux(0, r, n, un[0, here, :], me, (t, s))
        wet = w[0, here, :]
        hy[here, :] = tr_y
        st[out, :] = wet * (tc - (gx_t - west(gx_t) + (gy_t - gt[0, down, :])))
        ss[out, :] = wet * (sc - (gx_s - west(gx_s) + (gy_s - gs[0, down, :])))
        inflow = tr_x - west(tr_x) + (tr_y - hy[down, :])
        for step in (16, 32, 64):
            inflow = inflow + pltpu.roll(inflow, step, 1)
        sh[out, :] = e[here, :] - HEIGHT * inflow

    copies = []

    def send(x, y):
        copies.append(pltpu.make_async_copy(x, y, sems.at[len(copies)]))
        copies[-1].start()

    complete()
    strip_pressure(BASE, rows + 8)
    for x in (t, s, u, v, w, p):
        x[0, pl.ds(BASE - 8, 8), :] = x[0, pl.ds(BASE + rows, 8), :]
    e[pl.ds(BASE - 8, 8), :] = e[pl.ds(BASE + rows, 8), :]
    strip_velocities(BASE - 8, rows + 16)
    hy[pl.ds(BASE - 8, 8), :] = north_flux(0, BASE - 8, 8, vel, mn, (t, s), (gt, gs))[0]
    whole = pl.ds(BASE, rows)

    def merge(out, strip, inner):
        edge = on_edge(strip.shape[0])
        for k, value in enumerate(placed(strip)):
            out[k] = jnp.where(edge, value, inner[k])

    merge(ou, un[0, whole, :], mu)
    send(ou, u_hbm)
    merge(ov, vel[0, whole, :], mv)
    send(ov, v_hbm)
    strip_tracers(BASE, rows)
    merge(ot, st[...], mt)
    send(ot, t_hbm)
    oh[...] = jnp.where(on_edge(rows), placed(sh[...], 2)[0], mh[...])
    send(oh, h_hbm)
    edge = on_edge(rows)
    for k, value in enumerate(placed(ss[...])):
        os[k] = jnp.where(edge, value, ms[k])
        if k % (LEVELS // 2) == LEVELS // 2 - 1:
            half = pl.ds(k + 1 - LEVELS // 2, LEVELS // 2)
            send(os.at[half], s_hbm.at[half])
    for x in copies:
        x.wait()


def last(c, m0, m1, place, outs):
    rows = outs[4].shape[0]
    tall = rows + BASE + 16
    big = pltpu.VMEM((1, tall, LANES), F32)
    flat = pltpu.VMEM((tall, LANES), F32)
    short = pltpu.VMEM((rows, LANES), F32)
    out3 = jax.ShapeDtypeStruct((LEVELS, rows, LANES), F32)
    wide = pltpu.VMEM((LEVELS, rows, LANES), F32)
    return pl.pallas_call(
        last_kernel,
        in_specs=[VMEM] * 9,
        out_specs=[HBM] * 5,
        out_shape=[out3] * 4 + [jax.ShapeDtypeStruct((rows, LANES), F32)],
        scratch_shapes=[big] * 5
        + [flat]
        + [big] * 7
        + [flat]
        + [short] * 3
        + [wide] * 4
        + [short, pltpu.SemaphoreType.DMA((6,))],
        compiler_params=params(24),
        name="last",
    )(c, m0, m1, place, *outs)


def swaps():
    lon, lat = lax.axis_size("lon"), lax.axis_size("lat")

    def device(o, a):
        return o % lon * lat + a

    lat_first, lat_second, lon_first, lon_second = [], [], [], []
    for o in range(lon):
        for a in range(lat):
            lat_first.append((device(o, a), device(o, a ^ 1)))
            if a == lat - 1:
                lat_second.append((device(o, a), device(lon - 1 - o, a)))
            elif a > 0:
                lat_second.append((device(o, a), device(o, a + 1 if a % 2 else a - 1)))
            else:
                lat_second.append((device(o, a), device(o ^ 1, a)))
            lon_first.append((device(o, a), device(o ^ 1, a)))
            lon_second.append((device(o, a), device(o + 1 if o % 2 else o - 1, a)))
    return lat_first, lat_second, lon_first, lon_second


def on_device(
    heat_anomaly,
    saltiness_anomaly,
    zonal_current,
    meridional_current,
    free_elevation,
    ocean_indicator,
    floor_layer_index,
):
    lat_first, lat_second, lon_first, lon_second = swaps()
    send = functools.partial(lax.ppermute, axis_name=("lon", "lat"))
    fields = (heat_anomaly, saltiness_anomaly, zonal_current, meridional_current, ocean_indicator)
    a, b = row_pack(fields, free_elevation)
    a = send(a, perm=lat_first)
    b = send(b, perm=lat_second)
    *arrays, face, slope, xu, xv, me, place = column_pack(fields, free_elevation)
    t, s, u, v, w, e, p, c, m0, m1 = ghosts(a, b, arrays)
    m0 = send(m0, perm=lon_first)
    m1, *velocities = early(u, v, w, p, xu, xv, m1)
    m1 = send(m1, perm=lon_second)
    u_next, v_next, _, _, *tracers = main((t, s, u, v, w, e, p, face, slope, xu, xv, me), velocities)
    return tuple(last(c, m0, m1, place, (*tracers[:2], u_next, v_next, tracers[2])))


def solution(mesh):
    return jax.shard_map(
        on_device,
        mesh=mesh,
        in_specs=(
            P(None, "lat", "lon"),
            P(None, "lat", "lon"),
            P(None, "lat", "lon"),
            P(None, "lat", "lon"),
            P("lat", "lon"),
            P(None, "lat", "lon"),
            P("lat", "lon"),
        ),
        out_specs=(
            P(None, "lat", "lon"),
            P(None, "lat", "lon"),
            P(None, "lat", "lon"),
            P(None, "lat", "lon"),
            P("lat", "lon"),
        ),
        check_vma=False,
    )
```
